128 devices in a mesh: leaf: 128 (over x, z, y, core).
Axes of the slice: x: 4, y: 4, z: 4, core: 2. Of those that a mesh axis runs over, the one named last changes fastest.
Arguments:
- points: bfloat16 [16, 1048576], P(None, 'leaf'), may hold values from -6 to 6
- coords: float32 [3, 1048576], P(None, 'leaf'), may hold values from 0 to 1, as said below
- basis: bfloat16 [16384, 2048], P('leaf'), may hold values from -0.75 to 0.75
- far_list: int32 [16384, 16], P('leaf'), may hold values from -1 to 16383, as said below
- far_coupling: bfloat16 [16384, 16, 1024], P('leaf'), may hold values from -0.25 to 0.25
- near_list: int32 [16384, 12], P('leaf'), may hold values from -1 to 16383, as said below
- local_transfer: bfloat16 [32512, 1024], P('leaf'), may hold values from -0.875 to 0.875
- top_transfer: bfloat16 [254, 1024], replicated, may hold values from -0.875 to 0.875
- top_coupling: bfloat16 [252, 2, 1024], replicated, may hold values from -0.75 to 0.75
Outputs:
- product: float32 [16, 1048576], P(None, 'leaf')
The draws below stay inside these ranges and needn't reach their ends.
Inputs may be any that keep to these rules, and one draw needn't show every extreme that they name: `far_list`: -1 marks an empty slot; every other entry is a leaf of the leaf's own device or of a device whose index differs from it in exactly one bit (devices hold 128 leaves each, in order). `near_list`: -1 marks an empty slot; slot 0 holds the leaf itself; every other entry is another leaf at most 8 positions away from it in leaf order. `coords`: the points of leaf i lie in cell i of a k-d split of the unit cube that halves x, y, z in turn, by the bits of i from the most significant.
All inputs are finite; a program needn't handle non-finite values.
Results may differ from the reference program's by a relative error of at most 0.0013.
The reference program's roundings to bfloat16 on the way (of `leaf_coeff` and `kernel`) count: a program that leaves them out, or rounds other values in their place, can miss the bound.
Values may be sent and summed in bfloat16 or wider, within the bound.
No kernel may reach another device: no remote copies, remote signals or barrier semaphores. Data moves between devices by JAX's collectives and lax.ppermute only.
A program may use at most 128 MiB of HBM per device.

```python
import math
import jax
import jax.numpy as jnp
from jax import lax

R = 16
LEAF = 64
RANK = 32
LEAF_DEV = 128
NF = 16
NN = 12
SPAN = 8
LEAVES = 16384
N = 1048576
N_LEAF = 128


def draw_coords(key, part):
    key = jax.random.fold_in(key, 13)
    bit_total = LEAVES.bit_length() - 1
    leaf_ids = jnp.arange(N, dtype=jnp.int32) // LEAF
    cells = [jnp.zeros((N,), jnp.int32) for component in range(3)]
    splits = [0, 0, 0]
    for bit_num in range(bit_total):
        component = bit_num % 3
        bit_value = jnp.bitwise_and(jnp.right_shift(leaf_ids, bit_total - 1 - bit_num), 1)
        cells[component] = cells[component] * 2 + bit_value
        splits[component] += 1
    inside = jax.random.uniform(key, (3, N), jnp.float32, 0.0, 1.0)
    rows = []
    for component in range(3):
        side = 1.0 / float(2 ** splits[component])
        rows.append((cells[component].astype(jnp.float32) + inside[component]) * side)
    return jnp.clip(jnp.stack(rows), 0.0, 1.0).astype(jnp.float32)


def draw_far_list(key, part):
    key = jax.random.fold_in(key, 11)
    key_count, key_opening, key_within = jax.random.split(key, 3)
    device_total = LEAVES // LEAF_DEV
    tree_bits = device_total.bit_length() - 1
    leaf_ids = jnp.arange(LEAVES, dtype=jnp.int32)
    owner = leaf_ids // LEAF_DEV
    filled = jax.random.randint(key_count, (LEAVES, 1), NF // 2, NF + 1)
    opening = jax.random.randint(key_opening, (LEAVES, 1), 0, tree_bits + 1)
    slot_ids = jnp.arange(NF, dtype=jnp.int32)[None, :]
    choose_bit = (opening + slot_ids) % (tree_bits + 1)
    flips = jnp.where(choose_bit < tree_bits, jnp.left_shift(jnp.ones_like(choose_bit), choose_bit), 0)
    partner_device = jnp.bitwise_xor(owner[:, None], flips)
    within = jax.random.randint(key_within, (LEAVES, NF), 0, LEAF_DEV)
    return jnp.where(slot_ids < filled, partner_device * LEAF_DEV + within, -1).astype(jnp.int32)


def draw_near_list(key, part):
    key = jax.random.fold_in(key, 12)
    key_count, key_reach, key_heading = jax.random.split(key, 3)
    leaf_ids = jnp.arange(LEAVES, dtype=jnp.int32)
    filled = jax.random.randint(key_count, (LEAVES, 1), 3, NN + 1)
    reach = jax.random.randint(key_reach, (LEAVES, NN), 1, SPAN + 1)
    heading = jax.random.randint(key_heading, (LEAVES, NN), 0, 2) * 2 - 1
    target = leaf_ids[:, None] + reach * heading
    slot_ids = jnp.arange(NN, dtype=jnp.int32)[None, :]
    target = jnp.where(slot_ids == 1, leaf_ids[:, None] + SPAN, target)
    target = jnp.where(slot_ids == 2, leaf_ids[:, None] - SPAN, target)
    usable = (slot_ids < filled) & (target >= 0) & (target < LEAVES)
    result = jnp.where(usable, target, -1)
    result = jnp.where(slot_ids == 0, leaf_ids[:, None], result)
    return result.astype(jnp.int32)


def level_of(own_key, extent, shards, smallest, largest):
    factor_of = 1.0
    for axis_at, shards_of in shards:
        steps = jax.random.uniform(jax.random.fold_in(jax.random.fold_in(own_key, 6), axis_at), (shards_of,), jnp.float32, smallest / len(shards), largest / len(shards))
        factor_of = factor_of * jnp.repeat(jnp.exp(steps), extent[axis_at] // shards_of).reshape((-1,) + (1,) * (len(extent) - 1 - axis_at))
    return factor_of


def scatter_about(stream_key, dims, deviation, most, shards=(), kind=jnp.bfloat16):
    values = deviation * jax.random.normal(stream_key, dims, jnp.float32)
    if shards:
        values = values * level_of(stream_key, dims, shards, -0.22, 0.18)
    return jnp.clip(values, -most, most).astype(kind)


def setup_inputs(seed: int = 0) -> dict:
    key_list = jax.random.split(jax.random.key(seed), 10)
    points = scatter_about(key_list[0], (R, N), 1.0, 6.0, ((1, 128),))
    coords = draw_coords(jax.random.fold_in(key_list[9], 71), 0)
    basis = scatter_about(key_list[2], (LEAVES, LEAF * RANK), LEAF ** -0.5, 0.75, ((0, 128),))
    far_list = draw_far_list(jax.random.fold_in(key_list[9], 71), 0)
    far_coupling = scatter_about(key_list[4], (LEAVES, NF, RANK * RANK), (RANK * NF) ** -0.5, 0.25, ((0, 128),))
    near_list = draw_near_list(jax.random.fold_in(key_list[9], 71), 0)
    local_transfer = scatter_about(key_list[6], (N_LEAF * (2 * LEAF_DEV - 2), RANK * RANK), (3 * RANK // 2) ** -0.5, 0.875, ((0, 128),))
    top_transfer = scatter_about(key_list[7], (2 * N_LEAF - 2, RANK * RANK), (3 * RANK // 2) ** -0.5, 0.875)
    top_coupling = scatter_about(key_list[8], (2 * N_LEAF - 4, 2, RANK * RANK), (2 * RANK) ** -0.5, 0.75)
    return dict(points=points, coords=coords, basis=basis, far_list=far_list, far_coupling=far_coupling, near_list=near_list, local_transfer=local_transfer, top_transfer=top_transfer, top_coupling=top_coupling)


variance = 1.0
nugget = 0.5
decay_rate = math.sqrt(3.0) / 0.3
highest = lax.Precision.HIGHEST

def matern_block(own_coords, part_coords, own_ids, part_ids, present):
    width = own_coords.shape[2]
    squared = jnp.zeros((own_coords.shape[1], width, part_coords.shape[2]), jnp.float32)
    for component in range(3):
        delta = own_coords[component][:, :, None] - part_coords[component][:, None, :]
        squared = squared + delta * delta
    scaled = decay_rate * jnp.sqrt(squared)
    kernel = variance * (1.0 + scaled) * jnp.exp(-scaled)
    column_pos = jnp.arange(part_coords.shape[2], dtype=jnp.int32) % width
    row_pos = jnp.arange(width, dtype=jnp.int32)
    same_leaf = jnp.repeat(part_ids == own_ids[:, None], width, axis=1)
    diagonal = same_leaf[:, None, :] & (column_pos[None, None, :] == row_pos[None, :, None])
    kernel = kernel + nugget * diagonal.astype(jnp.float32)
    live = jnp.repeat(present, width, axis=1).astype(jnp.float32)
    return (kernel * live[:, None, :]).astype(jnp.bfloat16)

def top_start(height, number):
    if height == 0:
        return 0
    return 2 * number - number // 2 ** (height - 1)

def reference(points, coords, basis, far_list, far_coupling, near_list, local_transfer, top_transfer, top_coupling):
    rhs_count = points.shape[0]
    leaf_total = LEAF_DEV * N_LEAF
    tree_bits = N_LEAF.bit_length() - 1
    basis_f = basis.reshape(leaf_total, LEAF, RANK).astype(jnp.float32)
    point_blocks = points.reshape(rhs_count, leaf_total, LEAF)
    leaf_coeff = jnp.einsum('lpk,rlp->lkr', basis_f, point_blocks.astype(jnp.float32), precision=highest).astype(jnp.bfloat16)

    def far_device(device_num):
        begin_leaf = device_num * LEAF_DEV
        partners = lax.dynamic_slice_in_dim(far_list, begin_leaf, LEAF_DEV, 0)
        coupling = lax.dynamic_slice_in_dim(far_coupling, begin_leaf, LEAF_DEV, 0).reshape(LEAF_DEV, NF, RANK, RANK)
        present = partners >= 0
        gathered = leaf_coeff[jnp.where(present, partners, 0)]
        gathered = jnp.where(present[:, :, None, None], gathered, jnp.zeros_like(gathered))
        return jnp.einsum('lsab,lsbr->lar', coupling.astype(jnp.float32), gathered.astype(jnp.float32), precision=highest)
    far_terms = lax.map(far_device, jnp.arange(N_LEAF, dtype=jnp.int32))
    transfer = local_transfer.reshape(N_LEAF, 2 * LEAF_DEV - 2, RANK, RANK).astype(jnp.float32)
    current = leaf_coeff.astype(jnp.float32).reshape(N_LEAF, LEAF_DEV, RANK, rhs_count)
    offset = 0
    number = LEAF_DEV
    matrices = []
    while number > 1:
        chosen = transfer[:, offset:offset + number]
        matrices.append(chosen)
        partial_value = jnp.einsum('dnab,dnar->dnbr', chosen, current, precision=highest)
        current = partial_value[:, 0::2] + partial_value[:, 1::2]
        offset += number
        number //= 2
    level_coeff = [current[:, 0]]
    for height in range(tree_bits - 2):
        number = N_LEAF >> height
        offset = top_start(height, N_LEAF)
        chosen = top_transfer[offset:offset + number].reshape(number, RANK, RANK).astype(jnp.float32)
        partial_value = jnp.einsum('nab,nar->nbr', chosen, level_coeff[height], precision=highest)
        level_coeff.append(partial_value[0::2] + partial_value[1::2])
    top_terms = []
    for height in range(tree_bits - 1):
        number = N_LEAF >> height
        offset = top_start(height, N_LEAF)
        coupling = top_coupling[offset:offset + number].reshape(number, 2, RANK, RANK).astype(jnp.float32)
        uncle = jnp.bitwise_xor(jnp.arange(number, dtype=jnp.int32) // 2, 1)
        cousin_left = level_coeff[height][2 * uncle]
        cousin_right = level_coeff[height][2 * uncle + 1]
        first_term = jnp.einsum('nab,nbr->nar', coupling[:, 0], cousin_left, precision=highest)
        second_term = jnp.einsum('nab,nbr->nar', coupling[:, 1], cousin_right, precision=highest)
        top_terms.append(first_term + second_term)
    field = top_terms[tree_bits - 2]
    for height in range(tree_bits - 2, 0, -1):
        number = N_LEAF >> height - 1
        offset = top_start(height - 1, N_LEAF)
        chosen = top_transfer[offset:offset + number].reshape(number, RANK, RANK).astype(jnp.float32)
        field = top_terms[height - 1] + jnp.einsum('nab,nbr->nar', chosen, jnp.repeat(field, 2, axis=0), precision=highest)
    field = field[:, None]
    for depth_num in range(len(matrices) - 1, -1, -1):
        spread = jnp.einsum('dnab,dnbr->dnar', matrices[depth_num], jnp.repeat(field, 2, axis=1), precision=highest)
        field = far_terms + spread if depth_num == 0 else spread
    leaf_field = field.reshape(leaf_total, RANK, rhs_count).astype(jnp.bfloat16)
    far_part = jnp.einsum('lpk,lkr->rlp', basis_f, leaf_field.astype(jnp.float32), precision=highest)
    far_part = far_part.reshape(rhs_count, leaf_total * LEAF)
    coord_blocks = coords.reshape(3, leaf_total, LEAF)
    block_leaves = min(16, LEAF_DEV)

    def near_block(block_num):
        begin_leaf = block_num * block_leaves
        own_ids = begin_leaf + jnp.arange(block_leaves, dtype=jnp.int32)
        partners = lax.dynamic_slice_in_dim(near_list, begin_leaf, block_leaves, 0)
        present = partners >= 0
        clamped = jnp.where(present, partners, own_ids[:, None])
        own_coords = lax.dynamic_slice_in_dim(coord_blocks, begin_leaf, block_leaves, 1)
        part_coords = coord_blocks[:, clamped].reshape(3, block_leaves, NN * LEAF)
        part_points = point_blocks[:, clamped].reshape(rhs_count, block_leaves, NN * LEAF)
        kernel = matern_block(own_coords, part_coords, own_ids, clamped, present)
        return jnp.einsum('bpq,rbq->rbp', kernel.astype(jnp.float32), part_points.astype(jnp.float32), precision=highest)
    near_part = lax.map(near_block, jnp.arange(leaf_total // block_leaves, dtype=jnp.int32))
    near_part = jnp.transpose(near_part, (1, 0, 2, 3)).reshape(rhs_count, leaf_total * LEAF)
    return near_part + far_part
```

```python
import functools
import math

import jax
import jax.numpy as jnp
from jax import lax
from jax.experimental import pallas as pl
from jax.experimental.pallas import tpu as pltpu
from jax.sharding import PartitionSpec as P

LEAF = 64
RANK = 32
NF = 16
NN = 12
SPAN = 8
LEAF_DEV = 128


variance = 1.0
nugget = 0.5
decay_rate = math.sqrt(3.0) / 0.3
highest = lax.Precision.HIGHEST


def padded(cells, sides, width):
    for axis, dim in sides:
        count = lax.axis_size(axis)
        ends = count - 1
        head = lax.slice_in_dim(cells, 0, width, axis=dim)
        tail = lax.slice_in_dim(cells, cells.shape[dim] - width, cells.shape[dim], axis=dim)
        cells = jnp.concatenate(
            [
                lax.ppermute(tail, axis, [(i, (i + 1) % count) for i in range(ends)]),
                cells,
                lax.ppermute(head, axis, [((i + 1) % count, i) for i in range(ends)]),
            ],
            axis=dim,
        )
    return cells


def swapped(block, axis, apart):
    count = lax.axis_size(axis)
    route = []
    for low in range(count):
        high = low | 1 << apart
        if high != low and high < count:
            route += [(low, high), (high, low)]
    return lax.ppermute(block, axis, route)


LOG2E = 1.4426950408889634
LN2 = 0.6931471805599453
SCALE = decay_rate * LOG2E
BLK = 256
BL = BLK // LEAF
f32 = jnp.float32
bf16 = jnp.bfloat16


def split3(v):
    a = v.astype(bf16)
    rest = v - a.astype(f32)
    b = rest.astype(bf16)
    c = (rest - b.astype(f32)).astype(bf16)
    return a.astype(f32), b.astype(f32), c.astype(f32)


def features(coords):
    v = (coords - 0.5) * SCALE
    parts = [split3(v[c : c + 1]) for c in range(3)]
    norm = split3(jnp.sum(v * v, axis=0, keepdims=True))
    one = jnp.ones_like(norm[0])
    zero = jnp.zeros_like(one)
    left = []
    right = []
    for one_part in parts:
        a, b, c = one_part
        left += [a, a, a, b, b, c]
        right += [-2.0 * a, -2.0 * b, -2.0 * c, -2.0 * a, -2.0 * b, -2.0 * a]
    left += list(norm) + [one, one, one] + [zero] * 8
    right += [one, one, one] + list(norm) + [zero] * 8
    return jnp.concatenate(left, axis=0), jnp.concatenate(right, axis=0)


def matern(squared):
    m = jnp.maximum(squared, 1e-20)
    t = m * lax.rsqrt(m)
    return (variance + (variance * LN2) * t) * jnp.exp2(-t)


def near_kernel(blocks, coords_ref, points_ref, rel_ref, out_ref, left_ref, right_ref, weight_ref, acc_ref, kern_ref):
    lanes_iota = lax.broadcasted_iota(jnp.int32, (32, LEAF_DEV), 1)
    row_iota = lax.broadcasted_iota(jnp.int32, (32, LEAF_DEV), 0)
    base = (lanes_iota // BL) * BL - SPAN
    count = jnp.zeros((32, LEAF_DEV), f32)
    for s in range(NN):
        count = count + jnp.where(rel_ref[s : s + 1, :] - base == row_iota, 1.0, 0.0)
    spread = (
        lax.broadcasted_iota(jnp.int32, (LEAF_DEV, BLK), 0)
        == lax.broadcasted_iota(jnp.int32, (LEAF_DEV, BLK), 1) // LEAF
    ).astype(f32).astype(bf16)
    total = blocks + 4
    zero_weight = jnp.zeros((32, BLK), f32)
    for b in (0, 1, total - 2, total - 1):
        weight_ref[b] = zero_weight
    for b in range(blocks):
        shifted = pltpu.roll(count, (LEAF_DEV - BL * b) % LEAF_DEV, 1) if b else count
        weight_ref[b + 2] = jnp.dot(shifted.astype(bf16), spread, preferred_element_type=f32)

    @pl.loop(0, total)
    def _(b):
        left, right = features(coords_ref[:, pl.ds(pl.multiple_of(b * BLK, BLK), BLK)])
        left_ref[pl.ds(pl.multiple_of(b * BLK, BLK), BLK), :] = jnp.transpose(left).astype(bf16)
        right_ref[:, pl.ds(pl.multiple_of(b * BLK, BLK), BLK)] = right.astype(bf16)
        acc_ref[b] = jnp.zeros((16, BLK), f32)

    leaf_of_lane = lax.broadcasted_iota(jnp.int32, (16, BLK), 1) // LEAF

    def expanded(b):
        x = points_ref[:, pl.ds(pl.multiple_of(b * BLK, BLK), BLK)]
        zero = jnp.zeros_like(x)
        return jnp.concatenate([jnp.where(leaf_of_lane == j, x, zero) for j in range(BL)], axis=0)

    diagonal = [
        lax.broadcasted_iota(jnp.int32, (64, BLK), 0) + 64 * c
        == lax.broadcasted_iota(jnp.int32, (64, BLK), 1)
        for c in range(BLK // 64)
    ]

    @pl.loop(0, total - 2)
    def _(i):
        right = right_ref[:, pl.ds(pl.multiple_of(i * BLK, BLK), BLK)]
        x_i = expanded(i)
        acc_i = acc_ref[i]
        for step in range(3):
            j = i + step
            for c in range(BLK // 64):
                left = left_ref[pl.ds(pl.multiple_of(j * BLK, BLK) + 64 * c, 64), :]
                block = matern(jnp.dot(left, right, preferred_element_type=f32))
                if step == 0:
                    block = block + jnp.where(diagonal[c], nugget, 0.0)
                kern_ref[step, 64 * c : 64 * c + 64, :] = block.astype(bf16)
        for step in range(3):
            j = i + step
            kern = kern_ref[step]
            x_j = x_i if step == 0 else expanded(j)
            part = jnp.dot(x_j, kern, preferred_element_type=f32)
            weight = weight_ref[i]
            for k in range(BL):
                row = SPAN + BL * step + k
                acc_i = acc_i + part[16 * k : 16 * k + 16] * weight[row : row + 1]
            if step:
                part = lax.dot_general(x_i, kern, (((1,), (1,)), ((), ())), preferred_element_type=f32)
                weight = weight_ref[j]
                acc = acc_ref[j]
                for k in range(BL):
                    row = SPAN - BL * step + k
                    acc = acc + part[16 * k : 16 * k + 16] * weight[row : row + 1]
                acc_ref[j] = acc
        acc_ref[i] = acc_i

    @pl.loop(0, blocks)
    def _(b):
        out_ref[:, pl.ds(pl.multiple_of(b * BLK, BLK), BLK)] = acc_ref[b + 2]


def near_field(ext_coords, ext_points, near_rel):
    blocks = LEAF_DEV // BL
    total = blocks + 4
    vmem = pl.BlockSpec(memory_space=pltpu.VMEM)
    return pl.pallas_call(
        functools.partial(near_kernel, blocks),
        out_shape=jax.ShapeDtypeStruct((16, LEAF_DEV * LEAF), f32),
        in_specs=[vmem] * 3,
        out_specs=vmem,
        scratch_shapes=[
            pltpu.VMEM((total * BLK, 32), bf16),
            pltpu.VMEM((32, total * BLK), bf16),
            pltpu.VMEM((total, 32, BLK), f32),
            pltpu.VMEM((total, 16, BLK), f32),
            pltpu.VMEM((3, BLK, BLK), bf16),
        ],
        compiler_params=pltpu.CompilerParams(vmem_limit_bytes=48 * 1024 * 1024),
        cost_estimate=pl.CostEstimate(flops=2_000_000_000, bytes_accessed=2_000_000, transcendentals=13_000_000),
    )(ext_coords, ext_points, near_rel)


def top_start(height, number):
    if height == 0:
        return 0
    return 2 * number - number // 2 ** (height - 1)


def per_device(
    points,
    coords,
    basis,
    far_list,
    far_coupling,
    near_list,
    local_transfer,
    top_transfer,
    top_coupling,
):
    rhs_count = points.shape[0]
    leaf_local = basis.shape[0]
    device = lax.axis_index("leaf")
    devices_all = lax.axis_size("leaf")
    tree_bits = devices_all.bit_length() - 1
    basis_blocks = basis.reshape(leaf_local, LEAF, RANK)
    point_blocks = points.reshape(rhs_count, leaf_local, LEAF)
    leaf_coeff = jnp.einsum(
        "lpk,rlp->lkr", basis_blocks, point_blocks, preferred_element_type=jnp.float32
    ).astype(jnp.bfloat16)
    flat_coeff = leaf_coeff.reshape(leaf_local, RANK * rhs_count)
    ext_points = padded(points, (("leaf", 1),), SPAN * LEAF)
    ext_coords = padded(coords, (("leaf", 1),), SPAN * LEAF)
    present = far_list >= 0
    table = lax.all_gather(flat_coeff, "leaf", axis=0, tiled=True)
    row_index = jnp.where(present, far_list, 0)
    gathered = table[row_index]
    gathered = jnp.where(present[:, :, None], gathered, jnp.zeros_like(gathered))
    gathered = gathered.reshape(leaf_local, NF, RANK, rhs_count)
    coupling = far_coupling.reshape(leaf_local, NF, RANK, RANK)
    far_terms = jnp.einsum("lsab,lsbr->lar", coupling, gathered, preferred_element_type=jnp.float32)
    current = leaf_coeff.astype(jnp.float32)
    offset = 0
    number = leaf_local
    matrices = []
    while number > 1:
        chosen = (
            local_transfer[offset : offset + number].reshape(number, RANK, RANK).astype(jnp.float32)
        )
        matrices.append(chosen)
        partial_value = jnp.einsum("nab,nar->nbr", chosen, current, precision=highest)
        current = partial_value[0::2] + partial_value[1::2]
        offset += number
        number //= 2
    device_coeff = current[0]

    def top_matrix(height, node):
        picked = lax.dynamic_index_in_dim(
            top_transfer, top_start(height, devices_all) + node, 0, keepdims=False
        )
        return picked.reshape(RANK, RANK).astype(jnp.float32)

    top_terms = []
    mine = device_coeff
    before_mine = jnp.zeros_like(mine)
    before_sibling = jnp.zeros_like(mine)
    for height in range(tree_bits):
        received = swapped(jnp.stack([mine, before_mine, before_sibling]), "leaf", height)
        if height >= 1:
            lower = jnp.right_shift(device, height - 1)
            partner_first = lower % 2 == 0
            cousin_left = jnp.where(partner_first, received[1], received[2])
            cousin_right = jnp.where(partner_first, received[2], received[1])
            coupled_height = height - 1
            coupled_picked = lax.dynamic_index_in_dim(
                top_coupling, top_start(coupled_height, devices_all) + lower, 0, keepdims=False
            )
            pair = coupled_picked.reshape(2, RANK, RANK).astype(jnp.float32)
            top_terms.append(
                jnp.dot(pair[0], cousin_left, precision=highest)
                + jnp.dot(pair[1], cousin_right, precision=highest)
            )
        sibling = received[0]
        before_mine = mine
        before_sibling = sibling
        if height <= tree_bits - 3:
            node = jnp.right_shift(device, height)
            own_term = jnp.dot(top_matrix(height, node).T, mine, precision=highest)
            sibling_term = jnp.dot(
                top_matrix(height, jnp.bitwise_xor(node, 1)).T, sibling, precision=highest
            )
            mine = own_term + sibling_term
        else:
            mine = jnp.zeros_like(mine)
    field = top_terms[tree_bits - 2]
    for height in range(tree_bits - 2, 0, -1):
        child = jnp.right_shift(device, height - 1)
        field = top_terms[height - 1] + jnp.dot(
            top_matrix(height - 1, child), field, precision=highest
        )
    field = field[None]
    for depth_num in range(len(matrices) - 1, -1, -1):
        spread = jnp.einsum(
            "nab,nbr->nar", matrices[depth_num], jnp.repeat(field, 2, axis=0), precision=highest
        )
        field = far_terms + spread if depth_num == 0 else spread
    leaf_field = field.astype(jnp.bfloat16)
    far_part = jnp.einsum(
        "lpk,lkr->rlp", basis_blocks, leaf_field, preferred_element_type=jnp.float32
    )
    far_part = far_part.reshape(rhs_count, leaf_local * LEAF)
    first_global = device * leaf_local
    near_rel = jnp.transpose(jnp.where(near_list >= 0, near_list - first_global, -1000))
    near_part = near_field(ext_coords, ext_points, near_rel)
    return near_part + far_part


def solution(mesh):
    return jax.shard_map(
        per_device,
        mesh=mesh,
        in_specs=(
            P(None, "leaf"),
            P(None, "leaf"),
            P("leaf", None),
            P("leaf", None),
            P("leaf", None, None),
            P("leaf", None),
            P("leaf", None),
            P(),
            P(),
        ),
        out_specs=P(None, "leaf"),
        check_vma=False,
    )
```

```python
import functools
import math

import jax
import jax.numpy as jnp
from jax import lax
from jax.experimental import pallas as pl
from jax.experimental.pallas import tpu as pltpu
from jax.sharding import PartitionSpec as P

LEAF = 64
RANK = 32
NF = 16
NN = 12
SPAN = 8
LEAF_DEV = 128
N_DEV = 128


variance = 1.0
nugget = 0.5
decay_rate = math.sqrt(3.0) / 0.3
highest = lax.Precision.HIGHEST


def padded(cells, sides, width):
    for axis, dim in sides:
        count = lax.axis_size(axis)
        ends = count - 1
        head = lax.slice_in_dim(cells, 0, width, axis=dim)
        tail = lax.slice_in_dim(cells, cells.shape[dim] - width, cells.shape[dim], axis=dim)
        cells = jnp.concatenate(
            [
                lax.ppermute(tail, axis, [(i, (i + 1) % count) for i in range(ends)]),
                cells,
                lax.ppermute(head, axis, [((i + 1) % count, i) for i in range(ends)]),
            ],
            axis=dim,
        )
    return cells


LOG2E = 1.4426950408889634
LN2 = 0.6931471805599453
SCALE = decay_rate * LOG2E
BLK = 256
BL = BLK // LEAF
f32 = jnp.float32
bf16 = jnp.bfloat16


def split3(v):
    a = v.astype(bf16)
    rest = v - a.astype(f32)
    b = rest.astype(bf16)
    c = (rest - b.astype(f32)).astype(bf16)
    return a.astype(f32), b.astype(f32), c.astype(f32)


def features(coords):
    v = (coords - 0.5) * SCALE
    parts = [split3(v[c : c + 1]) for c in range(3)]
    norm = split3(jnp.sum(v * v, axis=0, keepdims=True))
    one = jnp.ones_like(norm[0])
    zero = jnp.zeros_like(one)
    left = []
    right = []
    for one_part in parts:
        a, b, c = one_part
        left += [a, a, a, b, b, c]
        right += [-2.0 * a, -2.0 * b, -2.0 * c, -2.0 * a, -2.0 * b, -2.0 * a]
    left += list(norm) + [one, one, one] + [zero] * 8
    right += [one, one, one] + list(norm) + [zero] * 8
    return jnp.concatenate(left, axis=0), jnp.concatenate(right, axis=0)


def matern(squared):
    m = jnp.maximum(squared, 1e-20)
    t = m * lax.rsqrt(m)
    return (variance + (variance * LN2) * t) * jnp.exp2(-t)


def near_kernel(blocks, coords_ref, points_ref, rel_ref, out_ref, left_ref, right_ref, weight_ref, acc_ref, kern_ref):
    lanes_iota = lax.broadcasted_iota(jnp.int32, (32, LEAF_DEV), 1)
    row_iota = lax.broadcasted_iota(jnp.int32, (32, LEAF_DEV), 0)
    base = (lanes_iota // BL) * BL - SPAN
    count = jnp.zeros((32, LEAF_DEV), f32)
    for s in range(NN):
        count = count + jnp.where(rel_ref[s : s + 1, :] - base == row_iota, 1.0, 0.0)
    spread = (
        lax.broadcasted_iota(jnp.int32, (LEAF_DEV, BLK), 0)
        == lax.broadcasted_iota(jnp.int32, (LEAF_DEV, BLK), 1) // LEAF
    ).astype(f32).astype(bf16)
    total = blocks + 4
    zero_weight = jnp.zeros((32, BLK), f32)
    for b in (0, 1, total - 2, total - 1):
        weight_ref[b] = zero_weight
    for b in range(blocks):
        shifted = pltpu.roll(count, (LEAF_DEV - BL * b) % LEAF_DEV, 1) if b else count
        weight_ref[b + 2] = jnp.dot(shifted.astype(bf16), spread, preferred_element_type=f32)

    @pl.loop(0, total)
    def _(b):
        left, right = features(coords_ref[:, pl.ds(pl.multiple_of(b * BLK, BLK), BLK)])
        left_ref[pl.ds(pl.multiple_of(b * BLK, BLK), BLK), :] = jnp.transpose(left).astype(bf16)
        right_ref[:, pl.ds(pl.multiple_of(b * BLK, BLK), BLK)] = right.astype(bf16)
        acc_ref[b] = jnp.zeros((16, BLK), f32)

    leaf_of_lane = lax.broadcasted_iota(jnp.int32, (16, BLK), 1) // LEAF

    def expanded(b):
        x = points_ref[:, pl.ds(pl.multiple_of(b * BLK, BLK), BLK)]
        zero = jnp.zeros_like(x)
        return jnp.concatenate([jnp.where(leaf_of_lane == j, x, zero) for j in range(BL)], axis=0)

    diagonal = [
        lax.broadcasted_iota(jnp.int32, (64, BLK), 0) + 64 * c
        == lax.broadcasted_iota(jnp.int32, (64, BLK), 1)
        for c in range(BLK // 64)
    ]

    @pl.loop(0, total - 2)
    def _(i):
        right = right_ref[:, pl.ds(pl.multiple_of(i * BLK, BLK), BLK)]
        x_i = expanded(i)
        acc_i = acc_ref[i]
        for step in range(3):
            j = i + step
            for c in range(BLK // 64):
                left = left_ref[pl.ds(pl.multiple_of(j * BLK, BLK) + 64 * c, 64), :]
                block = matern(jnp.dot(left, right, preferred_element_type=f32))
                if step == 0:
                    block = block + jnp.where(diagonal[c], nugget, 0.0)
                kern_ref[step, 64 * c : 64 * c + 64, :] = block.astype(bf16)
        for step in range(3):
            j = i + step
            kern = kern_ref[step]
            x_j = x_i if step == 0 else expanded(j)
            part = jnp.dot(x_j, kern, preferred_element_type=f32)
            weight = weight_ref[i]
            for k in range(BL):
                row = SPAN + BL * step + k
                acc_i = acc_i + part[16 * k : 16 * k + 16] * weight[row : row + 1]
            if step:
                part = lax.dot_general(x_i, kern, (((1,), (1,)), ((), ())), preferred_element_type=f32)
                weight = weight_ref[j]
                acc = acc_ref[j]
                for k in range(BL):
                    row = SPAN - BL * step + k
                    acc = acc + part[16 * k : 16 * k + 16] * weight[row : row + 1]
                acc_ref[j] = acc
        acc_ref[i] = acc_i

    @pl.loop(0, blocks)
    def _(b):
        out_ref[:, pl.ds(pl.multiple_of(b * BLK, BLK), BLK)] = acc_ref[b + 2]


def near_field(ext_coords, ext_points, near_rel):
    blocks = LEAF_DEV // BL
    total = blocks + 4
    vmem = pl.BlockSpec(memory_space=pltpu.VMEM)
    return pl.pallas_call(
        functools.partial(near_kernel, blocks),
        out_shape=jax.ShapeDtypeStruct((16, LEAF_DEV * LEAF), f32),
        in_specs=[vmem] * 3,
        out_specs=vmem,
        scratch_shapes=[
            pltpu.VMEM((total * BLK, 32), bf16),
            pltpu.VMEM((32, total * BLK), bf16),
            pltpu.VMEM((total, 32, BLK), f32),
            pltpu.VMEM((total, 16, BLK), f32),
            pltpu.VMEM((3, BLK, BLK), bf16),
        ],
        compiler_params=pltpu.CompilerParams(vmem_limit_bytes=48 * 1024 * 1024),
        cost_estimate=pl.CostEstimate(flops=2_000_000_000, bytes_accessed=2_000_000, transcendentals=13_000_000),
    )(ext_coords, ext_points, near_rel)


TABLE = LEAF_DEV * RANK
STATE = 256
WIDTH = TABLE + STATE
GROUPS = LEAF_DEV // 8
UPPER = 17
PARTNERS = (1, 2, 6, 8, 24, 32, 96)


def iota(shape, dim):
    return lax.broadcasted_iota(jnp.int32, shape, dim)


def where_eq(a, b):
    return jnp.where(a == b, 1.0, 0.0).astype(bf16)


def dot(a, b):
    return jnp.dot(a, b, preferred_element_type=f32)


def dot_nt(a, b):
    return lax.dot_general(a, b, (((1,), (1,)), ((), ())), preferred_element_type=f32)


def halves(v):
    high = v.astype(bf16)
    low = (v - high.astype(f32)).astype(bf16)
    return jnp.concatenate([high, low], axis=0)


def joined(v):
    rows = v.shape[0] // 2
    return v[:rows] + v[rows:]


def pack_state(first, second, third):
    parts = []
    for v in (first, second, third):
        high = v.astype(bf16).astype(f32)
        parts += [high, v - high]
    left = parts[0] + pltpu.roll(parts[1], 32, 1) + pltpu.roll(parts[2], 64, 1) + pltpu.roll(parts[3], 96, 1)
    right = parts[4] + pltpu.roll(parts[5], 32, 1)
    return jnp.concatenate([left, right], axis=1).astype(bf16)


def unpack_state(state):
    lanes = iota((16, 128), 1)
    left = state[:, :128].astype(f32)
    right = state[:, 128:].astype(f32)
    pair_left = left + pltpu.roll(left, 96, 1)
    pair_right = right + pltpu.roll(right, 96, 1)
    keep = lanes < RANK
    return (
        jnp.where(keep, pair_left, 0.0),
        jnp.where(keep, pltpu.roll(pair_left, 64, 1), 0.0),
        jnp.where(keep, pair_right, 0.0),
    )


def up_kernel(points_ref, basis_ref, local_ref, pair_ref, couple_ref, payload_ref, ub_ref, bd_ref, bdup_ref, em_ref, sm_ref, rep_ref, x_ref, c_ref, y_ref):
    step = pl.program_id(0)
    lanes = iota((8, 256), 1) % 8
    rows = iota((8, 256), 0)

    @pl.when(step == 0)
    def _():
        rep_ref[...] = where_eq(iota((128, 1024), 0), iota((128, 1024), 1) // 8)
        column = iota((512, 512), 1)
        perm = where_eq(iota((512, 512), 0), (column % 8) * LEAF + column // 8)
        stacked = jnp.concatenate([points_ref[:, 512 * g : 512 * g + 512] for g in range(GROUPS)], axis=0)
        x_ref[...] = dot(stacked, perm).astype(bf16)
        fold_row = iota((1024, 128), 0) % RANK
        fold_col = iota((1024, 128), 1)
        fold_first = where_eq(fold_row, fold_col)
        fold_second = where_eq(fold_row + RANK, fold_col)
        own = iota((RANK, 1024), 1) // RANK == iota((RANK, 1024), 0)
        pairs = pair_ref[...].astype(f32)
        couples = couple_ref[...].astype(f32)

        def opened(values, k):
            return jnp.where(own, values[k : k + 1, :], 0.0).astype(bf16)

        em_ref[...] = dot(jnp.concatenate([opened(pairs, k) for k in range(10)], axis=0), fold_first).astype(bf16)
        sm_ref[...] = (
            dot(jnp.concatenate([opened(couples, 2 * k) for k in range(6)], axis=0), fold_first)
            + dot(jnp.concatenate([opened(couples, 2 * k + 1) for k in range(6)], axis=0), fold_second)
        ).astype(bf16)

    basis = basis_ref[...]
    wide = dot(jnp.concatenate([basis[:, 128 * k : 128 * k + 128] for k in range(16)], axis=0), rep_ref[...])
    keep = lanes == rows
    for e in range(2):
        for p in range(0, LEAF, 2):
            both = []
            for q in (p, p + 1):
                k, low = q // 4, q % 4
                both.append(jnp.where(keep, wide[16 * k + 8 * e : 16 * k + 8 * e + 8, 256 * low : 256 * low + 256], 0.0))
            ub_ref[e, 8 * p : 8 * p + 16, :] = jnp.concatenate(both, axis=0).astype(bf16)
    local = local_ref[pl.ds(pl.multiple_of(16 * step, 16), 16), :]
    wide = dot(jnp.concatenate([local[:, 128 * k : 128 * k + 128] for k in range(8)], axis=0), rep_ref[...])
    total = jnp.zeros((16, 256), f32)
    for e in range(2):
        keep = lanes == rows // 2 + 4 * e
        for a in range(0, RANK, 2):
            both = []
            for q in (a, a + 1):
                k, low = q // 4, q % 4
                both.append(jnp.where(keep, wide[16 * k + 8 * e : 16 * k + 8 * e + 8, 256 * low : 256 * low + 256], 0.0))
            bd_ref[e, 8 * a : 8 * a + 16, :] = jnp.concatenate(both, axis=0).astype(bf16)
        own = x_ref[pl.ds(pl.multiple_of(32 * step + 16 * e, 16), 16), :]
        coeff = dot(own, ub_ref[e]).astype(bf16)
        payload_ref[:, pl.ds(pl.multiple_of(512 * step + 256 * e, 256), 256)] = coeff
        total = total + dot(coeff, bd_ref[e])
    c_ref[pl.ds(pl.multiple_of(16 * step, 16), 16), :] = total

    @pl.when(step == GROUPS // 2 - 1)
    def _():
        for k in range(8):
            y_ref[k, 0:126, :] = dot(local_ref[128:254, 128 * k : 128 * k + 128], rep_ref[...])
        tile = 0
        for level_tiles in (8, 4, 2, 1):
            for q in range(level_tiles):
                fill_upper(y_ref, bdup_ref, tile, tile, lanes == rows // 2 + 4 * (q % 2))
                tile += 1
        fill_upper(y_ref, bdup_ref, 15, 15, (lanes == rows // 2 + 4) & (rows < 4))
        fill_upper(y_ref, bdup_ref, 16, 15, (lanes == 0) & (rows >= 4) & (rows < 6))
        current = [c_ref[16 * q : 16 * q + 16, :] for q in range(8)]
        tile = 0
        for level_tiles in (8, 4, 2, 1, 1, 1):
            parts = [joined(dot(halves(current[q]), bdup_ref[tile + q])) for q in range(level_tiles)]
            tile += level_tiles
            if level_tiles > 1:
                current = [parts[2 * q] + parts[2 * q + 1] for q in range(level_tiles // 2)]
            else:
                current = parts
        squeeze = where_eq(iota((256, 128), 0), iota((256, 128), 1) * 8)
        mine = joined(dot(halves(current[0]), squeeze))
        zero = jnp.zeros_like(mine)
        payload_ref[:, TABLE:] = pack_state(mine, zero, zero)


def fill_upper(y_ref, bdup_ref, target, tile, keep):
    for a in range(0, RANK, 2):
        both = []
        for q in (a, a + 1):
            k, low = q // 4, q % 4
            both.append(jnp.where(keep, y_ref[k, 8 * tile : 8 * tile + 8, 256 * low : 256 * low + 256], 0.0))
        bdup_ref[target, 8 * a : 8 * a + 16, :] = jnp.concatenate(both, axis=0).astype(bf16)


def upward(points, basis, local_transfer, pairs, couples):
    full = lambda *shape: pl.BlockSpec(shape, lambda i: (0,) * len(shape))
    return pl.pallas_call(
        up_kernel,
        grid=(GROUPS // 2,),
        out_shape=(
            jax.ShapeDtypeStruct((16, WIDTH), bf16),
            jax.ShapeDtypeStruct((GROUPS, 512, 256), bf16),
            jax.ShapeDtypeStruct((GROUPS, 256, 256), bf16),
            jax.ShapeDtypeStruct((UPPER, 256, 256), bf16),
            jax.ShapeDtypeStruct((320, 128), bf16),
            jax.ShapeDtypeStruct((192, 128), bf16),
        ),
        in_specs=[
            full(16, LEAF_DEV * LEAF),
            pl.BlockSpec((16, LEAF * RANK), lambda i: (i, 0)),
            full(254, 1024),
            full(10, 1024),
            full(12, 1024),
        ],
        out_specs=(
            full(16, WIDTH),
            pl.BlockSpec((2, 512, 256), lambda i: (i, 0, 0)),
            pl.BlockSpec((2, 256, 256), lambda i: (i, 0, 0)),
            full(UPPER, 256, 256),
            full(320, 128),
            full(192, 128),
        ),
        scratch_shapes=[
            pltpu.VMEM((128, 1024), bf16),
            pltpu.VMEM((256, 512), bf16),
            pltpu.VMEM((128, 256), f32),
            pltpu.VMEM((8, 128, 1024), f32),
        ],
        compiler_params=pltpu.CompilerParams(vmem_limit_bytes=48 * 1024 * 1024),
        cost_estimate=pl.CostEstimate(flops=1_000_000_000, bytes_accessed=10_000_000, transcendentals=0),
    )(points, basis, local_transfer, pairs, couples)


def step_kernel(height, bits_ref, first_ref, payload_ref, received_ref, em_ref, next_ref):
    forward = height % 2 == 1
    next_ref[:, :TABLE] = received_ref[:, :TABLE] if forward else first_ref[:, :TABLE]
    mine, _, _ = unpack_state(payload_ref[:, TABLE:])
    sibling, _, _ = unpack_state(received_ref[:, TABLE:])
    if height <= 4:
        first = bits_ref[height] == 0
        left = jnp.where(first, mine, sibling)
        right = jnp.where(first, sibling, mine)
        both = (left + pltpu.roll(right, 32, 1))[:, : 2 * RANK]
        parent = joined(dot(halves(both), em_ref[64 * height : 64 * height + 64, :]))
    else:
        parent = jnp.zeros_like(mine)
    next_ref[:, TABLE:] = pack_state(parent, mine, sibling)


def tree_step(height, bits, first, payload, received, em):
    vmem = pl.BlockSpec(memory_space=pltpu.VMEM)
    return pl.pallas_call(
        functools.partial(step_kernel, height),
        out_shape=jax.ShapeDtypeStruct((16, WIDTH), bf16),
        in_specs=[pl.BlockSpec(memory_space=pltpu.SMEM)] + [vmem] * 4,
        out_specs=vmem,
        cost_estimate=pl.CostEstimate(flops=1_000_000, bytes_accessed=400_000, transcendentals=0),
    )(bits, first, payload, received, em)


def regroup_kernel(c_ref, out_ref, x_ref):
    flat = c_ref[...].astype(f32).reshape(128, 1024)
    for k in range(8):
        x_ref[k] = flat[:, 128 * k : 128 * k + 128]
    lanes = iota((8, 128), 1)
    low_half = lanes < 64
    even = (lanes // RANK) % 2 == 0
    for s_high in range(4):
        for a_high in range(8):
            v = [
                x_ref[a_high, pl.ds(4 * s_high + k, 8, stride=NF), :]
                for k in range(4)
            ]
            u0 = jnp.where(low_half, v[0], pltpu.roll(v[2], 64, 1))
            u2 = jnp.where(low_half, pltpu.roll(v[0], 64, 1), v[2])
            u1 = jnp.where(low_half, v[1], pltpu.roll(v[3], 64, 1))
            u3 = jnp.where(low_half, pltpu.roll(v[1], 64, 1), v[3])
            w = []
            for p, q in ((u0, u1), (u2, u3)):
                w.append(jnp.where(even, p, pltpu.roll(q, 32, 1)))
                w.append(jnp.where(even, pltpu.roll(p, 96, 1), q))
            lane = 128 * s_high
            row = 32 * a_high
            out_ref[0, row : row + 16, lane : lane + 128] = jnp.concatenate(w[:2], axis=0).astype(bf16)
            out_ref[0, row + 16 : row + 32, lane : lane + 128] = jnp.concatenate(w[2:], axis=0).astype(bf16)


def regroup(far_coupling):
    return pl.pallas_call(
        regroup_kernel,
        grid=(GROUPS,),
        out_shape=jax.ShapeDtypeStruct((GROUPS, 256, 512), bf16),
        in_specs=[pl.BlockSpec((8, NF, 1024), lambda i: (i, 0, 0))],
        out_specs=pl.BlockSpec((1, 256, 512), lambda i: (i, 0, 0)),
        scratch_shapes=[pltpu.VMEM((8, 128, 128), f32)],
        compiler_params=pltpu.CompilerParams(vmem_limit_bytes=32 * 1024 * 1024),
        cost_estimate=pl.CostEstimate(flops=30_000_000, bytes_accessed=8_400_000, transcendentals=0),
    )(far_coupling)


def down_kernel(bits_ref, index_ref, payload_ref, *refs):
    received = refs[:7]
    em_ref, sm_ref, bdup_ref, d_ref, ub_ref, bd_ref, near_ref, out_ref, table_ref, field_ref, far_ref, gather_ref = refs[7:]
    step = pl.program_id(0)

    @pl.when(step == 0)
    def _():
        column = iota((256, 1024), 1)
        repeat = where_eq(iota((256, 1024), 0), (column % RANK) * 8 + column // 128)
        for k, ref in enumerate((payload_ref,) + received):
            stacked = jnp.concatenate([ref[:, 256 * g : 256 * g + 256] for g in range(GROUPS)], axis=0)
            wide = dot(stacked, repeat).astype(bf16)
            for m in range(8):
                table_ref[2048 * k + 256 * m : 2048 * k + 256 * m + 256, :] = wide[:, 128 * m : 128 * m + 128]
        table_ref[16384:16400, :] = jnp.zeros((16, 128), bf16)
        terms = []
        for height in range(1, 7):
            _, before_mine, before_sibling = unpack_state(received[height][:, TABLE:])
            plain = (bits_ref[height - 1] == 0) == (height % 2 == 1)
            left = jnp.where(plain, before_mine, before_sibling)
            right = jnp.where(plain, before_sibling, before_mine)
            both = left + pltpu.roll(right, 32, 1)
            terms.append(joined(dot_nt(halves(both), sm_ref[32 * height - 32 : 32 * height, :])))
        field = terms[5]
        for height in range(5, 0, -1):
            row = pl.multiple_of(64 * (height - 1) + 32 * bits_ref[height - 1], 32)
            matrix = em_ref[pl.ds(row, 32), 0:RANK]
            field = terms[height - 1] + joined(dot_nt(halves(field), matrix))
        stretch = where_eq(iota((RANK, 256), 0) * 8, iota((RANK, 256), 1))
        fields = [joined(dot(halves(field), stretch))]
        tile = UPPER
        for level_tiles in (1, 1, 1, 2, 4, 8):
            tile -= level_tiles
            fields = [
                joined(dot_nt(halves(fields[q // 2 if level_tiles > 1 else 0]), bdup_ref[tile + q]))
                for q in range(level_tiles)
            ]
        for q in range(8):
            field_ref[32 * q : 32 * q + 32, :] = halves(fields[q])

    block = iota((16, 128), 1) // RANK
    for leaf in range(8):
        for s_high in range(4):
            merged = None
            for low in range(4):
                entry = index_ref[(8 * step + leaf) * NF + 4 * s_high + low]
                value = table_ref[pl.ds(pl.multiple_of(entry * 16, 16), 16), :]
                merged = value if low == 0 else jnp.where(block == low, value, merged)
            gather_ref[16 * leaf : 16 * leaf + 16, 128 * s_high : 128 * s_high + 128] = merged
    result = dot_nt(gather_ref[...], d_ref[0])
    which = iota((16, 256), 1) % 8
    far = result[0:16]
    for leaf in range(1, 8):
        far = jnp.where(which == leaf, result[16 * leaf : 16 * leaf + 16], far)
    parent = field_ref[pl.ds(pl.multiple_of(32 * (step // 2), 32), 32), :]
    leaf_field = (far + joined(dot_nt(parent, bd_ref[0]))).astype(bf16)
    part = dot_nt(leaf_field, ub_ref[0])
    high = part.astype(bf16)
    far_ref[pl.ds(pl.multiple_of(16 * step, 16), 16), :] = high
    far_ref[pl.ds(pl.multiple_of(256 + 16 * step, 16), 16), :] = (part - high.astype(f32)).astype(bf16)

    @pl.when(step == GROUPS - 1)
    def _():
        column = iota((512, 512), 1)
        perm = where_eq(iota((512, 512), 0), (column % LEAF) * 8 + column // LEAF)
        whole = joined(dot(far_ref[...], perm))
        for g in range(GROUPS):
            out_ref[:, 512 * g : 512 * g + 512] = near_ref[:, 512 * g : 512 * g + 512] + whole[16 * g : 16 * g + 16, :]


def downward(bits, index, payload, received, em, sm, bdup, d, ub, bd, near):
    full = lambda *shape: pl.BlockSpec(shape, lambda i: (0,) * len(shape))
    smem = pl.BlockSpec(memory_space=pltpu.SMEM)
    each = lambda *shape: pl.BlockSpec((1,) + shape, lambda i: (i, 0, 0))
    return pl.pallas_call(
        down_kernel,
        grid=(GROUPS,),
        out_shape=jax.ShapeDtypeStruct((16, LEAF_DEV * LEAF), f32),
        in_specs=[smem, smem]
        + [full(16, WIDTH)] * 8
        + [full(320, 128), full(192, 128), full(UPPER, 256, 256)]
        + [each(256, 512), each(512, 256), each(256, 256), full(16, LEAF_DEV * LEAF)],
        out_specs=full(16, LEAF_DEV * LEAF),
        scratch_shapes=[
            pltpu.VMEM((16400, 128), bf16),
            pltpu.VMEM((256, 256), bf16),
            pltpu.VMEM((512, 512), bf16),
            pltpu.VMEM((128, 512), bf16),
        ],
        compiler_params=pltpu.CompilerParams(vmem_limit_bytes=48 * 1024 * 1024),
        cost_estimate=pl.CostEstimate(flops=3_000_000_000, bytes_accessed=16_000_000, transcendentals=0),
    )(bits, index, payload, *received, em, sm, bdup, d, ub, bd, near)


def top_start(height, number):
    if height == 0:
        return 0
    return 2 * number - number // 2 ** (height - 1)


def per_device(
    points,
    coords,
    basis,
    far_list,
    far_coupling,
    near_list,
    local_transfer,
    top_transfer,
    top_coupling,
):
    device = lax.axis_index("leaf")
    bits = jnp.right_shift(device, jnp.arange(8, dtype=jnp.int32)) & 1
    starts = jnp.array([top_start(h, N_DEV) for h in range(6)], jnp.int32)
    heights = jnp.arange(6, dtype=jnp.int32)
    nodes = starts + jnp.right_shift(device, heights)
    pair_rows = (starts + (jnp.right_shift(device, heights) & -2))[:5]
    pair_rows = (pair_rows[:, None] + jnp.arange(2, dtype=jnp.int32)[None, :]).reshape(10)
    pairs = top_transfer[pair_rows]
    couples = top_coupling[nodes].reshape(12, RANK * RANK)
    owner = jnp.bitwise_xor(jnp.right_shift(far_list, 7), device)
    slot = sum((owner >> k > 0).astype(jnp.int32) for k in range(7))
    within = far_list & (LEAF_DEV - 1)
    entry = slot * LEAF_DEV + (within & 7) * GROUPS + (within >> 3)
    index = jnp.where(far_list >= 0, entry, 8 * LEAF_DEV).reshape(LEAF_DEV * NF)
    payload, ub, bd, bdup, em, sm = upward(points, basis, local_transfer, pairs, couples)
    first = payload
    received = []
    for height, mask in enumerate(PARTNERS):
        route = [(i, i ^ mask) for i in range(N_DEV)]
        received.append(lax.ppermute(payload, "leaf", route))
        if height < 6:
            payload = tree_step(height, bits, first, payload, received[height], em)
    ext_points = padded(points, (("leaf", 1),), SPAN * LEAF)
    ext_coords = padded(coords, (("leaf", 1),), SPAN * LEAF)
    near_rel = jnp.transpose(jnp.where(near_list >= 0, near_list - device * LEAF_DEV, -1000))
    near_part = near_field(ext_coords, ext_points, near_rel)
    d = regroup(far_coupling)
    return downward(bits, index, first, received, em, sm, bdup, d, ub, bd, near_part)


def solution(mesh):
    return jax.shard_map(
        per_device,
        mesh=mesh,
        in_specs=(
            P(None, "leaf"),
            P(None, "leaf"),
            P("leaf", None),
            P("leaf", None),
            P("leaf", None, None),
            P("leaf", None),
            P("leaf", None),
            P(),
            P(),
        ),
        out_specs=P(None, "leaf"),
        check_vma=False,
    )
```

```python
import functools
import math

import jax
import jax.numpy as jnp
from jax import lax
from jax.experimental import pallas as pl
from jax.experimental.pallas import tpu as pltpu
from jax.sharding import PartitionSpec as P

LEAF = 64
RANK = 32
NF = 16
NN = 12
SPAN = 8
LEAF_DEV = 128
N_DEV = 128


variance = 1.0
nugget = 0.5
decay_rate = math.sqrt(3.0) / 0.3
highest = lax.Precision.HIGHEST


LOG2E = 1.4426950408889634
LN2 = 0.6931471805599453
SCALE = decay_rate * LOG2E
BLK = 256
BL = BLK // LEAF
FEAT = 64
f32 = jnp.float32
bf16 = jnp.bfloat16


def split3(v):
    a = v.astype(bf16).astype(f32)
    rest = v - a
    b = rest.astype(bf16).astype(f32)
    c = (rest - b).astype(bf16).astype(f32)
    return a, b, c


def scaled(coords):
    return (coords - 0.5) * SCALE


def widened(v):
    return jnp.concatenate([v, jnp.zeros((5, v.shape[1]), f32)], axis=0)


def features(parts):
    a, b, c = parts
    n = a.shape[1]
    v = a + b + c
    norm = split3(jnp.sum(v * v, axis=0, keepdims=True))
    row = lax.broadcasted_iota(jnp.int32, (8, n), 0)

    def place(first, second):
        out = jnp.zeros((8, n), f32)
        for k in range(3):
            out = jnp.where(row == k, first[k], out)
            out = jnp.where(row == k + 3, second[k], out)
        return out

    ones = [jnp.ones((1, n), f32)] * 3
    zero = jnp.zeros((8, n), f32)
    left = jnp.concatenate([a, a, a, b, b, c, place(norm, ones), zero], axis=0)
    a2, b2, c2 = -2.0 * a, -2.0 * b, -2.0 * c
    right = jnp.concatenate([a2, b2, c2, a2, b2, a2, place(ones, norm), zero], axis=0)
    return left, right


def matern(squared):
    m = jnp.maximum(squared, 1e-20)
    t = m * lax.rsqrt(m)
    return (variance + (variance * LN2) * t) * jnp.exp2(-t)


def expanded(x):
    leaf_of_lane = lax.broadcasted_iota(jnp.int32, (16, BLK), 1) // LEAF
    zero = jnp.zeros_like(x)
    return jnp.concatenate([jnp.where(leaf_of_lane == j, x, zero) for j in range(BL)], axis=0)


def slot_counts(rel_ref):
    leaf = lax.broadcasted_iota(jnp.int32, (32, LEAF_DEV), 1)
    row = lax.broadcasted_iota(jnp.int32, (32, LEAF_DEV), 0)
    base = (leaf // BL) * BL - SPAN
    count = jnp.zeros((32, LEAF_DEV), f32)
    for s in range(NN):
        count = count + jnp.where(rel_ref[s : s + 1, :] - base == row, 1.0, 0.0)
    return count


def spread_counts(count, b):
    spread = (
        lax.broadcasted_iota(jnp.int32, (LEAF_DEV, BLK), 0)
        == lax.broadcasted_iota(jnp.int32, (LEAF_DEV, BLK), 1) // LEAF
    ).astype(f32).astype(bf16)
    shifted = pltpu.roll(count, (LEAF_DEV - BL * b) % LEAF_DEV, 1) if b else count
    return jnp.dot(shifted.astype(bf16), spread, preferred_element_type=f32)


def weighed(acc, part, weight, offset):
    for k in range(BL):
        acc = acc + part[16 * k : 16 * k + 16] * weight[SPAN + offset + k : SPAN + offset + k + 1]
    return acc


def near_kernel(blocks, coords_ref, points_ref, rel_ref, out_ref, left_ref, right_ref, weight_ref, acc_ref, x_ref, *kerns):
    total = blocks + 2
    count = slot_counts(rel_ref)
    for b in range(blocks):
        weight_ref[b] = spread_counts(count, b)
    for b in (blocks, blocks + 1):
        weight_ref[b] = jnp.zeros((32, BLK), f32)
    x_ref[:, : blocks * BLK] = points_ref[...]
    x_ref[:, blocks * BLK :] = jnp.zeros((16, 2 * BLK), bf16)
    left_ref[blocks * BLK :, :] = jnp.zeros((2 * BLK, FEAT), bf16)

    @pl.loop(0, blocks // 2)
    def _(b):
        at = pl.multiple_of(2 * b * BLK, BLK)
        left, right = features(split3(widened(scaled(coords_ref[:, pl.ds(at, 2 * BLK)]))))
        left_ref[pl.ds(at, 2 * BLK), :] = jnp.transpose(left).astype(bf16)
        right_ref[:, pl.ds(at, 2 * BLK)] = right.astype(bf16)

    @pl.loop(0, total)
    def _(b):
        acc_ref[b] = jnp.zeros((16, BLK), f32)

    rows = 128
    diagonal = [
        lax.broadcasted_iota(jnp.int32, (rows, BLK), 0) + rows * c
        == lax.broadcasted_iota(jnp.int32, (rows, BLK), 1)
        for c in range(BLK // rows)
    ]

    def block_x(b):
        return expanded(x_ref[:, pl.ds(pl.multiple_of(b * BLK, BLK), BLK)])

    def evaluate(n, step, next_ref):
        right = right_ref[:, pl.ds(pl.multiple_of(n * BLK, BLK), BLK)]
        for c in range(BLK // rows):
            left = left_ref[pl.ds(pl.multiple_of((n + step) * BLK, BLK) + rows * c, rows), :]
            block = matern(jnp.dot(left, right, preferred_element_type=f32))
            if step == 0:
                block = block + jnp.where(diagonal[c], nugget, 0.0)
            next_ref[step, rows * c : rows * c + rows, :] = block.astype(bf16)

    def both(i, kern_ref, n, next_ref):
        acc_i = acc_ref[i]
        x_i = block_x(i)
        weight_i = weight_ref[i]
        for step in range(3):
            j = i + step
            kern = kern_ref[step]
            part = jnp.dot(x_i if step == 0 else block_x(j), kern, preferred_element_type=f32)
            if step:
                mirror = lax.dot_general(x_i, kern, (((1,), (1,)), ((), ())), preferred_element_type=f32)
            evaluate(n, step, next_ref)
            acc_i = weighed(acc_i, part, weight_i, BL * step)
            if step:
                acc_ref[j] = weighed(acc_ref[j], mirror, weight_ref[j], -BL * step)
        acc_ref[i] = acc_i

    for step in range(3):
        evaluate(0, step, kerns[0])

    @pl.loop(0, blocks // 2)
    def _(m):
        both(2 * m, kerns[0], 2 * m + 1, kerns[1])
        both(2 * m + 1, kerns[1], jnp.minimum(2 * m + 2, blocks - 1), kerns[0])

    @pl.loop(0, blocks)
    def _(b):
        out_ref[:, pl.ds(pl.multiple_of(b * BLK, BLK), BLK)] = acc_ref[b]


def near_field(coords, points, near_rel):
    blocks = LEAF_DEV // BL
    total = blocks + 2
    vmem = pl.BlockSpec(memory_space=pltpu.VMEM)
    return pl.pallas_call(
        functools.partial(near_kernel, blocks),
        out_shape=jax.ShapeDtypeStruct((16, LEAF_DEV * LEAF), f32),
        in_specs=[vmem] * 3,
        out_specs=vmem,
        scratch_shapes=[
            pltpu.VMEM((total * BLK, FEAT), bf16),
            pltpu.VMEM((FEAT, total * BLK), bf16),
            pltpu.VMEM((total, 32, BLK), f32),
            pltpu.VMEM((total, 16, BLK), f32),
            pltpu.VMEM((16, total * BLK), bf16),
            pltpu.VMEM((3, BLK, BLK), bf16),
            pltpu.VMEM((3, BLK, BLK), bf16),
        ],
        compiler_params=pltpu.CompilerParams(vmem_limit_bytes=32 * 1024 * 1024),
        cost_estimate=pl.CostEstimate(flops=2_000_000_000, bytes_accessed=2_000_000, transcendentals=13_000_000),
    )(coords, points, near_rel)


EDGES = ((0, -2, 0), (0, -1, 1), (1, -2, 1), (30, 2, 0), (31, 1, 0), (31, 2, 1))


def edge_products(left_halo, right_halo, coords_ref, rel_ref, add):
    count = slot_counts(rel_ref)
    halo_rows = []
    for halo in (left_halo, right_halo):
        splits = halo[:, SPAN * LEAF :].astype(f32)
        parts = [widened(splits[3 * k : 3 * k + 3]) for k in range(3)]
        halo_rows.append(jnp.transpose(features(parts)[0]).astype(bf16))
    for own in (0, 1, 30, 31):
        right = features(split3(widened(scaled(coords_ref[:, BLK * own : BLK * own + BLK]))))[1].astype(bf16)
        weight = spread_counts(count, own)
        acc = jnp.zeros((16, BLK), f32)
        for edge_own, offset, at in EDGES:
            if edge_own == own:
                side = 0 if offset < 0 else 1
                halo = (left_halo, right_halo)[side]
                left = halo_rows[side][BLK * at : BLK * at + BLK]
                kern = matern(jnp.dot(left, right, preferred_element_type=f32)).astype(bf16)
                part = jnp.dot(expanded(halo[:, BLK * at : BLK * at + BLK]), kern, preferred_element_type=f32)
                acc = weighed(acc, part, weight, BL * offset)
        add(own, acc)


TABLE = LEAF_DEV * RANK
STATE = 256
HALO = 2 * SPAN * LEAF
EDGE = TABLE + STATE
WIDTH = EDGE + HALO
FIRST = WIDTH + HALO
GROUPS = LEAF_DEV // 8
UPPER = 17
PARTNERS = (1, 2, 6, 8, 24, 32, 96)


def iota(shape, dim):
    return lax.broadcasted_iota(jnp.int32, shape, dim)


def where_eq(a, b):
    return jnp.where(a == b, 1.0, 0.0).astype(bf16)


def dot(a, b):
    return jnp.dot(a, b, preferred_element_type=f32)


def dot_nt(a, b):
    return lax.dot_general(a, b, (((1,), (1,)), ((), ())), preferred_element_type=f32)


def halves(v):
    high = v.astype(bf16)
    low = (v - high.astype(f32)).astype(bf16)
    return jnp.concatenate([high, low], axis=0)


def joined(v):
    rows = v.shape[0] // 2
    return v[:rows] + v[rows:]


def pack_state(first, second, third):
    parts = []
    for v in (first, second, third):
        high = v.astype(bf16).astype(f32)
        parts += [high, v - high]
    left = parts[0] + pltpu.roll(parts[1], 32, 1) + pltpu.roll(parts[2], 64, 1) + pltpu.roll(parts[3], 96, 1)
    right = parts[4] + pltpu.roll(parts[5], 32, 1)
    return jnp.concatenate([left, right], axis=1).astype(bf16)


def unpack_state(state):
    lanes = iota((16, 128), 1)
    left = state[:, :128].astype(f32)
    right = state[:, 128:].astype(f32)
    pair_left = left + pltpu.roll(left, 96, 1)
    pair_right = right + pltpu.roll(right, 96, 1)
    keep = lanes < RANK
    return (
        jnp.where(keep, pair_left, 0.0),
        jnp.where(keep, pltpu.roll(pair_left, 64, 1), 0.0),
        jnp.where(keep, pair_right, 0.0),
    )


def up_kernel(bits_ref, points_ref, coords_ref, basis_ref, local_ref, payload_ref, ub_ref, bd_ref, bdup_ref, rep_ref, x_ref, c_ref, y_ref):
    step = pl.program_id(0)
    lanes = iota((8, 256), 1) % 8
    rows = iota((8, 256), 0)

    @pl.when(step == 0)
    def _():
        rep_ref[...] = where_eq(iota((128, 1024), 0), iota((128, 1024), 1) // 8)
        column = iota((512, 512), 1)
        perm = where_eq(iota((512, 512), 0), (column % 8) * LEAF + column // 8)
        stacked = jnp.concatenate([points_ref[:, 512 * g : 512 * g + 512] for g in range(GROUPS)], axis=0)
        x_ref[...] = dot(stacked, perm).astype(bf16)
    basis = basis_ref[...]
    wide = dot(jnp.concatenate([basis[:, 128 * k : 128 * k + 128] for k in range(16)], axis=0), rep_ref[...])
    keep = lanes == rows
    for e in range(2):
        for p in range(0, LEAF, 2):
            both = []
            for q in (p, p + 1):
                k, low = q // 4, q % 4
                both.append(jnp.where(keep, wide[16 * k + 8 * e : 16 * k + 8 * e + 8, 256 * low : 256 * low + 256], 0.0))
            ub_ref[e, 8 * p : 8 * p + 16, :] = jnp.concatenate(both, axis=0).astype(bf16)
    local = local_ref[pl.ds(pl.multiple_of(16 * step, 16), 16), :]
    wide = dot(jnp.concatenate([local[:, 128 * k : 128 * k + 128] for k in range(8)], axis=0), rep_ref[...])
    total = jnp.zeros((16, 256), f32)
    for e in range(2):
        keep = lanes == rows // 2 + 4 * e
        for a in range(0, RANK, 2):
            both = []
            for q in (a, a + 1):
                k, low = q // 4, q % 4
                both.append(jnp.where(keep, wide[16 * k + 8 * e : 16 * k + 8 * e + 8, 256 * low : 256 * low + 256], 0.0))
            bd_ref[e, 8 * a : 8 * a + 16, :] = jnp.concatenate(both, axis=0).astype(bf16)
        own = x_ref[pl.ds(pl.multiple_of(32 * step + 16 * e, 16), 16), :]
        coeff = dot(own, ub_ref[e]).astype(bf16)
        payload_ref[:, pl.ds(pl.multiple_of(512 * step + 256 * e, 256), 256)] = coeff
        total = total + dot(coeff, bd_ref[e])
    c_ref[pl.ds(pl.multiple_of(16 * step, 16), 16), :] = total

    @pl.when(step == GROUPS // 2 - 1)
    def _():
        for k in range(8):
            y_ref[k, 0:126, :] = dot(local_ref[128:254, 128 * k : 128 * k + 128], rep_ref[...])
        tile = 0
        for level_tiles in (8, 4, 2, 1):
            for q in range(level_tiles):
                fill_upper(y_ref, bdup_ref, tile, tile, lanes == rows // 2 + 4 * (q % 2))
                tile += 1
        fill_upper(y_ref, bdup_ref, 15, 15, (lanes == rows // 2 + 4) & (rows < 4))
        fill_upper(y_ref, bdup_ref, 16, 15, (lanes == 0) & (rows >= 4) & (rows < 6))
        current = [c_ref[16 * q : 16 * q + 16, :] for q in range(8)]
        tile = 0
        for level_tiles in (8, 4, 2, 1, 1, 1):
            parts = [joined(dot(halves(current[q]), bdup_ref[tile + q])) for q in range(level_tiles)]
            tile += level_tiles
            if level_tiles > 1:
                current = [parts[2 * q] + parts[2 * q + 1] for q in range(level_tiles // 2)]
            else:
                current = parts
        squeeze = where_eq(iota((256, 128), 0), iota((256, 128), 1) * 8)
        mine = joined(dot(halves(current[0]), squeeze))
        zero = jnp.zeros_like(mine)
        payload_ref[:, TABLE:EDGE] = pack_state(mine, zero, zero)
        head = side(points_ref, coords_ref, 0)
        tail = side(points_ref, coords_ref, (LEAF_DEV - SPAN) * LEAF)
        even = bits_ref[0] == 0
        payload_ref[:, EDGE:WIDTH] = jnp.where(even, tail, head)
        payload_ref[:, WIDTH:] = jnp.where(even, head, tail)


def side(points_ref, coords_ref, start):
    end = start + SPAN * LEAF
    parts = split3(scaled(coords_ref[:, start:end]))
    rows = jnp.concatenate(list(parts) + [jnp.zeros((7, SPAN * LEAF), f32)], axis=0)
    return jnp.concatenate([points_ref[:, start:end], rows.astype(bf16)], axis=1)


def open_kernel(pair_ref, couple_ref, em_ref, sm_ref):
    fold_row = iota((1024, 128), 0) % RANK
    fold_col = iota((1024, 128), 1)
    fold_first = where_eq(fold_row, fold_col)
    fold_second = where_eq(fold_row + RANK, fold_col)
    own = iota((RANK, 1024), 1) // RANK == iota((RANK, 1024), 0)
    pairs = pair_ref[...].astype(f32)
    couples = couple_ref[...].astype(f32)

    def opened(values, k):
        return jnp.where(own, values[k : k + 1, :], 0.0).astype(bf16)

    em_ref[...] = dot(jnp.concatenate([opened(pairs, k) for k in range(10)], axis=0), fold_first).astype(bf16)
    sm_ref[...] = (
        dot(jnp.concatenate([opened(couples, 2 * k) for k in range(6)], axis=0), fold_first)
        + dot(jnp.concatenate([opened(couples, 2 * k + 1) for k in range(6)], axis=0), fold_second)
    ).astype(bf16)


def opened_top(pairs, couples):
    vmem = pl.BlockSpec(memory_space=pltpu.VMEM)
    return pl.pallas_call(
        open_kernel,
        out_shape=(jax.ShapeDtypeStruct((320, 128), bf16), jax.ShapeDtypeStruct((192, 128), bf16)),
        in_specs=[vmem] * 2,
        out_specs=(vmem, vmem),
        cost_estimate=pl.CostEstimate(flops=1_000_000, bytes_accessed=400_000, transcendentals=0),
    )(pairs, couples)


def fill_upper(y_ref, bdup_ref, target, tile, keep):
    for a in range(0, RANK, 2):
        both = []
        for q in (a, a + 1):
            k, low = q // 4, q % 4
            both.append(jnp.where(keep, y_ref[k, 8 * tile : 8 * tile + 8, 256 * low : 256 * low + 256], 0.0))
        bdup_ref[target, 8 * a : 8 * a + 16, :] = jnp.concatenate(both, axis=0).astype(bf16)


def upward(bits, points, coords, basis, local_transfer):
    full = lambda *shape: pl.BlockSpec(shape, lambda i: (0,) * len(shape))
    return pl.pallas_call(
        up_kernel,
        grid=(GROUPS // 2,),
        out_shape=(
            jax.ShapeDtypeStruct((16, FIRST), bf16),
            jax.ShapeDtypeStruct((GROUPS, 512, 256), bf16),
            jax.ShapeDtypeStruct((GROUPS, 256, 256), bf16),
            jax.ShapeDtypeStruct((UPPER, 256, 256), bf16),
        ),
        in_specs=[
            pl.BlockSpec(memory_space=pltpu.SMEM),
            full(16, LEAF_DEV * LEAF),
            full(3, LEAF_DEV * LEAF),
            pl.BlockSpec((16, LEAF * RANK), lambda i: (i, 0)),
            full(254, 1024),
        ],
        out_specs=(
            full(16, FIRST),
            pl.BlockSpec((2, 512, 256), lambda i: (i, 0, 0)),
            pl.BlockSpec((2, 256, 256), lambda i: (i, 0, 0)),
            full(UPPER, 256, 256),
        ),
        scratch_shapes=[
            pltpu.VMEM((128, 1024), bf16),
            pltpu.VMEM((256, 512), bf16),
            pltpu.VMEM((128, 256), f32),
            pltpu.VMEM((8, 128, 1024), f32),
        ],
        compiler_params=pltpu.CompilerParams(vmem_limit_bytes=48 * 1024 * 1024),
        cost_estimate=pl.CostEstimate(flops=1_000_000_000, bytes_accessed=10_000_000, transcendentals=0),
    )(bits, points, coords, basis, local_transfer)


def step_kernel(height, bits_ref, first_ref, payload_ref, received_ref, em_ref, next_ref):
    forward = height % 2 == 1
    next_ref[:, :TABLE] = received_ref[:, :TABLE] if forward else first_ref[:, :TABLE]
    start = WIDTH if height == 0 else EDGE
    next_ref[:, EDGE:] = payload_ref[:, EDGE:WIDTH] if forward else received_ref[:, start : start + HALO]
    mine, _, _ = unpack_state(payload_ref[:, TABLE:EDGE])
    sibling, _, _ = unpack_state(received_ref[:, TABLE:EDGE])
    if height <= 4:
        first = bits_ref[height] == 0
        left = jnp.where(first, mine, sibling)
        right = jnp.where(first, sibling, mine)
        both = (left + pltpu.roll(right, 32, 1))[:, : 2 * RANK]
        parent = joined(dot(halves(both), em_ref[64 * height : 64 * height + 64, :]))
    else:
        parent = jnp.zeros_like(mine)
    next_ref[:, TABLE:EDGE] = pack_state(parent, mine, sibling)


def tree_step(height, bits, first, payload, received, em):
    vmem = pl.BlockSpec(memory_space=pltpu.VMEM)
    return pl.pallas_call(
        functools.partial(step_kernel, height),
        out_shape=jax.ShapeDtypeStruct((16, WIDTH), bf16),
        in_specs=[pl.BlockSpec(memory_space=pltpu.SMEM)] + [vmem] * 4,
        out_specs=vmem,
        cost_estimate=pl.CostEstimate(flops=1_000_000, bytes_accessed=400_000, transcendentals=0),
    )(bits, first, payload, received, em)


def regroup_kernel(c_ref, out_ref, x_ref):
    flat = c_ref[...].astype(f32).reshape(128, 1024)
    for k in range(8):
        x_ref[k] = flat[:, 128 * k : 128 * k + 128]
    lanes = iota((8, 128), 1)
    low_half = lanes < 64
    even = (lanes // RANK) % 2 == 0
    for s_high in range(4):
        for a_high in range(8):
            v = [
                x_ref[a_high, pl.ds(4 * s_high + k, 8, stride=NF), :]
                for k in range(4)
            ]
            u0 = jnp.where(low_half, v[0], pltpu.roll(v[2], 64, 1))
            u2 = jnp.where(low_half, pltpu.roll(v[0], 64, 1), v[2])
            u1 = jnp.where(low_half, v[1], pltpu.roll(v[3], 64, 1))
            u3 = jnp.where(low_half, pltpu.roll(v[1], 64, 1), v[3])
            w = []
            for p, q in ((u0, u1), (u2, u3)):
                w.append(jnp.where(even, p, pltpu.roll(q, 32, 1)))
                w.append(jnp.where(even, pltpu.roll(p, 96, 1), q))
            lane = 128 * s_high
            row = 32 * a_high
            out_ref[0, row : row + 16, lane : lane + 128] = jnp.concatenate(w[:2], axis=0).astype(bf16)
            out_ref[0, row + 16 : row + 32, lane : lane + 128] = jnp.concatenate(w[2:], axis=0).astype(bf16)


def regroup(far_coupling):
    return pl.pallas_call(
        regroup_kernel,
        grid=(GROUPS,),
        out_shape=jax.ShapeDtypeStruct((GROUPS, 256, 512), bf16),
        in_specs=[pl.BlockSpec((8, NF, 1024), lambda i: (i, 0, 0))],
        out_specs=pl.BlockSpec((1, 256, 512), lambda i: (i, 0, 0)),
        scratch_shapes=[pltpu.VMEM((8, 128, 128), f32)],
        compiler_params=pltpu.CompilerParams(vmem_limit_bytes=32 * 1024 * 1024),
        cost_estimate=pl.CostEstimate(flops=30_000_000, bytes_accessed=8_400_000, transcendentals=0),
    )(far_coupling)


def down_kernel(bits_ref, index_ref, payload_ref, *refs):
    received = refs[:7]
    em_ref, sm_ref, bdup_ref, coords_ref, rel_ref, d_ref, ub_ref, bd_ref, near_ref, out_ref, table_ref, field_ref, far_ref, gather_ref, edge_ref = refs[7:]
    step = pl.program_id(0)

    @pl.when(step == 0)
    def _():
        column = iota((256, 1024), 1)
        repeat = where_eq(iota((256, 1024), 0), (column % RANK) * 8 + column // 128)
        for k, ref in enumerate((payload_ref,) + received):
            stacked = jnp.concatenate([ref[:, 256 * g : 256 * g + 256] for g in range(GROUPS)], axis=0)
            wide = dot(stacked, repeat).astype(bf16)
            for m in range(8):
                table_ref[2048 * k + 256 * m : 2048 * k + 256 * m + 256, :] = wide[:, 128 * m : 128 * m + 128]
        table_ref[16384:16400, :] = jnp.zeros((16, 128), bf16)
        terms = []
        for height in range(1, 7):
            _, before_mine, before_sibling = unpack_state(received[height][:, TABLE:EDGE])
            plain = (bits_ref[height - 1] == 0) == (height % 2 == 1)
            left = jnp.where(plain, before_mine, before_sibling)
            right = jnp.where(plain, before_sibling, before_mine)
            both = left + pltpu.roll(right, 32, 1)
            terms.append(joined(dot_nt(halves(both), sm_ref[32 * height - 32 : 32 * height, :])))
        field = terms[5]
        for height in range(5, 0, -1):
            row = pl.multiple_of(64 * (height - 1) + 32 * bits_ref[height - 1], 32)
            matrix = em_ref[pl.ds(row, 32), 0:RANK]
            field = terms[height - 1] + joined(dot_nt(halves(field), matrix))
        stretch = where_eq(iota((RANK, 256), 0) * 8, iota((RANK, 256), 1))
        fields = [joined(dot(halves(field), stretch))]
        tile = UPPER
        for level_tiles in (1, 1, 1, 2, 4, 8):
            tile -= level_tiles
            fields = [
                joined(dot_nt(halves(fields[q // 2 if level_tiles > 1 else 0]), bdup_ref[tile + q]))
                for q in range(level_tiles)
            ]
        near_side = received[0][:, EDGE:WIDTH]
        far_side = received[1][:, EDGE:WIDTH]
        for height in range(2, 7):
            far_side = jnp.where(bits_ref[7] == height, received[height][:, EDGE:WIDTH], far_side)
        even = bits_ref[0] == 0
        left_halo = jnp.where(even, far_side, near_side)
        right_halo = jnp.where(even, near_side, far_side)

        def add(own, acc):
            edge_ref[own % 4] = acc

        edge_products(left_halo, right_halo, coords_ref, rel_ref, add)
        for q in range(8):
            field_ref[32 * q : 32 * q + 32, :] = halves(fields[q])

    block = iota((16, 128), 1) // RANK
    for leaf in range(8):
        for s_high in range(4):
            merged = None
            for low in range(4):
                entry = index_ref[(8 * step + leaf) * NF + 4 * s_high + low]
                value = table_ref[pl.ds(pl.multiple_of(entry * 16, 16), 16), :]
                merged = value if low == 0 else jnp.where(block == low, value, merged)
            gather_ref[16 * leaf : 16 * leaf + 16, 128 * s_high : 128 * s_high + 128] = merged
    result = dot_nt(gather_ref[...], d_ref[0])
    which = iota((16, 256), 1) % 8
    far = result[0:16]
    for leaf in range(1, 8):
        far = jnp.where(which == leaf, result[16 * leaf : 16 * leaf + 16], far)
    parent = field_ref[pl.ds(pl.multiple_of(32 * (step // 2), 32), 32), :]
    leaf_field = (far + joined(dot_nt(parent, bd_ref[0]))).astype(bf16)
    part = dot_nt(leaf_field, ub_ref[0])
    high = part.astype(bf16)
    far_ref[pl.ds(pl.multiple_of(16 * step, 16), 16), :] = high
    far_ref[pl.ds(pl.multiple_of(256 + 16 * step, 16), 16), :] = (part - high.astype(f32)).astype(bf16)

    @pl.when(step == GROUPS - 1)
    def _():
        column = iota((512, 512), 1)
        perm = where_eq(iota((512, 512), 0), (column % LEAF) * 8 + column // LEAF)
        whole = joined(dot(far_ref[...], perm))
        for g in range(GROUPS):
            value = near_ref[:, 512 * g : 512 * g + 512] + whole[16 * g : 16 * g + 16, :]
            if g == 0:
                value = value + jnp.concatenate([edge_ref[0], edge_ref[1]], axis=1)
            if g == GROUPS - 1:
                value = value + jnp.concatenate([edge_ref[2], edge_ref[3]], axis=1)
            out_ref[:, 512 * g : 512 * g + 512] = value


def downward(bits, index, payload, received, em, sm, bdup, coords, near_rel, d, ub, bd, near):
    full = lambda *shape: pl.BlockSpec(shape, lambda i: (0,) * len(shape))
    smem = pl.BlockSpec(memory_space=pltpu.SMEM)
    each = lambda *shape: pl.BlockSpec((1,) + shape, lambda i: (i, 0, 0))
    return pl.pallas_call(
        down_kernel,
        grid=(GROUPS,),
        out_shape=jax.ShapeDtypeStruct((16, LEAF_DEV * LEAF), f32),
        in_specs=[smem, smem]
        + [full(16, FIRST)] * 2
        + [full(16, WIDTH)] * 6
        + [full(320, 128), full(192, 128), full(UPPER, 256, 256)]
        + [full(3, LEAF_DEV * LEAF), full(NN, LEAF_DEV)]
        + [each(256, 512), each(512, 256), each(256, 256), full(16, LEAF_DEV * LEAF)],
        out_specs=full(16, LEAF_DEV * LEAF),
        scratch_shapes=[
            pltpu.VMEM((16400, 128), bf16),
            pltpu.VMEM((256, 256), bf16),
            pltpu.VMEM((512, 512), bf16),
            pltpu.VMEM((128, 512), bf16),
            pltpu.VMEM((4, 16, BLK), f32),
        ],
        compiler_params=pltpu.CompilerParams(vmem_limit_bytes=48 * 1024 * 1024),
        cost_estimate=pl.CostEstimate(flops=3_000_000_000, bytes_accessed=16_000_000, transcendentals=0),
    )(bits, index, payload, *received, em, sm, bdup, coords, near_rel, d, ub, bd, near)


def top_start(height, number):
    if height == 0:
        return 0
    return 2 * number - number // 2 ** (height - 1)


def per_device(
    points,
    coords,
    basis,
    far_list,
    far_coupling,
    near_list,
    local_transfer,
    top_transfer,
    top_coupling,
):
    device = lax.axis_index("leaf")
    outer = jnp.bitwise_xor(device, device + 2 * (device & 1) - 1)
    level = sum((outer >> k > 0).astype(jnp.int32) for k in range(7)) - 1
    number = jnp.arange(8, dtype=jnp.int32)
    bits = jnp.where(number == 7, jnp.maximum(level, 1), jnp.right_shift(device, number) & 1)
    starts = jnp.array([top_start(h, N_DEV) for h in range(6)], jnp.int32)
    heights = jnp.arange(6, dtype=jnp.int32)
    nodes = starts + jnp.right_shift(device, heights)
    pair_rows = (starts + (jnp.right_shift(device, heights) & -2))[:5]
    pair_rows = (pair_rows[:, None] + jnp.arange(2, dtype=jnp.int32)[None, :]).reshape(10)
    pairs = top_transfer[pair_rows]
    couples = top_coupling[nodes].reshape(12, RANK * RANK)
    owner = jnp.bitwise_xor(jnp.right_shift(far_list, 7), device)
    slot = sum((owner >> k > 0).astype(jnp.int32) for k in range(7))
    within = far_list & (LEAF_DEV - 1)
    entry = slot * LEAF_DEV + (within & 7) * GROUPS + (within >> 3)
    index = jnp.where(far_list >= 0, entry, 8 * LEAF_DEV).reshape(LEAF_DEV * NF)
    payload, ub, bd, bdup = upward(bits, points, coords, basis, local_transfer)
    em, sm = opened_top(pairs, couples)
    first = payload
    received = []
    for height, mask in enumerate(PARTNERS):
        route = [(i, i ^ mask) for i in range(N_DEV)]
        received.append(lax.ppermute(payload, "leaf", route))
        if height < 6:
            payload = tree_step(height, bits, first, payload, received[height], em)
    near_rel = jnp.transpose(jnp.where(near_list >= 0, near_list - device * LEAF_DEV, -1000))
    near_part = near_field(coords, points, near_rel)
    d = regroup(far_coupling)
    return downward(bits, index, first, received, em, sm, bdup, coords, near_rel, d, ub, bd, near_part)


def solution(mesh):
    return jax.shard_map(
        per_device,
        mesh=mesh,
        in_specs=(
            P(None, "leaf"),
            P(None, "leaf"),
            P("leaf", None),
            P("leaf", None),
            P("leaf", None, None),
            P("leaf", None),
            P("leaf", None),
            P(),
            P(),
        ),
        out_specs=P(None, "leaf"),
        check_vma=False,
    )
```

```python
import functools
import math

import jax
import jax.numpy as jnp
from jax import lax
from jax.experimental import pallas as pl
from jax.experimental.pallas import tpu as pltpu
from jax.sharding import PartitionSpec as P

LEAF = 64
RANK = 32
NF = 16
NN = 12
SPAN = 8
LEAF_DEV = 128
N_DEV = 128


variance = 1.0
nugget = 0.5
decay_rate = math.sqrt(3.0) / 0.3
highest = lax.Precision.HIGHEST


LOG2E = 1.4426950408889634
LN2 = 0.6931471805599453
SCALE = decay_rate * LOG2E
BLK = 256
BL = BLK // LEAF
FEAT = 64
f32 = jnp.float32
bf16 = jnp.bfloat16


def split3(v):
    a = v.astype(bf16).astype(f32)
    rest = v - a
    b = rest.astype(bf16).astype(f32)
    c = (rest - b).astype(bf16).astype(f32)
    return a, b, c


def scaled(coords):
    return (coords - 0.5) * SCALE


def widened(v):
    return jnp.concatenate([v, jnp.zeros((5, v.shape[1]), f32)], axis=0)


def features(parts):
    a, b, c = parts
    n = a.shape[1]
    v = a + b + c
    norm = split3(jnp.sum(v * v, axis=0, keepdims=True))
    row = lax.broadcasted_iota(jnp.int32, (8, n), 0)

    def place(first, second):
        out = jnp.zeros((8, n), f32)
        for k in range(3):
            out = jnp.where(row == k, first[k], out)
            out = jnp.where(row == k + 3, second[k], out)
        return out

    ones = [jnp.ones((1, n), f32)] * 3
    zero = jnp.zeros((8, n), f32)
    left = jnp.concatenate([a, a, a, b, b, c, place(norm, ones), zero], axis=0)
    a2, b2, c2 = -2.0 * a, -2.0 * b, -2.0 * c
    right = jnp.concatenate([a2, b2, c2, a2, b2, a2, place(ones, norm), zero], axis=0)
    return left, right


def matern(squared):
    m = jnp.maximum(squared, 1e-20)
    t = m * lax.rsqrt(m)
    return (variance + (variance * LN2) * t) * jnp.exp2(-t)


def expanded(x):
    leaf_of_lane = lax.broadcasted_iota(jnp.int32, (16, BLK), 1) // LEAF
    zero = jnp.zeros_like(x)
    return jnp.concatenate([jnp.where(leaf_of_lane == j, x, zero) for j in range(BL)], axis=0)


def slot_counts(rel_ref):
    leaf = lax.broadcasted_iota(jnp.int32, (32, LEAF_DEV), 1)
    row = lax.broadcasted_iota(jnp.int32, (32, LEAF_DEV), 0)
    base = (leaf // BL) * BL - SPAN
    count = jnp.zeros((32, LEAF_DEV), f32)
    for s in range(NN):
        count = count + jnp.where(rel_ref[s : s + 1, :] - base == row, 1.0, 0.0)
    return count


def spread_counts(count, b):
    spread = (
        lax.broadcasted_iota(jnp.int32, (LEAF_DEV, BLK), 0)
        == lax.broadcasted_iota(jnp.int32, (LEAF_DEV, BLK), 1) // LEAF
    ).astype(f32).astype(bf16)
    shifted = pltpu.roll(count, (LEAF_DEV - BL * b) % LEAF_DEV, 1) if b else count
    return jnp.dot(shifted.astype(bf16), spread, preferred_element_type=f32)


def weighed(acc, part, weight, offset):
    for k in range(BL):
        acc = acc + part[16 * k : 16 * k + 16] * weight[SPAN + offset + k : SPAN + offset + k + 1]
    return acc


def near_kernel(chunk, blocks, coords_ref, points_ref, rel_ref, after_ref, out_ref, token_ref, left_ref, right_ref, weight_ref, acc_ref, x_ref, *kerns):
    del after_ref
    total = blocks + 2
    begin = chunk * blocks
    valid = min(total, LEAF_DEV // BL - begin)
    token_ref[...] = jnp.zeros_like(token_ref)
    count = slot_counts(rel_ref)
    x_ref[:, : valid * BLK] = points_ref[:, begin * BLK : (begin + valid) * BLK]
    if valid < total:
        x_ref[:, valid * BLK :] = jnp.zeros((16, (total - valid) * BLK), bf16)
        left_ref[valid * BLK :, :] = jnp.zeros(((total - valid) * BLK, FEAT), bf16)
    for b in range(total):
        acc_ref[b] = jnp.zeros((16, BLK), f32)
        weight_ref[b] = spread_counts(count, begin + b) if b < valid else jnp.zeros((32, BLK), f32)
    for b in range(0, valid, 2):
        at = b * BLK
        left, right = features(split3(widened(scaled(coords_ref[:, begin * BLK + at : begin * BLK + at + 2 * BLK]))))
        left_ref[at : at + 2 * BLK, :] = jnp.transpose(left).astype(bf16)
        right_ref[:, at : at + 2 * BLK] = right.astype(bf16)

    rows = 128
    diagonal = [
        lax.broadcasted_iota(jnp.int32, (rows, BLK), 0) + rows * c
        == lax.broadcasted_iota(jnp.int32, (rows, BLK), 1)
        for c in range(BLK // rows)
    ]

    def block_x(b):
        return expanded(x_ref[:, pl.ds(pl.multiple_of(b * BLK, BLK), BLK)])

    def evaluate(n, step, next_ref):
        right = right_ref[:, pl.ds(pl.multiple_of(n * BLK, BLK), BLK)]
        for c in range(BLK // rows):
            left = left_ref[pl.ds(pl.multiple_of((n + step) * BLK, BLK) + rows * c, rows), :]
            block = matern(jnp.dot(left, right, preferred_element_type=f32))
            if step == 0:
                block = block + jnp.where(diagonal[c], nugget, 0.0)
            next_ref[step, rows * c : rows * c + rows, :] = block.astype(bf16)

    def both(i, kern_ref, n, next_ref):
        acc_i = acc_ref[i]
        x_i = block_x(i)
        weight_i = weight_ref[i]
        for step in range(3):
            j = i + step
            kern = kern_ref[step]
            part = jnp.dot(x_i if step == 0 else block_x(j), kern, preferred_element_type=f32)
            if step:
                mirror = lax.dot_general(x_i, kern, (((1,), (1,)), ((), ())), preferred_element_type=f32)
            if n is not None:
                evaluate(n, step, next_ref)
            acc_i = weighed(acc_i, part, weight_i, BL * step)
            if step:
                acc_ref[j] = weighed(acc_ref[j], mirror, weight_ref[j], -BL * step)
        acc_ref[i] = acc_i

    for step in range(3):
        evaluate(0, step, kerns[0])

    @pl.loop(0, blocks // 2 - 1)
    def _(m):
        both(2 * m, kerns[0], 2 * m + 1, kerns[1])
        both(2 * m + 1, kerns[1], 2 * m + 2, kerns[0])

    both(blocks - 2, kerns[0], blocks - 1, kerns[1])
    both(blocks - 1, kerns[1], None, None)
    for b in range(total):
        out_ref[:, b * BLK : b * BLK + BLK] = acc_ref[b]


CHUNKS = 4


def near_chunk(chunk, coords, points, near_rel, after):
    blocks = LEAF_DEV // BL // CHUNKS
    total = blocks + 2
    vmem = pl.BlockSpec(memory_space=pltpu.VMEM)
    return pl.pallas_call(
        functools.partial(near_kernel, chunk, blocks),
        out_shape=(
            jax.ShapeDtypeStruct((16, total * BLK), f32),
            jax.ShapeDtypeStruct((8, 128), f32),
        ),
        in_specs=[vmem] * 3 + [pl.BlockSpec(memory_space=pl.ANY)],
        out_specs=(vmem, vmem),
        scratch_shapes=[
            pltpu.VMEM((total * BLK, FEAT), bf16),
            pltpu.VMEM((FEAT, total * BLK), bf16),
            pltpu.VMEM((total, 32, BLK), f32),
            pltpu.VMEM((total, 16, BLK), f32),
            pltpu.VMEM((16, total * BLK), bf16),
            pltpu.VMEM((3, BLK, BLK), bf16),
            pltpu.VMEM((3, BLK, BLK), bf16),
        ],
        compiler_params=pltpu.CompilerParams(vmem_limit_bytes=16 * 1024 * 1024),
        cost_estimate=pl.CostEstimate(flops=1_000_000_000, bytes_accessed=1_000_000, transcendentals=4_000_000),
    )(coords, points, near_rel, after)


EDGES = ((0, -2, 0), (0, -1, 1), (1, -2, 1), (30, 2, 0), (31, 1, 0), (31, 2, 1))


def edge_products(left_halo, right_halo, coords_ref, rel_ref, add):
    count = slot_counts(rel_ref)
    halo_rows = []
    for halo in (left_halo, right_halo):
        splits = halo[:, SPAN * LEAF :].astype(f32)
        parts = [widened(splits[3 * k : 3 * k + 3]) for k in range(3)]
        halo_rows.append(jnp.transpose(features(parts)[0]).astype(bf16))
    for own in (0, 1, 30, 31):
        right = features(split3(widened(scaled(coords_ref[:, BLK * own : BLK * own + BLK]))))[1].astype(bf16)
        weight = spread_counts(count, own)
        acc = jnp.zeros((16, BLK), f32)
        for edge_own, offset, at in EDGES:
            if edge_own == own:
                side = 0 if offset < 0 else 1
                halo = (left_halo, right_halo)[side]
                left = halo_rows[side][BLK * at : BLK * at + BLK]
                kern = matern(jnp.dot(left, right, preferred_element_type=f32)).astype(bf16)
                part = jnp.dot(expanded(halo[:, BLK * at : BLK * at + BLK]), kern, preferred_element_type=f32)
                acc = weighed(acc, part, weight, BL * offset)
        add(own, acc)


TABLE = LEAF_DEV * RANK
STATE = 256
HALO = 2 * SPAN * LEAF
EDGE = TABLE + STATE
WIDTH = EDGE + HALO
FIRST = WIDTH + HALO
GROUPS = LEAF_DEV // 8
UPPER = 17
PARTNERS = (1, 2, 6, 8, 24, 32, 96)


def iota(shape, dim):
    return lax.broadcasted_iota(jnp.int32, shape, dim)


def where_eq(a, b):
    return jnp.where(a == b, 1.0, 0.0).astype(bf16)


def dot(a, b):
    return jnp.dot(a, b, preferred_element_type=f32)


def dot_nt(a, b):
    return lax.dot_general(a, b, (((1,), (1,)), ((), ())), preferred_element_type=f32)


def halves(v):
    high = v.astype(bf16)
    low = (v - high.astype(f32)).astype(bf16)
    return jnp.concatenate([high, low], axis=0)


def joined(v):
    rows = v.shape[0] // 2
    return v[:rows] + v[rows:]


def pack_state(first, second, third):
    parts = []
    for v in (first, second, third):
        high = v.astype(bf16).astype(f32)
        parts += [high, v - high]
    left = parts[0] + pltpu.roll(parts[1], 32, 1) + pltpu.roll(parts[2], 64, 1) + pltpu.roll(parts[3], 96, 1)
    right = parts[4] + pltpu.roll(parts[5], 32, 1)
    return jnp.concatenate([left, right], axis=1).astype(bf16)


def unpack_state(state):
    lanes = iota((16, 128), 1)
    left = state[:, :128].astype(f32)
    right = state[:, 128:].astype(f32)
    pair_left = left + pltpu.roll(left, 96, 1)
    pair_right = right + pltpu.roll(right, 96, 1)
    keep = lanes < RANK
    return (
        jnp.where(keep, pair_left, 0.0),
        jnp.where(keep, pltpu.roll(pair_left, 64, 1), 0.0),
        jnp.where(keep, pair_right, 0.0),
    )


def up_kernel(bits_ref, points_ref, coords_ref, basis_ref, local_ref, payload_ref, ub_ref, bd_ref, bdup_ref, rep_ref, x_ref, c_ref, y_ref):
    step = pl.program_id(0)
    lanes = iota((8, 256), 1) % 8
    rows = iota((8, 256), 0)

    @pl.when(step == 0)
    def _():
        rep_ref[...] = where_eq(iota((128, 1024), 0), iota((128, 1024), 1) // 8)
        column = iota((512, 512), 1)
        perm = where_eq(iota((512, 512), 0), (column % 8) * LEAF + column // 8)
        stacked = jnp.concatenate([points_ref[:, 512 * g : 512 * g + 512] for g in range(GROUPS)], axis=0)
        x_ref[...] = dot(stacked, perm).astype(bf16)
    basis = basis_ref[...]
    wide = dot(jnp.concatenate([basis[:, 128 * k : 128 * k + 128] for k in range(16)], axis=0), rep_ref[...])
    keep = lanes == rows
    for e in range(2):
        for p in range(0, LEAF, 2):
            both = []
            for q in (p, p + 1):
                k, low = q // 4, q % 4
                both.append(jnp.where(keep, wide[16 * k + 8 * e : 16 * k + 8 * e + 8, 256 * low : 256 * low + 256], 0.0))
            ub_ref[e, 8 * p : 8 * p + 16, :] = jnp.concatenate(both, axis=0).astype(bf16)
    local = local_ref[pl.ds(pl.multiple_of(16 * step, 16), 16), :]
    wide = dot(jnp.concatenate([local[:, 128 * k : 128 * k + 128] for k in range(8)], axis=0), rep_ref[...])
    total = jnp.zeros((16, 256), f32)
    for e in range(2):
        keep = lanes == rows // 2 + 4 * e
        for a in range(0, RANK, 2):
            both = []
            for q in (a, a + 1):
                k, low = q // 4, q % 4
                both.append(jnp.where(keep, wide[16 * k + 8 * e : 16 * k + 8 * e + 8, 256 * low : 256 * low + 256], 0.0))
            bd_ref[e, 8 * a : 8 * a + 16, :] = jnp.concatenate(both, axis=0).astype(bf16)
        own = x_ref[pl.ds(pl.multiple_of(32 * step + 16 * e, 16), 16), :]
        coeff = dot(own, ub_ref[e]).astype(bf16)
        payload_ref[:, pl.ds(pl.multiple_of(512 * step + 256 * e, 256), 256)] = coeff
        total = total + dot(coeff, bd_ref[e])
    c_ref[pl.ds(pl.multiple_of(16 * step, 16), 16), :] = total

    @pl.when(step == GROUPS // 2 - 1)
    def _():
        for k in range(8):
            y_ref[k, 0:126, :] = dot(local_ref[128:254, 128 * k : 128 * k + 128], rep_ref[...])
        tile = 0
        for level_tiles in (8, 4, 2, 1):
            for q in range(level_tiles):
                fill_upper(y_ref, bdup_ref, tile, tile, lanes == rows // 2 + 4 * (q % 2))
                tile += 1
        fill_upper(y_ref, bdup_ref, 15, 15, (lanes == rows // 2 + 4) & (rows < 4))
        fill_upper(y_ref, bdup_ref, 16, 15, (lanes == 0) & (rows >= 4) & (rows < 6))
        current = [c_ref[16 * q : 16 * q + 16, :] for q in range(8)]
        tile = 0
        for level_tiles in (8, 4, 2, 1, 1, 1):
            parts = [joined(dot(halves(current[q]), bdup_ref[tile + q])) for q in range(level_tiles)]
            tile += level_tiles
            if level_tiles > 1:
                current = [parts[2 * q] + parts[2 * q + 1] for q in range(level_tiles // 2)]
            else:
                current = parts
        squeeze = where_eq(iota((256, 128), 0), iota((256, 128), 1) * 8)
        mine = joined(dot(halves(current[0]), squeeze))
        zero = jnp.zeros_like(mine)
        payload_ref[:, TABLE:EDGE] = pack_state(mine, zero, zero)
        head = side(points_ref, coords_ref, 0)
        tail = side(points_ref, coords_ref, (LEAF_DEV - SPAN) * LEAF)
        even = bits_ref[0] == 0
        payload_ref[:, EDGE:WIDTH] = jnp.where(even, tail, head)
        payload_ref[:, WIDTH:] = jnp.where(even, head, tail)


def side(points_ref, coords_ref, start):
    end = start + SPAN * LEAF
    parts = split3(scaled(coords_ref[:, start:end]))
    rows = jnp.concatenate(list(parts) + [jnp.zeros((7, SPAN * LEAF), f32)], axis=0)
    return jnp.concatenate([points_ref[:, start:end], rows.astype(bf16)], axis=1)


def open_kernel(nodes_ref, transfer_ref, couple_ref, after_ref, em_ref, sm_ref, token_ref, rows_ref, sem):
    del after_ref
    token_ref[...] = jnp.zeros_like(token_ref)
    copies = [
        pltpu.make_async_copy(couple_ref.at[pl.ds(nodes_ref[k], 1)], rows_ref.at[pl.ds(k, 1)], sem.at[k])
        for k in range(6)
    ]
    for copy in copies:
        copy.start()
    which = iota((16, 254), 0)
    wanted = jnp.full((16, 254), -1, jnp.int32)
    for k in range(5):
        first = nodes_ref[k] - nodes_ref[8 + k]
        wanted = jnp.where(which == 2 * k, first, wanted)
        wanted = jnp.where(which == 2 * k + 1, first + 1, wanted)
    pairs = dot(where_eq(wanted, iota((16, 254), 1)), transfer_ref[...])
    fold_row = iota((1024, 128), 0) % RANK
    fold_col = iota((1024, 128), 1)
    fold_first = where_eq(fold_row, fold_col)
    fold_second = where_eq(fold_row + RANK, fold_col)
    own = iota((RANK, 1024), 1) // RANK == iota((RANK, 1024), 0)

    def opened(values, k):
        return jnp.where(own, values[k : k + 1, :], 0.0).astype(bf16)

    for copy in copies:
        copy.wait()
    couples = [rows_ref[k].astype(f32) for k in range(6)]
    em_ref[...] = dot(jnp.concatenate([opened(pairs, k) for k in range(10)], axis=0), fold_first).astype(bf16)
    sm_ref[...] = (
        dot(jnp.concatenate([opened(couples[k], 0) for k in range(6)], axis=0), fold_first)
        + dot(jnp.concatenate([opened(couples[k], 1) for k in range(6)], axis=0), fold_second)
    ).astype(bf16)


def opened_top(nodes, top_transfer, top_coupling, after):
    vmem = pl.BlockSpec(memory_space=pltpu.VMEM)
    anywhere = pl.BlockSpec(memory_space=pl.ANY)
    return pl.pallas_call(
        open_kernel,
        out_shape=(
            jax.ShapeDtypeStruct((320, 128), bf16),
            jax.ShapeDtypeStruct((192, 128), bf16),
            jax.ShapeDtypeStruct((8, 128), f32),
        ),
        in_specs=[pl.BlockSpec(memory_space=pltpu.SMEM), vmem, anywhere, anywhere],
        out_specs=(vmem, vmem, vmem),
        scratch_shapes=[pltpu.VMEM((6, 2, 1024), bf16), pltpu.SemaphoreType.DMA((6,))],
        compiler_params=pltpu.CompilerParams(vmem_limit_bytes=60 * 1024 * 1024),
        cost_estimate=pl.CostEstimate(flops=100_000_000, bytes_accessed=800_000, transcendentals=0),
    )(nodes, top_transfer, top_coupling, after)


def fill_upper(y_ref, bdup_ref, target, tile, keep):
    for a in range(0, RANK, 2):
        both = []
        for q in (a, a + 1):
            k, low = q // 4, q % 4
            both.append(jnp.where(keep, y_ref[k, 8 * tile : 8 * tile + 8, 256 * low : 256 * low + 256], 0.0))
        bdup_ref[target, 8 * a : 8 * a + 16, :] = jnp.concatenate(both, axis=0).astype(bf16)


def upward(bits, points, coords, basis, local_transfer):
    full = lambda *shape: pl.BlockSpec(shape, lambda i: (0,) * len(shape))
    return pl.pallas_call(
        up_kernel,
        grid=(GROUPS // 2,),
        out_shape=(
            jax.ShapeDtypeStruct((16, FIRST), bf16),
            jax.ShapeDtypeStruct((GROUPS, 512, 256), bf16),
            jax.ShapeDtypeStruct((GROUPS, 256, 256), bf16),
            jax.ShapeDtypeStruct((UPPER, 256, 256), bf16),
        ),
        in_specs=[
            pl.BlockSpec(memory_space=pltpu.SMEM),
            full(16, LEAF_DEV * LEAF),
            full(3, LEAF_DEV * LEAF),
            pl.BlockSpec((16, LEAF * RANK), lambda i: (i, 0)),
            full(254, 1024),
        ],
        out_specs=(
            full(16, FIRST),
            pl.BlockSpec((2, 512, 256), lambda i: (i, 0, 0)),
            pl.BlockSpec((2, 256, 256), lambda i: (i, 0, 0)),
            full(UPPER, 256, 256),
        ),
        scratch_shapes=[
            pltpu.VMEM((128, 1024), bf16),
            pltpu.VMEM((256, 512), bf16),
            pltpu.VMEM((128, 256), f32),
            pltpu.VMEM((8, 128, 1024), f32),
        ],
        compiler_params=pltpu.CompilerParams(vmem_limit_bytes=60 * 1024 * 1024),
        cost_estimate=pl.CostEstimate(flops=1_000_000_000, bytes_accessed=10_000_000, transcendentals=0),
    )(bits, points, coords, basis, local_transfer)


def step_kernel(height, bits_ref, first_ref, payload_ref, received_ref, em_ref, after_ref, next_ref):
    del after_ref
    forward = height % 2 == 1
    next_ref[:, :TABLE] = received_ref[:, :TABLE] if forward else first_ref[:, :TABLE]
    start = WIDTH if height == 0 else EDGE
    next_ref[:, EDGE:] = payload_ref[:, EDGE:WIDTH] if forward else received_ref[:, start : start + HALO]
    mine, _, _ = unpack_state(payload_ref[:, TABLE:EDGE])
    sibling, _, _ = unpack_state(received_ref[:, TABLE:EDGE])
    if height <= 4:
        first = bits_ref[height] == 0
        left = jnp.where(first, mine, sibling)
        right = jnp.where(first, sibling, mine)
        both = (left + pltpu.roll(right, 32, 1))[:, : 2 * RANK]
        parent = joined(dot(halves(both), em_ref[64 * height : 64 * height + 64, :]))
    else:
        parent = jnp.zeros_like(mine)
    next_ref[:, TABLE:EDGE] = pack_state(parent, mine, sibling)


def tree_step(height, bits, first, payload, received, em, after):
    vmem = pl.BlockSpec(memory_space=pltpu.VMEM)
    return pl.pallas_call(
        functools.partial(step_kernel, height),
        out_shape=jax.ShapeDtypeStruct((16, WIDTH), bf16),
        in_specs=[pl.BlockSpec(memory_space=pltpu.SMEM)] + [vmem] * 4 + [pl.BlockSpec(memory_space=pl.ANY)],
        out_specs=vmem,
        compiler_params=pltpu.CompilerParams(vmem_limit_bytes=4 * 1024 * 1024),
        cost_estimate=pl.CostEstimate(flops=1_000_000, bytes_accessed=400_000, transcendentals=0),
    )(bits, first, payload, received, em, after)


def regroup_kernel(c_ref, after_ref, out_ref, token_ref):
    del after_ref
    token_ref[...] = jnp.zeros_like(token_ref)
    row = iota((128, 128), 0)
    perm = where_eq((row % 8) * NF + row // 8, iota((128, 128), 1))
    x = dot(perm, c_ref[...].reshape(128, 1024))
    lanes = iota((8, 128), 1)
    low_half = lanes < 64
    even = (lanes // RANK) % 2 == 0
    for s_high in range(4):
        for a_high in range(8):
            v = [
                x[32 * s_high + 8 * k : 32 * s_high + 8 * k + 8, 128 * a_high : 128 * a_high + 128]
                for k in range(4)
            ]
            u0 = jnp.where(low_half, v[0], pltpu.roll(v[2], 64, 1))
            u2 = jnp.where(low_half, pltpu.roll(v[0], 64, 1), v[2])
            u1 = jnp.where(low_half, v[1], pltpu.roll(v[3], 64, 1))
            u3 = jnp.where(low_half, pltpu.roll(v[1], 64, 1), v[3])
            w = []
            for p, q in ((u0, u1), (u2, u3)):
                w.append(jnp.where(even, p, pltpu.roll(q, 32, 1)))
                w.append(jnp.where(even, pltpu.roll(p, 96, 1), q))
            lane = 128 * s_high
            row = 32 * a_high
            out_ref[0, row : row + 16, lane : lane + 128] = jnp.concatenate(w[:2], axis=0).astype(bf16)
            out_ref[0, row + 16 : row + 32, lane : lane + 128] = jnp.concatenate(w[2:], axis=0).astype(bf16)


def regroup(half, far_coupling, after):
    groups = GROUPS // 2
    return pl.pallas_call(
        regroup_kernel,
        grid=(groups,),
        out_shape=(
            jax.ShapeDtypeStruct((groups, 256, 512), bf16),
            jax.ShapeDtypeStruct((8, 128), f32),
        ),
        in_specs=[
            pl.BlockSpec((8, NF, 1024), lambda i: (i + half * groups, 0, 0)),
            pl.BlockSpec(memory_space=pl.ANY),
        ],
        out_specs=(
            pl.BlockSpec((1, 256, 512), lambda i: (i, 0, 0)),
            pl.BlockSpec((8, 128), lambda i: (0, 0)),
        ),
        compiler_params=pltpu.CompilerParams(vmem_limit_bytes=60 * 1024 * 1024),
        cost_estimate=pl.CostEstimate(flops=600_000_000, bytes_accessed=4_200_000, transcendentals=0),
    )(far_coupling, after)


def down_kernel(bits_ref, index_ref, payload_ref, *refs):
    received = refs[:7]
    em_ref, sm_ref, bdup_ref, coords_ref, rel_ref, d0_ref, d1_ref, ub_ref, bd_ref, near0_ref, near1_ref, near2_ref, near3_ref, out_ref, table_ref, field_ref, far_ref, gather_ref, edge_ref = refs[7:]
    step = pl.program_id(0)

    @pl.when(step == 0)
    def _():
        column = iota((256, 1024), 1)
        repeat = where_eq(iota((256, 1024), 0), (column % RANK) * 8 + column // 128)
        for k, ref in enumerate((payload_ref,) + received):
            stacked = jnp.concatenate([ref[:, 256 * g : 256 * g + 256] for g in range(GROUPS)], axis=0)
            wide = dot(stacked, repeat).astype(bf16)
            for m in range(8):
                table_ref[2048 * k + 256 * m : 2048 * k + 256 * m + 256, :] = wide[:, 128 * m : 128 * m + 128]
        table_ref[16384:16400, :] = jnp.zeros((16, 128), bf16)
        terms = []
        for height in range(1, 7):
            _, before_mine, before_sibling = unpack_state(received[height][:, TABLE:EDGE])
            plain = (bits_ref[height - 1] == 0) == (height % 2 == 1)
            left = jnp.where(plain, before_mine, before_sibling)
            right = jnp.where(plain, before_sibling, before_mine)
            both = left + pltpu.roll(right, 32, 1)
            terms.append(joined(dot_nt(halves(both), sm_ref[32 * height - 32 : 32 * height, :])))
        field = terms[5]
        for height in range(5, 0, -1):
            row = pl.multiple_of(64 * (height - 1) + 32 * bits_ref[height - 1], 32)
            matrix = em_ref[pl.ds(row, 32), 0:RANK]
            field = terms[height - 1] + joined(dot_nt(halves(field), matrix))
        stretch = where_eq(iota((RANK, 256), 0) * 8, iota((RANK, 256), 1))
        fields = [joined(dot(halves(field), stretch))]
        tile = UPPER
        for level_tiles in (1, 1, 1, 2, 4, 8):
            tile -= level_tiles
            fields = [
                joined(dot_nt(halves(fields[q // 2 if level_tiles > 1 else 0]), bdup_ref[tile + q]))
                for q in range(level_tiles)
            ]
        near_side = received[0][:, EDGE:WIDTH]
        far_side = received[1][:, EDGE:WIDTH]
        for height in range(2, 7):
            far_side = jnp.where(bits_ref[7] == height, received[height][:, EDGE:WIDTH], far_side)
        even = bits_ref[0] == 0
        left_halo = jnp.where(even, far_side, near_side)
        right_halo = jnp.where(even, near_side, far_side)

        def add(own, acc):
            edge_ref[own % 4] = acc

        edge_products(left_halo, right_halo, coords_ref, rel_ref, add)
        for q in range(8):
            field_ref[32 * q : 32 * q + 32, :] = halves(fields[q])

    block = iota((16, 128), 1) // RANK
    for leaf in range(8):
        for s_high in range(4):
            merged = None
            for low in range(4):
                entry = index_ref[(8 * step + leaf) * NF + 4 * s_high + low]
                value = table_ref[pl.ds(pl.multiple_of(entry * 16, 16), 16), :]
                merged = value if low == 0 else jnp.where(block == low, value, merged)
            gather_ref[16 * leaf : 16 * leaf + 16, 128 * s_high : 128 * s_high + 128] = merged
    coupling = jnp.where(step < GROUPS // 2, d0_ref[0], d1_ref[0])
    result = dot_nt(gather_ref[...], coupling)
    which = iota((16, 256), 1) % 8
    far = result[0:16]
    for leaf in range(1, 8):
        far = jnp.where(which == leaf, result[16 * leaf : 16 * leaf + 16], far)
    parent = field_ref[pl.ds(pl.multiple_of(32 * (step // 2), 32), 32), :]
    leaf_field = (far + joined(dot_nt(parent, bd_ref[0]))).astype(bf16)
    part = dot_nt(leaf_field, ub_ref[0])
    high = part.astype(bf16)
    far_ref[pl.ds(pl.multiple_of(16 * step, 16), 16), :] = high
    far_ref[pl.ds(pl.multiple_of(256 + 16 * step, 16), 16), :] = (part - high.astype(f32)).astype(bf16)

    @pl.when(step == GROUPS - 1)
    def _():
        column = iota((512, 512), 1)
        perm = where_eq(iota((512, 512), 0), (column % LEAF) * 8 + column // LEAF)
        whole = joined(dot(far_ref[...], perm))
        nears = (near0_ref, near1_ref, near2_ref, near3_ref)
        for g in range(GROUPS):
            per = GROUPS // CHUNKS
            chunk, place = g // per, 512 * (g % per)
            value = nears[chunk][:, place : place + 512] + whole[16 * g : 16 * g + 16, :]
            if chunk and g % per == 0:
                value = value + nears[chunk - 1][:, 512 * per : 512 * per + 512]
            if g == 0:
                value = value + jnp.concatenate([edge_ref[0], edge_ref[1]], axis=1)
            if g == GROUPS - 1:
                value = value + jnp.concatenate([edge_ref[2], edge_ref[3]], axis=1)
            out_ref[:, 512 * g : 512 * g + 512] = value


def downward(bits, index, payload, received, em, sm, bdup, coords, near_rel, d, ub, bd, nears):
    full = lambda *shape: pl.BlockSpec(shape, lambda i: (0,) * len(shape))
    smem = pl.BlockSpec(memory_space=pltpu.SMEM)
    each = lambda *shape: pl.BlockSpec((1,) + shape, lambda i: (i, 0, 0))
    return pl.pallas_call(
        down_kernel,
        grid=(GROUPS,),
        out_shape=jax.ShapeDtypeStruct((16, LEAF_DEV * LEAF), f32),
        in_specs=[smem, smem]
        + [full(16, FIRST)] * 2
        + [full(16, WIDTH)] * 6
        + [full(320, 128), full(192, 128), full(UPPER, 256, 256)]
        + [full(3, LEAF_DEV * LEAF), full(NN, LEAF_DEV)]
        + [
            pl.BlockSpec((1, 256, 512), lambda i: (jnp.minimum(i, GROUPS // 2 - 1), 0, 0)),
            pl.BlockSpec((1, 256, 512), lambda i: (jnp.maximum(i - GROUPS // 2, 0), 0, 0)),
        ]
        + [each(512, 256), each(256, 256)]
        + [full(16, (LEAF_DEV // BL // CHUNKS + 2) * BLK)] * CHUNKS,
        out_specs=full(16, LEAF_DEV * LEAF),
        scratch_shapes=[
            pltpu.VMEM((16400, 128), bf16),
            pltpu.VMEM((256, 256), bf16),
            pltpu.VMEM((512, 512), bf16),
            pltpu.VMEM((128, 512), bf16),
            pltpu.VMEM((4, 16, BLK), f32),
        ],
        compiler_params=pltpu.CompilerParams(vmem_limit_bytes=24 * 1024 * 1024),
        cost_estimate=pl.CostEstimate(flops=3_000_000_000, bytes_accessed=16_000_000, transcendentals=0),
    )(bits, index, payload, *received, em, sm, bdup, coords, near_rel, *d, ub, bd, *nears)


def top_start(height, number):
    if height == 0:
        return 0
    return 2 * number - number // 2 ** (height - 1)


def per_device(
    points,
    coords,
    basis,
    far_list,
    far_coupling,
    near_list,
    local_transfer,
    top_transfer,
    top_coupling,
):
    device = lax.axis_index("leaf")
    outer = jnp.bitwise_xor(device, device + 2 * (device & 1) - 1)
    level = sum((outer >> k > 0).astype(jnp.int32) for k in range(7)) - 1
    number = jnp.arange(8, dtype=jnp.int32)
    bits = jnp.where(number == 7, jnp.maximum(level, 1), jnp.right_shift(device, number) & 1)
    starts = jnp.array([top_start(h, N_DEV) for h in range(6)], jnp.int32)
    heights = jnp.arange(6, dtype=jnp.int32)
    parity = jnp.right_shift(device, heights) & 1
    blank = jnp.zeros((2,), jnp.int32)
    nodes = jnp.concatenate([starts + jnp.right_shift(device, heights), blank, parity, blank])
    owner = jnp.bitwise_xor(jnp.right_shift(far_list, 7), device)
    slot = sum((owner >> k > 0).astype(jnp.int32) for k in range(7))
    within = far_list & (LEAF_DEV - 1)
    entry = slot * LEAF_DEV + (within & 7) * GROUPS + (within >> 3)
    index = jnp.where(far_list >= 0, entry, 8 * LEAF_DEV).reshape(LEAF_DEV * NF)
    payload, ub, bd, bdup = upward(bits, points, coords, basis, local_transfer)
    near_rel = jnp.transpose(jnp.where(near_list >= 0, near_list - device * LEAF_DEV, -1000))
    first = payload
    received = []
    nears = []
    halves_of = []
    for height, mask in enumerate(PARTNERS):
        route = [(i, i ^ mask) for i in range(N_DEV)]
        received.append(lax.ppermute(payload, "leaf", route))
        if height == 0:
            em, sm, token = opened_top(nodes, top_transfer, top_coupling, payload)
        elif height in (4, 5):
            part, token = regroup(height - 4, far_coupling, payload)
            halves_of.append(part)
        else:
            part, token = near_chunk(len(nears), coords, points, near_rel, payload)
            nears.append(part)
        if height < 6:
            payload = tree_step(height, bits, first, payload, received[height], em, token)
    return downward(bits, index, first, received, em, sm, bdup, coords, near_rel, halves_of, ub, bd, nears)


def solution(mesh):
    return jax.shard_map(
        per_device,
        mesh=mesh,
        in_specs=(
            P(None, "leaf"),
            P(None, "leaf"),
            P("leaf", None),
            P("leaf", None),
            P("leaf", None, None),
            P("leaf", None),
            P("leaf", None),
            P(),
            P(),
        ),
        out_specs=P(None, "leaf"),
        check_vma=False,
    )
```

```python
import functools
import math

import jax
import jax.numpy as jnp
from jax import lax
from jax.experimental import pallas as pl
from jax.experimental.pallas import tpu as pltpu
from jax.sharding import PartitionSpec as P

LEAF = 64
RANK = 32
NF = 16
NN = 12
SPAN = 8
LEAF_DEV = 128
N_DEV = 128


variance = 1.0
nugget = 0.5
decay_rate = math.sqrt(3.0) / 0.3
highest = lax.Precision.HIGHEST


LOG2E = 1.4426950408889634
LN2 = 0.6931471805599453
SCALE = decay_rate * LOG2E
BLK = 256
BL = BLK // LEAF
FEAT = 64
f32 = jnp.float32
bf16 = jnp.bfloat16


def split3(v):
    a = v.astype(bf16).astype(f32)
    rest = v - a
    b = rest.astype(bf16).astype(f32)
    c = (rest - b).astype(bf16).astype(f32)
    return a, b, c


def scaled(coords):
    return (coords - 0.5) * SCALE


def widened(v):
    return jnp.concatenate([v, jnp.zeros((5, v.shape[1]), f32)], axis=0)


def features(parts):
    a, b, c = parts
    n = a.shape[1]
    v = a + b + c
    norm = split3(jnp.sum(v * v, axis=0, keepdims=True))
    row = lax.broadcasted_iota(jnp.int32, (8, n), 0)

    def place(first, second):
        out = jnp.zeros((8, n), f32)
        for k in range(3):
            out = jnp.where(row == k, first[k], out)
            out = jnp.where(row == k + 3, second[k], out)
        return out

    ones = [jnp.ones((1, n), f32)] * 3
    zero = jnp.zeros((8, n), f32)
    left = jnp.concatenate([a, a, a, b, b, c, place(norm, ones), zero], axis=0)
    a2, b2, c2 = -2.0 * a, -2.0 * b, -2.0 * c
    right = jnp.concatenate([a2, b2, c2, a2, b2, a2, place(ones, norm), zero], axis=0)
    return left, right


def matern(squared):
    m = jnp.maximum(squared, 1e-20)
    t = m * lax.rsqrt(m)
    return (variance + (variance * LN2) * t) * jnp.exp2(-t)


def expanded(x):
    leaf_of_lane = lax.broadcasted_iota(jnp.int32, (16, BLK), 1) // LEAF
    zero = jnp.zeros_like(x)
    return jnp.concatenate([jnp.where(leaf_of_lane == j, x, zero) for j in range(BL)], axis=0)


def slot_counts(rel_ref):
    leaf = lax.broadcasted_iota(jnp.int32, (32, LEAF_DEV), 1)
    row = lax.broadcasted_iota(jnp.int32, (32, LEAF_DEV), 0)
    base = (leaf // BL) * BL - SPAN
    count = jnp.zeros((32, LEAF_DEV), f32)
    for s in range(NN):
        count = count + jnp.where(rel_ref[s : s + 1, :] - base == row, 1.0, 0.0)
    return count


def spread_counts(count, b):
    spread = (
        lax.broadcasted_iota(jnp.int32, (LEAF_DEV, BLK), 0)
        == lax.broadcasted_iota(jnp.int32, (LEAF_DEV, BLK), 1) // LEAF
    ).astype(f32).astype(bf16)
    shifted = pltpu.roll(count, (LEAF_DEV - BL * b) % LEAF_DEV, 1) if b else count
    return jnp.dot(shifted.astype(bf16), spread, preferred_element_type=f32)


def weighed(acc, part, weight, offset):
    for k in range(BL):
        acc = acc + part[16 * k : 16 * k + 16] * weight[SPAN + offset + k : SPAN + offset + k + 1]
    return acc


def near_kernel(chunk, blocks, coords_ref, points_ref, rel_ref, after_ref, out_ref, token_ref, left_ref, right_ref, weight_ref, acc_ref, x_ref, *kerns):
    del after_ref
    total = blocks + 2
    begin = chunk * blocks
    valid = min(total, LEAF_DEV // BL - begin)
    token_ref[...] = jnp.zeros_like(token_ref)
    count = slot_counts(rel_ref)
    x_ref[:, : valid * BLK] = points_ref[:, begin * BLK : (begin + valid) * BLK]
    if valid < total:
        x_ref[:, valid * BLK :] = jnp.zeros((16, (total - valid) * BLK), bf16)
        left_ref[valid * BLK :, :] = jnp.zeros(((total - valid) * BLK, FEAT), bf16)
    for b in range(total):
        acc_ref[b] = jnp.zeros((16, BLK), f32)
        weight_ref[b] = spread_counts(count, begin + b) if b < valid else jnp.zeros((32, BLK), f32)
    for b in range(0, valid, 2):
        at = b * BLK
        left, right = features(split3(widened(scaled(coords_ref[:, begin * BLK + at : begin * BLK + at + 2 * BLK]))))
        left_ref[at : at + 2 * BLK, :] = jnp.transpose(left).astype(bf16)
        right_ref[:, at : at + 2 * BLK] = right.astype(bf16)

    rows = 128
    diagonal = [
        lax.broadcasted_iota(jnp.int32, (rows, BLK), 0) + rows * c
        == lax.broadcasted_iota(jnp.int32, (rows, BLK), 1)
        for c in range(BLK // rows)
    ]

    def block_x(b):
        return expanded(x_ref[:, pl.ds(pl.multiple_of(b * BLK, BLK), BLK)])

    def evaluate(n, step, next_ref):
        right = right_ref[:, pl.ds(pl.multiple_of(n * BLK, BLK), BLK)]
        for c in range(BLK // rows):
            left = left_ref[pl.ds(pl.multiple_of((n + step) * BLK, BLK) + rows * c, rows), :]
            block = matern(jnp.dot(left, right, preferred_element_type=f32))
            if step == 0:
                block = block + jnp.where(diagonal[c], nugget, 0.0)
            next_ref[step, rows * c : rows * c + rows, :] = block.astype(bf16)

    def both(i, kern_ref, n, next_ref):
        acc_i = acc_ref[i]
        x_i = block_x(i)
        weight_i = weight_ref[i]
        for step in range(3):
            j = i + step
            kern = kern_ref[step]
            part = jnp.dot(x_i if step == 0 else block_x(j), kern, preferred_element_type=f32)
            if step:
                mirror = lax.dot_general(x_i, kern, (((1,), (1,)), ((), ())), preferred_element_type=f32)
            if n is not None:
                evaluate(n, step, next_ref)
            acc_i = weighed(acc_i, part, weight_i, BL * step)
            if step:
                acc_ref[j] = weighed(acc_ref[j], mirror, weight_ref[j], -BL * step)
        acc_ref[i] = acc_i

    for step in range(3):
        evaluate(0, step, kerns[0])

    @pl.loop(0, blocks // 2 - 1)
    def _(m):
        both(2 * m, kerns[0], 2 * m + 1, kerns[1])
        both(2 * m + 1, kerns[1], 2 * m + 2, kerns[0])

    both(blocks - 2, kerns[0], blocks - 1, kerns[1])
    both(blocks - 1, kerns[1], None, None)
    for b in range(total):
        out_ref[:, b * BLK : b * BLK + BLK] = acc_ref[b]


CHUNKS = 4


def near_chunk(chunk, coords, points, near_rel, after):
    blocks = LEAF_DEV // BL // CHUNKS
    total = blocks + 2
    vmem = pl.BlockSpec(memory_space=pltpu.VMEM)
    return pl.pallas_call(
        functools.partial(near_kernel, chunk, blocks),
        out_shape=(
            jax.ShapeDtypeStruct((16, total * BLK), f32),
            jax.ShapeDtypeStruct((8, 128), f32),
        ),
        in_specs=[vmem] * 3 + [pl.BlockSpec(memory_space=pl.ANY)],
        out_specs=(vmem, vmem),
        scratch_shapes=[
            pltpu.VMEM((total * BLK, FEAT), bf16),
            pltpu.VMEM((FEAT, total * BLK), bf16),
            pltpu.VMEM((total, 32, BLK), f32),
            pltpu.VMEM((total, 16, BLK), f32),
            pltpu.VMEM((16, total * BLK), bf16),
            pltpu.VMEM((3, BLK, BLK), bf16),
            pltpu.VMEM((3, BLK, BLK), bf16),
        ],
        compiler_params=pltpu.CompilerParams(vmem_limit_bytes=16 * 1024 * 1024),
        cost_estimate=pl.CostEstimate(flops=1_000_000_000, bytes_accessed=1_000_000, transcendentals=4_000_000),
    )(coords, points, near_rel, after)


EDGES = ((0, -2, 0), (0, -1, 1), (1, -2, 1), (30, 2, 0), (31, 1, 0), (31, 2, 1))


def edge_products(left_halo, right_halo, coords_ref, rel_ref, add):
    count = slot_counts(rel_ref)
    halo_rows = []
    for halo in (left_halo, right_halo):
        splits = halo[:, SPAN * LEAF :].astype(f32)
        parts = [widened(splits[3 * k : 3 * k + 3]) for k in range(3)]
        halo_rows.append(jnp.transpose(features(parts)[0]).astype(bf16))
    for own in (0, 1, 30, 31):
        right = features(split3(widened(scaled(coords_ref[:, BLK * own : BLK * own + BLK]))))[1].astype(bf16)
        weight = spread_counts(count, own)
        acc = jnp.zeros((16, BLK), f32)
        for edge_own, offset, at in EDGES:
            if edge_own == own:
                side = 0 if offset < 0 else 1
                halo = (left_halo, right_halo)[side]
                left = halo_rows[side][BLK * at : BLK * at + BLK]
                kern = matern(jnp.dot(left, right, preferred_element_type=f32)).astype(bf16)
                part = jnp.dot(expanded(halo[:, BLK * at : BLK * at + BLK]), kern, preferred_element_type=f32)
                acc = weighed(acc, part, weight, BL * offset)
        add(own, acc)


TABLE = LEAF_DEV * RANK
STATE = 256
HALO = 2 * SPAN * LEAF
EDGE = TABLE + STATE
WIDTH = EDGE + HALO
FIRST = WIDTH + HALO
GROUPS = LEAF_DEV // 8
UPPER = 17
PARTNERS = (1, 2, 6, 8, 24, 32, 96)


def iota(shape, dim):
    return lax.broadcasted_iota(jnp.int32, shape, dim)


def where_eq(a, b):
    return jnp.where(a == b, 1.0, 0.0).astype(bf16)


def dot(a, b):
    return jnp.dot(a, b, preferred_element_type=f32)


def dot_nt(a, b):
    return lax.dot_general(a, b, (((1,), (1,)), ((), ())), preferred_element_type=f32)


def halves(v):
    high = v.astype(bf16)
    low = (v - high.astype(f32)).astype(bf16)
    return jnp.concatenate([high, low], axis=0)


def joined(v):
    rows = v.shape[0] // 2
    return v[:rows] + v[rows:]


def pack_state(first, second, third):
    parts = []
    for v in (first, second, third):
        high = v.astype(bf16).astype(f32)
        parts += [high, v - high]
    left = parts[0] + pltpu.roll(parts[1], 32, 1) + pltpu.roll(parts[2], 64, 1) + pltpu.roll(parts[3], 96, 1)
    right = parts[4] + pltpu.roll(parts[5], 32, 1)
    return jnp.concatenate([left, right], axis=1).astype(bf16)


def unpack_state(state):
    lanes = iota((16, 128), 1)
    left = state[:, :128].astype(f32)
    right = state[:, 128:].astype(f32)
    pair_left = left + pltpu.roll(left, 96, 1)
    pair_right = right + pltpu.roll(right, 96, 1)
    keep = lanes < RANK
    return (
        jnp.where(keep, pair_left, 0.0),
        jnp.where(keep, pltpu.roll(pair_left, 64, 1), 0.0),
        jnp.where(keep, pair_right, 0.0),
    )


def up_step(step, lanes, rows, basis_ref, local_ref, payload_ref, ub_ref, bd_ref, rep_ref, x_ref, c_ref):
    basis = basis_ref[16 * step : 16 * step + 16, :]
    wide = dot(jnp.concatenate([basis[:, 128 * k : 128 * k + 128] for k in range(16)], axis=0), rep_ref[...])
    keep = lanes == rows
    for e in range(2):
        for p in range(0, LEAF, 2):
            both = []
            for q in (p, p + 1):
                k, low = q // 4, q % 4
                both.append(jnp.where(keep, wide[16 * k + 8 * e : 16 * k + 8 * e + 8, 256 * low : 256 * low + 256], 0.0))
            ub_ref[2 * step + e, 8 * p : 8 * p + 16, :] = jnp.concatenate(both, axis=0).astype(bf16)
    local = local_ref[16 * step : 16 * step + 16, :]
    wide = dot(jnp.concatenate([local[:, 128 * k : 128 * k + 128] for k in range(8)], axis=0), rep_ref[...])
    total = jnp.zeros((16, 256), f32)
    for e in range(2):
        keep = lanes == rows // 2 + 4 * e
        for a in range(0, RANK, 2):
            both = []
            for q in (a, a + 1):
                k, low = q // 4, q % 4
                both.append(jnp.where(keep, wide[16 * k + 8 * e : 16 * k + 8 * e + 8, 256 * low : 256 * low + 256], 0.0))
            bd_ref[2 * step + e, 8 * a : 8 * a + 16, :] = jnp.concatenate(both, axis=0).astype(bf16)
        own = x_ref[32 * step + 16 * e : 32 * step + 16 * e + 16, :]
        coeff = dot(own, ub_ref[2 * step + e]).astype(bf16)
        payload_ref[:, 512 * step + 256 * e : 512 * step + 256 * e + 256] = coeff
        total = total + dot(coeff, bd_ref[2 * step + e])
    c_ref[16 * step : 16 * step + 16, :] = total


def up_kernel(bits_ref, points_in, coords_in, basis_in, local_in, payload_ref, ub_out, bd_out, bdup_out, rep_ref, x_ref, c_ref, y_ref, points_ref, coords_ref, basis_ref, local_ref, ub_ref, bd_ref, bdup_ref, in_sem, out_sem):
    arrivals = [
        pltpu.make_async_copy(source, target, in_sem.at[k])
        for k, (source, target) in enumerate(
            ((points_in, points_ref), (basis_in, basis_ref), (local_in, local_ref), (coords_in, coords_ref))
        )
    ]
    for copy in arrivals:
        copy.start()
    lanes = iota((8, 256), 1) % 8
    rows = iota((8, 256), 0)
    rep_ref[...] = where_eq(iota((128, 1024), 0), iota((128, 1024), 1) // 8)
    column = iota((512, 512), 1)
    perm = where_eq(iota((512, 512), 0), (column % 8) * LEAF + column // 8)
    for copy in arrivals:
        copy.wait()
    stacked = jnp.concatenate([points_ref[:, 512 * g : 512 * g + 512] for g in range(GROUPS)], axis=0)
    x_ref[...] = dot(stacked, perm).astype(bf16)
    departures = []
    for step in range(GROUPS // 2):
        up_step(step, lanes, rows, basis_ref, local_ref, payload_ref, ub_ref, bd_ref, rep_ref, x_ref, c_ref)
        part = pl.ds(2 * step, 2)
        departures.append(pltpu.make_async_copy(ub_ref.at[part], ub_out.at[part], out_sem.at[step]))
        departures[-1].start()
    departures.append(pltpu.make_async_copy(bd_ref, bd_out, out_sem.at[8]))
    departures[-1].start()
    for k in range(8):
        y_ref[k, 0:126, :] = dot(local_ref[128:254, 128 * k : 128 * k + 128], rep_ref[...])
    tile = 0
    for level_tiles in (8, 4, 2, 1):
        for q in range(level_tiles):
            fill_upper(y_ref, bdup_ref, tile, tile, lanes == rows // 2 + 4 * (q % 2))
            tile += 1
    fill_upper(y_ref, bdup_ref, 15, 15, (lanes == rows // 2 + 4) & (rows < 4))
    fill_upper(y_ref, bdup_ref, 16, 15, (lanes == 0) & (rows >= 4) & (rows < 6))
    departures.append(pltpu.make_async_copy(bdup_ref, bdup_out, out_sem.at[9]))
    departures[-1].start()
    current = [c_ref[16 * q : 16 * q + 16, :] for q in range(8)]
    tile = 0
    for level_tiles in (8, 4, 2, 1, 1, 1):
        parts = [joined(dot(halves(current[q]), bdup_ref[tile + q])) for q in range(level_tiles)]
        tile += level_tiles
        if level_tiles > 1:
            current = [parts[2 * q] + parts[2 * q + 1] for q in range(level_tiles // 2)]
        else:
            current = parts
    squeeze = where_eq(iota((256, 128), 0), iota((256, 128), 1) * 8)
    mine = joined(dot(halves(current[0]), squeeze))
    zero = jnp.zeros_like(mine)
    payload_ref[:, TABLE:EDGE] = pack_state(mine, zero, zero)
    head = side(points_ref, coords_ref, 0)
    tail = side(points_ref, coords_ref, (LEAF_DEV - SPAN) * LEAF)
    even = bits_ref[0] == 0
    payload_ref[:, EDGE:WIDTH] = jnp.where(even, tail, head)
    payload_ref[:, WIDTH:] = jnp.where(even, head, tail)
    for copy in departures:
        copy.wait()


def side(points_ref, coords_ref, start):
    end = start + SPAN * LEAF
    parts = split3(scaled(coords_ref[:, start:end]))
    rows = jnp.concatenate(list(parts) + [jnp.zeros((7, SPAN * LEAF), f32)], axis=0)
    return jnp.concatenate([points_ref[:, start:end], rows.astype(bf16)], axis=1)


def open_kernel(nodes_ref, transfer_ref, couple_ref, after_ref, em_ref, sm_ref, token_ref, rows_ref, sem):
    del after_ref
    token_ref[...] = jnp.zeros_like(token_ref)
    copies = [
        pltpu.make_async_copy(couple_ref.at[pl.ds(nodes_ref[k], 1)], rows_ref.at[pl.ds(k, 1)], sem.at[k])
        for k in range(6)
    ]
    for copy in copies:
        copy.start()
    which = iota((16, 254), 0)
    wanted = jnp.full((16, 254), -1, jnp.int32)
    for k in range(5):
        first = nodes_ref[k] - nodes_ref[8 + k]
        wanted = jnp.where(which == 2 * k, first, wanted)
        wanted = jnp.where(which == 2 * k + 1, first + 1, wanted)
    pairs = dot(where_eq(wanted, iota((16, 254), 1)), transfer_ref[...])
    fold_row = iota((1024, 128), 0) % RANK
    fold_col = iota((1024, 128), 1)
    fold_first = where_eq(fold_row, fold_col)
    fold_second = where_eq(fold_row + RANK, fold_col)
    own = iota((RANK, 1024), 1) // RANK == iota((RANK, 1024), 0)

    def opened(values, k):
        return jnp.where(own, values[k : k + 1, :], 0.0).astype(bf16)

    for copy in copies:
        copy.wait()
    couples = [rows_ref[k].astype(f32) for k in range(6)]
    em_ref[...] = dot(jnp.concatenate([opened(pairs, k) for k in range(10)], axis=0), fold_first).astype(bf16)
    sm_ref[...] = (
        dot(jnp.concatenate([opened(couples[k], 0) for k in range(6)], axis=0), fold_first)
        + dot(jnp.concatenate([opened(couples[k], 1) for k in range(6)], axis=0), fold_second)
    ).astype(bf16)


def opened_top(nodes, top_transfer, top_coupling, after):
    vmem = pl.BlockSpec(memory_space=pltpu.VMEM)
    anywhere = pl.BlockSpec(memory_space=pl.ANY)
    return pl.pallas_call(
        open_kernel,
        out_shape=(
            jax.ShapeDtypeStruct((320, 128), bf16),
            jax.ShapeDtypeStruct((192, 128), bf16),
            jax.ShapeDtypeStruct((8, 128), f32),
        ),
        in_specs=[pl.BlockSpec(memory_space=pltpu.SMEM), vmem, anywhere, anywhere],
        out_specs=(vmem, vmem, vmem),
        scratch_shapes=[pltpu.VMEM((6, 2, 1024), bf16), pltpu.SemaphoreType.DMA((6,))],
        compiler_params=pltpu.CompilerParams(vmem_limit_bytes=8 * 1024 * 1024),
        cost_estimate=pl.CostEstimate(flops=100_000_000, bytes_accessed=800_000, transcendentals=0),
    )(nodes, top_transfer, top_coupling, after)


def fill_upper(y_ref, bdup_ref, target, tile, keep):
    for a in range(0, RANK, 2):
        both = []
        for q in (a, a + 1):
            k, low = q // 4, q % 4
            both.append(jnp.where(keep, y_ref[k, 8 * tile : 8 * tile + 8, 256 * low : 256 * low + 256], 0.0))
        bdup_ref[target, 8 * a : 8 * a + 16, :] = jnp.concatenate(both, axis=0).astype(bf16)


def upward(bits, points, coords, basis, local_transfer):
    vmem = pl.BlockSpec(memory_space=pltpu.VMEM)
    hbm = pl.BlockSpec(memory_space=pltpu.HBM)
    return pl.pallas_call(
        up_kernel,
        out_shape=(
            jax.ShapeDtypeStruct((16, FIRST), bf16),
            jax.ShapeDtypeStruct((GROUPS, 512, 256), bf16),
            jax.ShapeDtypeStruct((GROUPS, 256, 256), bf16),
            jax.ShapeDtypeStruct((UPPER, 256, 256), bf16),
        ),
        in_specs=[pl.BlockSpec(memory_space=pltpu.SMEM)] + [hbm] * 4,
        out_specs=(vmem,) + (hbm,) * 3,
        scratch_shapes=[
            pltpu.VMEM((128, 1024), bf16),
            pltpu.VMEM((256, 512), bf16),
            pltpu.VMEM((128, 256), f32),
            pltpu.VMEM((8, 128, 1024), f32),
            pltpu.VMEM((16, LEAF_DEV * LEAF), bf16),
            pltpu.VMEM((3, LEAF_DEV * LEAF), f32),
            pltpu.VMEM((LEAF_DEV, LEAF * RANK), bf16),
            pltpu.VMEM((254, 1024), bf16),
            pltpu.VMEM((GROUPS, 512, 256), bf16),
            pltpu.VMEM((GROUPS, 256, 256), bf16),
            pltpu.VMEM((UPPER, 256, 256), bf16),
            pltpu.SemaphoreType.DMA((4,)),
            pltpu.SemaphoreType.DMA((10,)),
        ],
        compiler_params=pltpu.CompilerParams(vmem_limit_bytes=60 * 1024 * 1024),
        cost_estimate=pl.CostEstimate(flops=1_000_000_000, bytes_accessed=10_000_000, transcendentals=0),
    )(bits, points, coords, basis, local_transfer)


def step_kernel(height, bits_ref, first_ref, payload_ref, received_ref, em_ref, *rest):
    next_ref = rest[-1]
    forward = height % 2 == 1
    next_ref[:, :TABLE] = received_ref[:, :TABLE] if forward else first_ref[:, :TABLE]
    start = WIDTH if height == 0 else EDGE
    next_ref[:, EDGE:] = payload_ref[:, EDGE:WIDTH] if forward else received_ref[:, start : start + HALO]
    mine, _, _ = unpack_state(payload_ref[:, TABLE:EDGE])
    sibling, _, _ = unpack_state(received_ref[:, TABLE:EDGE])
    if height <= 4:
        first = bits_ref[height] == 0
        left = jnp.where(first, mine, sibling)
        right = jnp.where(first, sibling, mine)
        both = (left + pltpu.roll(right, 32, 1))[:, : 2 * RANK]
        parent = joined(dot(halves(both), em_ref[64 * height : 64 * height + 64, :]))
    else:
        parent = jnp.zeros_like(mine)
    next_ref[:, TABLE:EDGE] = pack_state(parent, mine, sibling)


def tree_step(height, bits, first, payload, received, em, *after):
    vmem = pl.BlockSpec(memory_space=pltpu.VMEM)
    return pl.pallas_call(
        functools.partial(step_kernel, height),
        out_shape=jax.ShapeDtypeStruct((16, WIDTH), bf16),
        in_specs=[pl.BlockSpec(memory_space=pltpu.SMEM)] + [vmem] * 4 + [pl.BlockSpec(memory_space=pl.ANY)] * len(after),
        out_specs=vmem,
        compiler_params=pltpu.CompilerParams(vmem_limit_bytes=4 * 1024 * 1024),
        cost_estimate=pl.CostEstimate(flops=1_000_000, bytes_accessed=400_000, transcendentals=0),
    )(bits, first, payload, received, em, *after)


def regroup_kernel(c_ref, after_ref, out_ref, token_ref):
    del after_ref
    token_ref[...] = jnp.zeros_like(token_ref)
    row = iota((128, 128), 0)
    perm = where_eq((row % 8) * NF + row // 8, iota((128, 128), 1))
    x = dot(perm, c_ref[...].reshape(128, 1024))
    lanes = iota((8, 128), 1)
    low_half = lanes < 64
    even = (lanes // RANK) % 2 == 0
    for s_high in range(4):
        for a_high in range(8):
            v = [
                x[32 * s_high + 8 * k : 32 * s_high + 8 * k + 8, 128 * a_high : 128 * a_high + 128]
                for k in range(4)
            ]
            u0 = jnp.where(low_half, v[0], pltpu.roll(v[2], 64, 1))
            u2 = jnp.where(low_half, pltpu.roll(v[0], 64, 1), v[2])
            u1 = jnp.where(low_half, v[1], pltpu.roll(v[3], 64, 1))
            u3 = jnp.where(low_half, pltpu.roll(v[1], 64, 1), v[3])
            w = []
            for p, q in ((u0, u1), (u2, u3)):
                w.append(jnp.where(even, p, pltpu.roll(q, 32, 1)))
                w.append(jnp.where(even, pltpu.roll(p, 96, 1), q))
            lane = 128 * s_high
            row = 32 * a_high
            out_ref[0, row : row + 16, lane : lane + 128] = jnp.concatenate(w[:2], axis=0).astype(bf16)
            out_ref[0, row + 16 : row + 32, lane : lane + 128] = jnp.concatenate(w[2:], axis=0).astype(bf16)


def regroup(half, far_coupling, after):
    groups = GROUPS // 2
    return pl.pallas_call(
        regroup_kernel,
        grid=(groups,),
        out_shape=(
            jax.ShapeDtypeStruct((groups, 256, 512), bf16),
            jax.ShapeDtypeStruct((8, 128), f32),
        ),
        in_specs=[
            pl.BlockSpec((8, NF, 1024), lambda i: (i + half * groups, 0, 0)),
            pl.BlockSpec(memory_space=pl.ANY),
        ],
        out_specs=(
            pl.BlockSpec((1, 256, 512), lambda i: (i, 0, 0)),
            pl.BlockSpec((8, 128), lambda i: (0, 0)),
        ),
        compiler_params=pltpu.CompilerParams(vmem_limit_bytes=12 * 1024 * 1024),
        cost_estimate=pl.CostEstimate(flops=600_000_000, bytes_accessed=4_200_000, transcendentals=0),
    )(far_coupling, after)


def down_kernel(bits_ref, index_ref, payload_ref, *refs):
    received = refs[:7]
    em_ref, sm_ref, coords_ref, rel_ref, bdup_in, d0_ref, d1_ref, bd_in, ub_in, near0_ref, near1_ref, near2_ref, near3_ref, out_ref, table_ref, field_ref, far_ref, gather_ref, edge_ref, d_ref, bdup_ref, bd_ref, ub_ref, sem = refs[7:]
    half = GROUPS // 2
    copies = [
        pltpu.make_async_copy(source, target, sem.at[k])
        for k, (source, target) in enumerate(
            (
                (bdup_in, bdup_ref),
                (d0_ref, d_ref.at[pl.ds(0, half)]),
                (bd_in, bd_ref),
                (ub_in, ub_ref),
                (d1_ref, d_ref.at[pl.ds(half, half)]),
            )
        )
    ]
    for copy in copies:
        copy.start()

    column = iota((256, 1024), 1)
    repeat = where_eq(iota((256, 1024), 0), (column % RANK) * 8 + column // 128)
    for k, ref in enumerate((payload_ref,) + received):
        stacked = jnp.concatenate([ref[:, 256 * g : 256 * g + 256] for g in range(GROUPS)], axis=0)
        wide = dot(stacked, repeat).astype(bf16)
        for m in range(8):
            table_ref[2048 * k + 256 * m : 2048 * k + 256 * m + 256, :] = wide[:, 128 * m : 128 * m + 128]
    table_ref[16384:16400, :] = jnp.zeros((16, 128), bf16)
    terms = []
    for height in range(1, 7):
        _, before_mine, before_sibling = unpack_state(received[height][:, TABLE:EDGE])
        plain = (bits_ref[height - 1] == 0) == (height % 2 == 1)
        left = jnp.where(plain, before_mine, before_sibling)
        right = jnp.where(plain, before_sibling, before_mine)
        both = left + pltpu.roll(right, 32, 1)
        terms.append(joined(dot_nt(halves(both), sm_ref[32 * height - 32 : 32 * height, :])))
    field = terms[5]
    for height in range(5, 0, -1):
        row = pl.multiple_of(64 * (height - 1) + 32 * bits_ref[height - 1], 32)
        matrix = em_ref[pl.ds(row, 32), 0:RANK]
        field = terms[height - 1] + joined(dot_nt(halves(field), matrix))
    stretch = where_eq(iota((RANK, 256), 0) * 8, iota((RANK, 256), 1))
    fields = [joined(dot(halves(field), stretch))]
    copies[0].wait()
    tile = UPPER
    for level_tiles in (1, 1, 1, 2, 4, 8):
        tile -= level_tiles
        fields = [
            joined(dot_nt(halves(fields[q // 2 if level_tiles > 1 else 0]), bdup_ref[tile + q]))
            for q in range(level_tiles)
        ]
    near_side = received[0][:, EDGE:WIDTH]
    far_side = received[1][:, EDGE:WIDTH]
    for height in range(2, 7):
        far_side = jnp.where(bits_ref[7] == height, received[height][:, EDGE:WIDTH], far_side)
    even = bits_ref[0] == 0
    left_halo = jnp.where(even, far_side, near_side)
    right_halo = jnp.where(even, near_side, far_side)

    def add(own, acc):
        edge_ref[own % 4] = acc

    edge_products(left_halo, right_halo, coords_ref, rel_ref, add)
    for q in range(8):
        field_ref[32 * q : 32 * q + 32, :] = halves(fields[q])
    for copy in copies[1:]:
        copy.wait()
    block = iota((16, 128), 1) // RANK
    which = iota((16, 256), 1) % 8
    for step in range(GROUPS):
        for leaf in range(8):
            for s_high in range(4):
                merged = None
                for low in range(4):
                    entry = index_ref[(8 * step + leaf) * NF + 4 * s_high + low]
                    value = table_ref[pl.ds(pl.multiple_of(entry, 16), 16), :]
                    merged = value if low == 0 else jnp.where(block == low, value, merged)
                gather_ref[step % 2, 16 * leaf : 16 * leaf + 16, 128 * s_high : 128 * s_high + 128] = merged
        result = dot_nt(gather_ref[step % 2], d_ref[step])
        far = result[0:16]
        for leaf in range(1, 8):
            far = jnp.where(which == leaf, result[16 * leaf : 16 * leaf + 16], far)
        parent = field_ref[32 * (step // 2) : 32 * (step // 2) + 32, :]
        leaf_field = (far + joined(dot_nt(parent, bd_ref[step]))).astype(bf16)
        part = dot_nt(leaf_field, ub_ref[step])
        high = part.astype(bf16)
        far_ref[16 * step : 16 * step + 16, :] = high
        far_ref[256 + 16 * step : 272 + 16 * step, :] = (part - high.astype(f32)).astype(bf16)
    column = iota((512, 512), 1)
    perm = where_eq(iota((512, 512), 0), (column % LEAF) * 8 + column // LEAF)
    whole = joined(dot(far_ref[...], perm))
    nears = (near0_ref, near1_ref, near2_ref, near3_ref)
    for g in range(GROUPS):
        per = GROUPS // CHUNKS
        chunk, place = g // per, 512 * (g % per)
        value = nears[chunk][:, place : place + 512] + whole[16 * g : 16 * g + 16, :]
        if chunk and g % per == 0:
            value = value + nears[chunk - 1][:, 512 * per : 512 * per + 512]
        if g == 0:
            value = value + jnp.concatenate([edge_ref[0], edge_ref[1]], axis=1)
        if g == GROUPS - 1:
            value = value + jnp.concatenate([edge_ref[2], edge_ref[3]], axis=1)
        out_ref[:, 512 * g : 512 * g + 512] = value


def downward(bits, index, payload, received, em, sm, bdup, coords, near_rel, d, ub, bd, nears):
    smem = pl.BlockSpec(memory_space=pltpu.SMEM)
    vmem = pl.BlockSpec(memory_space=pltpu.VMEM)
    hbm = pl.BlockSpec(memory_space=pltpu.HBM)
    return pl.pallas_call(
        down_kernel,
        out_shape=jax.ShapeDtypeStruct((16, LEAF_DEV * LEAF), f32),
        in_specs=[smem, smem] + [vmem] * 12 + [hbm] * 5 + [vmem] * CHUNKS,
        out_specs=vmem,
        scratch_shapes=[
            pltpu.VMEM((16400, 128), bf16),
            pltpu.VMEM((256, 256), bf16),
            pltpu.VMEM((512, 512), bf16),
            pltpu.VMEM((2, 128, 512), bf16),
            pltpu.VMEM((4, 16, BLK), f32),
            pltpu.VMEM((GROUPS, 256, 512), bf16),
            pltpu.VMEM((UPPER, 256, 256), bf16),
            pltpu.VMEM((GROUPS, 256, 256), bf16),
            pltpu.VMEM((GROUPS, 512, 256), bf16),
            pltpu.SemaphoreType.DMA((5,)),
        ],
        compiler_params=pltpu.CompilerParams(vmem_limit_bytes=40 * 1024 * 1024),
        cost_estimate=pl.CostEstimate(flops=3_000_000_000, bytes_accessed=16_000_000, transcendentals=0),
    )(bits, index, payload, *received, em, sm, coords, near_rel, bdup, *d, bd, ub, *nears)


def top_start(height, number):
    if height == 0:
        return 0
    return 2 * number - number // 2 ** (height - 1)


def per_device(
    points,
    coords,
    basis,
    far_list,
    far_coupling,
    near_list,
    local_transfer,
    top_transfer,
    top_coupling,
):
    device = lax.axis_index("leaf")
    outer = jnp.bitwise_xor(device, device + 2 * (device & 1) - 1)
    level = sum((outer >> k > 0).astype(jnp.int32) for k in range(7)) - 1
    number = jnp.arange(8, dtype=jnp.int32)
    bits = jnp.where(number == 7, jnp.maximum(level, 1), jnp.right_shift(device, number) & 1)
    starts = jnp.array([top_start(h, N_DEV) for h in range(6)], jnp.int32)
    heights = jnp.arange(6, dtype=jnp.int32)
    parity = jnp.right_shift(device, heights) & 1
    blank = jnp.zeros((2,), jnp.int32)
    nodes = jnp.concatenate([starts + jnp.right_shift(device, heights), blank, parity, blank])
    owner = jnp.bitwise_xor(jnp.right_shift(far_list, 7), device)
    slot = sum((owner >> k > 0).astype(jnp.int32) for k in range(7))
    within = far_list & (LEAF_DEV - 1)
    entry = slot * LEAF_DEV + (within & 7) * GROUPS + (within >> 3)
    index = 16 * jnp.where(far_list >= 0, entry, 8 * LEAF_DEV).reshape(LEAF_DEV * NF)
    payload, ub, bd, bdup = upward(bits, points, coords, basis, local_transfer)
    near_rel = jnp.transpose(jnp.where(near_list >= 0, near_list - device * LEAF_DEV, -1000))
    first = payload
    received = []
    nears = []
    halves_of = []
    for height, mask in enumerate(PARTNERS):
        route = [(i, i ^ mask) for i in range(N_DEV)]
        received.append(lax.ppermute(payload, "leaf", route))
        if height == 0:
            em, sm, token = opened_top(nodes, top_transfer, top_coupling, payload)
        elif height in (4, 5):
            part, token = regroup(height - 4, far_coupling, payload)
            halves_of.append(part)
        else:
            part, token = near_chunk(len(nears), coords, points, near_rel, payload)
            nears.append(part)
        if height < 6:
            extra = (token, index) if height == 1 else (token,)
            payload = tree_step(height, bits, first, payload, received[height], em, *extra)
    return downward(bits, index, first, received, em, sm, bdup, coords, near_rel, halves_of, ub, bd, nears)


def solution(mesh):
    return jax.shard_map(
        per_device,
        mesh=mesh,
        in_specs=(
            P(None, "leaf"),
            P(None, "leaf"),
            P("leaf", None),
            P("leaf", None),
            P("leaf", None, None),
            P("leaf", None),
            P("leaf", None),
            P(),
            P(),
        ),
        out_specs=P(None, "leaf"),
        check_vma=False,
    )
```

```python
import functools
import math

import jax
import jax.numpy as jnp
from jax import lax
from jax.experimental import pallas as pl
from jax.experimental.pallas import tpu as pltpu
from jax.sharding import PartitionSpec as P

LEAF = 64
RANK = 32
NF = 16
NN = 12
SPAN = 8
LEAF_DEV = 128
N_DEV = 128


variance = 1.0
nugget = 0.5
decay_rate = math.sqrt(3.0) / 0.3
highest = lax.Precision.HIGHEST


LOG2E = 1.4426950408889634
LN2 = 0.6931471805599453
SCALE = decay_rate * LOG2E
BLK = 256
BL = BLK // LEAF
FEAT = 64
f32 = jnp.float32
bf16 = jnp.bfloat16


def split3(v):
    a = v.astype(bf16).astype(f32)
    rest = v - a
    b = rest.astype(bf16).astype(f32)
    c = (rest - b).astype(bf16).astype(f32)
    return a, b, c


def scaled(coords):
    return (coords - 0.5) * SCALE


def widened(v):
    return jnp.concatenate([v, jnp.zeros((5, v.shape[1]), f32)], axis=0)


def features(parts):
    a, b, c = parts
    n = a.shape[1]
    v = a + b + c
    norm = split3(jnp.sum(v * v, axis=0, keepdims=True))
    row = lax.broadcasted_iota(jnp.int32, (8, n), 0)

    def place(first, second):
        out = jnp.zeros((8, n), f32)
        for k in range(3):
            out = jnp.where(row == k, first[k], out)
            out = jnp.where(row == k + 3, second[k], out)
        return out

    ones = [jnp.ones((1, n), f32)] * 3
    zero = jnp.zeros((8, n), f32)
    left = jnp.concatenate([a, a, a, b, b, c, place(norm, ones), zero], axis=0)
    a2, b2, c2 = -2.0 * a, -2.0 * b, -2.0 * c
    right = jnp.concatenate([a2, b2, c2, a2, b2, a2, place(ones, norm), zero], axis=0)
    return left, right


def matern(squared):
    m = jnp.maximum(squared, 1e-20)
    t = m * lax.rsqrt(m)
    return (variance + (variance * LN2) * t) * jnp.exp2(-t)


def expanded(x):
    leaf_of_lane = lax.broadcasted_iota(jnp.int32, (16, BLK), 1) // LEAF
    zero = jnp.zeros_like(x)
    return jnp.concatenate([jnp.where(leaf_of_lane == j, x, zero) for j in range(BL)], axis=0)


def slot_counts(rel_ref):
    leaf = lax.broadcasted_iota(jnp.int32, (32, LEAF_DEV), 1)
    row = lax.broadcasted_iota(jnp.int32, (32, LEAF_DEV), 0)
    base = (leaf // BL) * BL - SPAN
    count = jnp.zeros((32, LEAF_DEV), f32)
    for s in range(NN):
        count = count + jnp.where(rel_ref[s : s + 1, :] - base == row, 1.0, 0.0)
    return count


def spread_counts(count, b):
    spread = (
        lax.broadcasted_iota(jnp.int32, (LEAF_DEV, BLK), 0)
        == lax.broadcasted_iota(jnp.int32, (LEAF_DEV, BLK), 1) // LEAF
    ).astype(f32).astype(bf16)
    shifted = pltpu.roll(count, (LEAF_DEV - BL * b) % LEAF_DEV, 1) if b else count
    return jnp.dot(shifted.astype(bf16), spread, preferred_element_type=f32)


def weighed(acc, part, weight, offset):
    for k in range(BL):
        acc = acc + part[16 * k : 16 * k + 16] * weight[SPAN + offset + k : SPAN + offset + k + 1]
    return acc


def near_kernel(chunk, blocks, coords_ref, points_ref, rel_ref, after_ref, out_ref, token_ref, left_ref, right_ref, weight_ref, acc_ref, x_ref, *kerns):
    del after_ref
    total = blocks + 2
    begin = chunk * blocks
    valid = min(total, LEAF_DEV // BL - begin)
    token_ref[...] = jnp.zeros_like(token_ref)
    count = slot_counts(rel_ref)
    x_ref[:, : valid * BLK] = points_ref[:, begin * BLK : (begin + valid) * BLK]
    if valid < total:
        x_ref[:, valid * BLK :] = jnp.zeros((16, (total - valid) * BLK), bf16)
        left_ref[valid * BLK :, :] = jnp.zeros(((total - valid) * BLK, FEAT), bf16)
    for b in range(total):
        acc_ref[b] = jnp.zeros((16, BLK), f32)
        weight_ref[b] = spread_counts(count, begin + b) if b < valid else jnp.zeros((32, BLK), f32)
    for b in range(0, valid, 2):
        at = b * BLK
        left, right = features(split3(widened(scaled(coords_ref[:, begin * BLK + at : begin * BLK + at + 2 * BLK]))))
        left_ref[at : at + 2 * BLK, :] = jnp.transpose(left).astype(bf16)
        right_ref[:, at : at + 2 * BLK] = right.astype(bf16)

    rows = 128
    diagonal = [
        lax.broadcasted_iota(jnp.int32, (rows, BLK), 0) + rows * c
        == lax.broadcasted_iota(jnp.int32, (rows, BLK), 1)
        for c in range(BLK // rows)
    ]

    def block_x(b):
        return expanded(x_ref[:, pl.ds(pl.multiple_of(b * BLK, BLK), BLK)])

    def evaluate(n, step, next_ref):
        right = right_ref[:, pl.ds(pl.multiple_of(n * BLK, BLK), BLK)]
        for c in range(BLK // rows):
            left = left_ref[pl.ds(pl.multiple_of((n + step) * BLK, BLK) + rows * c, rows), :]
            block = matern(jnp.dot(left, right, preferred_element_type=f32))
            if step == 0:
                block = block + jnp.where(diagonal[c], nugget, 0.0)
            next_ref[step, rows * c : rows * c + rows, :] = block.astype(bf16)

    def both(i, kern_ref, n, next_ref):
        acc_i = acc_ref[i]
        x_i = block_x(i)
        weight_i = weight_ref[i]
        for step in range(3):
            j = i + step
            kern = kern_ref[step]
            part = jnp.dot(x_i if step == 0 else block_x(j), kern, preferred_element_type=f32)
            if step:
                mirror = lax.dot_general(x_i, kern, (((1,), (1,)), ((), ())), preferred_element_type=f32)
            if n is not None:
                evaluate(n, step, next_ref)
            acc_i = weighed(acc_i, part, weight_i, BL * step)
            if step:
                acc_ref[j] = weighed(acc_ref[j], mirror, weight_ref[j], -BL * step)
        acc_ref[i] = acc_i

    for step in range(3):
        evaluate(0, step, kerns[0])

    @pl.loop(0, blocks // 2 - 1)
    def _(m):
        both(2 * m, kerns[0], 2 * m + 1, kerns[1])
        both(2 * m + 1, kerns[1], 2 * m + 2, kerns[0])

    both(blocks - 2, kerns[0], blocks - 1, kerns[1])
    both(blocks - 1, kerns[1], None, None)
    for b in range(total):
        out_ref[:, b * BLK : b * BLK + BLK] = acc_ref[b]


CHUNKS = 4


def near_chunk(chunk, coords, points, near_rel, after):
    blocks = LEAF_DEV // BL // CHUNKS
    total = blocks + 2
    vmem = pl.BlockSpec(memory_space=pltpu.VMEM)
    return pl.pallas_call(
        functools.partial(near_kernel, chunk, blocks),
        out_shape=(
            jax.ShapeDtypeStruct((16, total * BLK), f32),
            jax.ShapeDtypeStruct((8, 128), f32),
        ),
        in_specs=[vmem] * 3 + [pl.BlockSpec(memory_space=pl.ANY)],
        out_specs=(vmem, vmem),
        scratch_shapes=[
            pltpu.VMEM((total * BLK, FEAT), bf16),
            pltpu.VMEM((FEAT, total * BLK), bf16),
            pltpu.VMEM((total, 32, BLK), f32),
            pltpu.VMEM((total, 16, BLK), f32),
            pltpu.VMEM((16, total * BLK), bf16),
            pltpu.VMEM((3, BLK, BLK), bf16),
            pltpu.VMEM((3, BLK, BLK), bf16),
        ],
        compiler_params=pltpu.CompilerParams(vmem_limit_bytes=16 * 1024 * 1024),
        cost_estimate=pl.CostEstimate(flops=1_000_000_000, bytes_accessed=1_000_000, transcendentals=4_000_000),
    )(coords, points, near_rel, after)


EDGES = ((0, -2, 0), (0, -1, 1), (1, -2, 1), (30, 2, 0), (31, 1, 0), (31, 2, 1))


def edge_products(left_halo, right_halo, coords_ref, rel_ref, add):
    count = slot_counts(rel_ref)
    halo_rows = []
    for halo in (left_halo, right_halo):
        splits = halo[:, SPAN * LEAF :].astype(f32)
        parts = [widened(splits[3 * k : 3 * k + 3]) for k in range(3)]
        halo_rows.append(jnp.transpose(features(parts)[0]).astype(bf16))
    for own in (0, 1, 30, 31):
        right = features(split3(widened(scaled(coords_ref[:, BLK * own : BLK * own + BLK]))))[1].astype(bf16)
        weight = spread_counts(count, own)
        acc = jnp.zeros((16, BLK), f32)
        for edge_own, offset, at in EDGES:
            if edge_own == own:
                side = 0 if offset < 0 else 1
                halo = (left_halo, right_halo)[side]
                left = halo_rows[side][BLK * at : BLK * at + BLK]
                kern = matern(jnp.dot(left, right, preferred_element_type=f32)).astype(bf16)
                part = jnp.dot(expanded(halo[:, BLK * at : BLK * at + BLK]), kern, preferred_element_type=f32)
                acc = weighed(acc, part, weight, BL * offset)
        add(own, acc)


TABLE = LEAF_DEV * RANK
STATE = 256
HALO = 2 * SPAN * LEAF
EDGE = TABLE + STATE
WIDTH = EDGE + HALO
FIRST = WIDTH + HALO
GROUPS = LEAF_DEV // 8
UPPER = 17
PARTNERS = (1, 2, 6, 8, 24, 32, 96)


def iota(shape, dim):
    return lax.broadcasted_iota(jnp.int32, shape, dim)


def where_eq(a, b):
    return jnp.where(a == b, 1.0, 0.0).astype(bf16)


def dot(a, b):
    return jnp.dot(a, b, preferred_element_type=f32)


def dot_nt(a, b):
    return lax.dot_general(a, b, (((1,), (1,)), ((), ())), preferred_element_type=f32)


def halves(v):
    high = v.astype(bf16)
    low = (v - high.astype(f32)).astype(bf16)
    return jnp.concatenate([high, low], axis=0)


def joined(v):
    rows = v.shape[0] // 2
    return v[:rows] + v[rows:]


def pack_state(first, second, third):
    parts = []
    for v in (first, second, third):
        high = v.astype(bf16).astype(f32)
        parts += [high, v - high]
    left = parts[0] + pltpu.roll(parts[1], 32, 1) + pltpu.roll(parts[2], 64, 1) + pltpu.roll(parts[3], 96, 1)
    right = parts[4] + pltpu.roll(parts[5], 32, 1)
    return jnp.concatenate([left, right], axis=1).astype(bf16)


def unpack_state(state):
    lanes = iota((16, 128), 1)
    left = state[:, :128].astype(f32)
    right = state[:, 128:].astype(f32)
    pair_left = left + pltpu.roll(left, 96, 1)
    pair_right = right + pltpu.roll(right, 96, 1)
    keep = lanes < RANK
    return (
        jnp.where(keep, pair_left, 0.0),
        jnp.where(keep, pltpu.roll(pair_left, 64, 1), 0.0),
        jnp.where(keep, pair_right, 0.0),
    )


def up_step(step, lanes, rows, basis_ref, local_ref, ub_ref, bd_ref, rep_ref):
    basis = basis_ref[16 * step : 16 * step + 16, :]
    wide = dot(jnp.concatenate([basis[:, 128 * k : 128 * k + 128] for k in range(16)], axis=0), rep_ref[...])
    keep = lanes == rows
    for e in range(2):
        for p in range(0, LEAF, 2):
            both = []
            for q in (p, p + 1):
                k, low = q // 4, q % 4
                both.append(jnp.where(keep, wide[16 * k + 8 * e : 16 * k + 8 * e + 8, 256 * low : 256 * low + 256], 0.0))
            ub_ref[2 * step + e, 8 * p : 8 * p + 16, :] = jnp.concatenate(both, axis=0).astype(bf16)
    local = local_ref[16 * step : 16 * step + 16, :]
    wide = dot(jnp.concatenate([local[:, 128 * k : 128 * k + 128] for k in range(8)], axis=0), rep_ref[...])
    for e in range(2):
        keep = lanes == rows // 2 + 4 * e
        for a in range(0, RANK, 2):
            both = []
            for q in (a, a + 1):
                k, low = q // 4, q % 4
                both.append(jnp.where(keep, wide[16 * k + 8 * e : 16 * k + 8 * e + 8, 256 * low : 256 * low + 256], 0.0))
            bd_ref[2 * step + e, 8 * a : 8 * a + 16, :] = jnp.concatenate(both, axis=0).astype(bf16)


def up_kernel(bits_ref, points_in, coords_in, basis_in, local_in, payload_ref, ub_out, bd_out, bdup_out, rep_ref, x_ref, y_ref, points_ref, coords_ref, basis_ref, local_ref, ub_ref, bd_ref, bdup_ref, in_sem, out_sem):
    arrivals = [
        pltpu.make_async_copy(source, target, in_sem.at[k])
        for k, (source, target) in enumerate(
            ((points_in, points_ref), (basis_in, basis_ref), (local_in, local_ref), (coords_in, coords_ref))
        )
    ]
    for copy in arrivals:
        copy.start()
    lanes = iota((8, 256), 1) % 8
    rows = iota((8, 256), 0)
    rep_ref[...] = where_eq(iota((128, 1024), 0), iota((128, 1024), 1) // 8)
    column = iota((512, 512), 1)
    perm = where_eq(iota((512, 512), 0), (column % 8) * LEAF + column // 8)
    for copy in arrivals:
        copy.wait()
    stacked = jnp.concatenate([points_ref[:, 512 * g : 512 * g + 512] for g in range(GROUPS)], axis=0)
    x_ref[...] = dot(stacked, perm).astype(bf16)
    departures = []
    for step in range(GROUPS // 2):
        up_step(step, lanes, rows, basis_ref, local_ref, ub_ref, bd_ref, rep_ref)
        part = pl.ds(2 * step, 2)
        departures.append(pltpu.make_async_copy(ub_ref.at[part], ub_out.at[part], out_sem.at[step]))
        departures[-1].start()
    coeffs = []
    for g in range(GROUPS):
        coeffs.append(dot(x_ref[16 * g : 16 * g + 16, :], ub_ref[g]).astype(bf16))
        payload_ref[:, 256 * g : 256 * g + 256] = coeffs[g]
    departures.append(pltpu.make_async_copy(bd_ref, bd_out, out_sem.at[8]))
    departures[-1].start()
    for k in range(8):
        y_ref[k, 0:126, :] = dot(local_ref[128:254, 128 * k : 128 * k + 128], rep_ref[...])
    tile = 0
    for level_tiles in (8, 4, 2, 1):
        for q in range(level_tiles):
            fill_upper(y_ref, bdup_ref, tile, tile, lanes == rows // 2 + 4 * (q % 2))
            tile += 1
    fill_upper(y_ref, bdup_ref, 15, 15, (lanes == rows // 2 + 4) & (rows < 4))
    fill_upper(y_ref, bdup_ref, 16, 15, (lanes == 0) & (rows >= 4) & (rows < 6))
    departures.append(pltpu.make_async_copy(bdup_ref, bdup_out, out_sem.at[9]))
    departures[-1].start()
    current = [dot(coeffs[2 * q], bd_ref[2 * q]) + dot(coeffs[2 * q + 1], bd_ref[2 * q + 1]) for q in range(8)]
    tile = 0
    for level_tiles in (8, 4, 2, 1, 1, 1):
        parts = [joined(dot(halves(current[q]), bdup_ref[tile + q])) for q in range(level_tiles)]
        tile += level_tiles
        if level_tiles > 1:
            current = [parts[2 * q] + parts[2 * q + 1] for q in range(level_tiles // 2)]
        else:
            current = parts
    squeeze = where_eq(iota((256, 128), 0), iota((256, 128), 1) * 8)
    mine = joined(dot(halves(current[0]), squeeze))
    zero = jnp.zeros_like(mine)
    payload_ref[:, TABLE:EDGE] = pack_state(mine, zero, zero)
    head = side(points_ref, coords_ref, 0)
    tail = side(points_ref, coords_ref, (LEAF_DEV - SPAN) * LEAF)
    even = bits_ref[0] == 0
    payload_ref[:, EDGE:WIDTH] = jnp.where(even, tail, head)
    payload_ref[:, WIDTH:] = jnp.where(even, head, tail)
    for copy in departures:
        copy.wait()


def side(points_ref, coords_ref, start):
    end = start + SPAN * LEAF
    parts = split3(scaled(coords_ref[:, start:end]))
    rows = jnp.concatenate(list(parts) + [jnp.zeros((7, SPAN * LEAF), f32)], axis=0)
    return jnp.concatenate([points_ref[:, start:end], rows.astype(bf16)], axis=1)


def open_kernel(nodes_ref, transfer_ref, couple_ref, after_ref, em_ref, sm_ref, token_ref, rows_ref, sem):
    del after_ref
    token_ref[...] = jnp.zeros_like(token_ref)
    copies = [
        pltpu.make_async_copy(couple_ref.at[pl.ds(nodes_ref[k], 1)], rows_ref.at[pl.ds(k, 1)], sem.at[k])
        for k in range(6)
    ]
    for copy in copies:
        copy.start()
    which = iota((16, 254), 0)
    wanted = jnp.full((16, 254), -1, jnp.int32)
    for k in range(5):
        first = nodes_ref[k] - nodes_ref[8 + k]
        wanted = jnp.where(which == 2 * k, first, wanted)
        wanted = jnp.where(which == 2 * k + 1, first + 1, wanted)
    pairs = dot(where_eq(wanted, iota((16, 254), 1)), transfer_ref[...])
    fold_row = iota((1024, 128), 0) % RANK
    fold_col = iota((1024, 128), 1)
    fold_first = where_eq(fold_row, fold_col)
    fold_second = where_eq(fold_row + RANK, fold_col)
    own = iota((RANK, 1024), 1) // RANK == iota((RANK, 1024), 0)

    def opened(values, k):
        return jnp.where(own, values[k : k + 1, :], 0.0).astype(bf16)

    for copy in copies:
        copy.wait()
    couples = [rows_ref[k].astype(f32) for k in range(6)]
    em_ref[...] = dot(jnp.concatenate([opened(pairs, k) for k in range(10)], axis=0), fold_first).astype(bf16)
    sm_ref[...] = (
        dot(jnp.concatenate([opened(couples[k], 0) for k in range(6)], axis=0), fold_first)
        + dot(jnp.concatenate([opened(couples[k], 1) for k in range(6)], axis=0), fold_second)
    ).astype(bf16)


def opened_top(nodes, top_transfer, top_coupling, after):
    vmem = pl.BlockSpec(memory_space=pltpu.VMEM)
    anywhere = pl.BlockSpec(memory_space=pl.ANY)
    return pl.pallas_call(
        open_kernel,
        out_shape=(
            jax.ShapeDtypeStruct((320, 128), bf16),
            jax.ShapeDtypeStruct((192, 128), bf16),
            jax.ShapeDtypeStruct((8, 128), f32),
        ),
        in_specs=[pl.BlockSpec(memory_space=pltpu.SMEM), vmem, anywhere, anywhere],
        out_specs=(vmem, vmem, vmem),
        scratch_shapes=[pltpu.VMEM((6, 2, 1024), bf16), pltpu.SemaphoreType.DMA((6,))],
        compiler_params=pltpu.CompilerParams(vmem_limit_bytes=8 * 1024 * 1024),
        cost_estimate=pl.CostEstimate(flops=100_000_000, bytes_accessed=800_000, transcendentals=0),
    )(nodes, top_transfer, top_coupling, after)


def fill_upper(y_ref, bdup_ref, target, tile, keep):
    for a in range(0, RANK, 2):
        both = []
        for q in (a, a + 1):
            k, low = q // 4, q % 4
            both.append(jnp.where(keep, y_ref[k, 8 * tile : 8 * tile + 8, 256 * low : 256 * low + 256], 0.0))
        bdup_ref[target, 8 * a : 8 * a + 16, :] = jnp.concatenate(both, axis=0).astype(bf16)


def upward(bits, points, coords, basis, local_transfer):
    vmem = pl.BlockSpec(memory_space=pltpu.VMEM)
    hbm = pl.BlockSpec(memory_space=pltpu.HBM)
    return pl.pallas_call(
        up_kernel,
        out_shape=(
            jax.ShapeDtypeStruct((16, FIRST), bf16),
            jax.ShapeDtypeStruct((GROUPS, 512, 256), bf16),
            jax.ShapeDtypeStruct((GROUPS, 256, 256), bf16),
            jax.ShapeDtypeStruct((UPPER, 256, 256), bf16),
        ),
        in_specs=[pl.BlockSpec(memory_space=pltpu.SMEM)] + [hbm] * 4,
        out_specs=(vmem,) + (hbm,) * 3,
        scratch_shapes=[
            pltpu.VMEM((128, 1024), bf16),
            pltpu.VMEM((256, 512), bf16),
            pltpu.VMEM((8, 128, 1024), f32),
            pltpu.VMEM((16, LEAF_DEV * LEAF), bf16),
            pltpu.VMEM((3, LEAF_DEV * LEAF), f32),
            pltpu.VMEM((LEAF_DEV, LEAF * RANK), bf16),
            pltpu.VMEM((254, 1024), bf16),
            pltpu.VMEM((GROUPS, 512, 256), bf16),
            pltpu.VMEM((GROUPS, 256, 256), bf16),
            pltpu.VMEM((UPPER, 256, 256), bf16),
            pltpu.SemaphoreType.DMA((4,)),
            pltpu.SemaphoreType.DMA((10,)),
        ],
        compiler_params=pltpu.CompilerParams(vmem_limit_bytes=60 * 1024 * 1024),
        cost_estimate=pl.CostEstimate(flops=1_000_000_000, bytes_accessed=10_000_000, transcendentals=0),
    )(bits, points, coords, basis, local_transfer)


def step_kernel(height, bits_ref, first_ref, payload_ref, received_ref, em_ref, *rest):
    next_ref = rest[-1]
    forward = height % 2 == 1
    next_ref[:, :TABLE] = received_ref[:, :TABLE] if forward else first_ref[:, :TABLE]
    start = WIDTH if height == 0 else EDGE
    next_ref[:, EDGE:] = payload_ref[:, EDGE:WIDTH] if forward else received_ref[:, start : start + HALO]
    mine, _, _ = unpack_state(payload_ref[:, TABLE:EDGE])
    sibling, _, _ = unpack_state(received_ref[:, TABLE:EDGE])
    if height <= 4:
        first = bits_ref[height] == 0
        left = jnp.where(first, mine, sibling)
        right = jnp.where(first, sibling, mine)
        both = (left + pltpu.roll(right, 32, 1))[:, : 2 * RANK]
        parent = joined(dot(halves(both), em_ref[64 * height : 64 * height + 64, :]))
    else:
        parent = jnp.zeros_like(mine)
    next_ref[:, TABLE:EDGE] = pack_state(parent, mine, sibling)


def tree_step(height, bits, first, payload, received, em, *after):
    vmem = pl.BlockSpec(memory_space=pltpu.VMEM)
    return pl.pallas_call(
        functools.partial(step_kernel, height),
        out_shape=jax.ShapeDtypeStruct((16, WIDTH), bf16),
        in_specs=[pl.BlockSpec(memory_space=pltpu.SMEM)] + [vmem] * 4 + [pl.BlockSpec(memory_space=pl.ANY)] * len(after),
        out_specs=vmem,
        compiler_params=pltpu.CompilerParams(vmem_limit_bytes=4 * 1024 * 1024),
        cost_estimate=pl.CostEstimate(flops=1_000_000, bytes_accessed=400_000, transcendentals=0),
    )(bits, first, payload, received, em, *after)


def regroup_kernel(c_ref, after_ref, out_ref, token_ref):
    del after_ref
    token_ref[...] = jnp.zeros_like(token_ref)
    row = iota((128, 128), 0)
    perm = where_eq((row % 8) * NF + row // 8, iota((128, 128), 1))
    x = dot(perm, c_ref[...].reshape(128, 1024))
    lanes = iota((8, 128), 1)
    low_half = lanes < 64
    even = (lanes // RANK) % 2 == 0
    for s_high in range(4):
        for a_high in range(8):
            v = [
                x[32 * s_high + 8 * k : 32 * s_high + 8 * k + 8, 128 * a_high : 128 * a_high + 128]
                for k in range(4)
            ]
            u0 = jnp.where(low_half, v[0], pltpu.roll(v[2], 64, 1))
            u2 = jnp.where(low_half, pltpu.roll(v[0], 64, 1), v[2])
            u1 = jnp.where(low_half, v[1], pltpu.roll(v[3], 64, 1))
            u3 = jnp.where(low_half, pltpu.roll(v[1], 64, 1), v[3])
            w = []
            for p, q in ((u0, u1), (u2, u3)):
                w.append(jnp.where(even, p, pltpu.roll(q, 32, 1)))
                w.append(jnp.where(even, pltpu.roll(p, 96, 1), q))
            lane = 128 * s_high
            row = 32 * a_high
            out_ref[0, row : row + 16, lane : lane + 128] = jnp.concatenate(w[:2], axis=0).astype(bf16)
            out_ref[0, row + 16 : row + 32, lane : lane + 128] = jnp.concatenate(w[2:], axis=0).astype(bf16)


def regroup(half, far_coupling, after):
    groups = GROUPS // 2
    return pl.pallas_call(
        regroup_kernel,
        grid=(groups,),
        out_shape=(
            jax.ShapeDtypeStruct((groups, 256, 512), bf16),
            jax.ShapeDtypeStruct((8, 128), f32),
        ),
        in_specs=[
            pl.BlockSpec((8, NF, 1024), lambda i: (i + half * groups, 0, 0)),
            pl.BlockSpec(memory_space=pl.ANY),
        ],
        out_specs=(
            pl.BlockSpec((1, 256, 512), lambda i: (i, 0, 0)),
            pl.BlockSpec((8, 128), lambda i: (0, 0)),
        ),
        compiler_params=pltpu.CompilerParams(vmem_limit_bytes=12 * 1024 * 1024),
        cost_estimate=pl.CostEstimate(flops=600_000_000, bytes_accessed=4_200_000, transcendentals=0),
    )(far_coupling, after)


def field_chain(bits_ref, received, em_ref, sm_ref, bdup_ref, field_ref):
    terms = []
    for height in range(1, 7):
        _, before_mine, before_sibling = unpack_state(received[height][:, TABLE:EDGE])
        plain = (bits_ref[height - 1] == 0) == (height % 2 == 1)
        left = jnp.where(plain, before_mine, before_sibling)
        right = jnp.where(plain, before_sibling, before_mine)
        both = left + pltpu.roll(right, 32, 1)
        yield
        terms.append(joined(dot_nt(halves(both), sm_ref[32 * height - 32 : 32 * height, :])))
    field = terms[5]
    for height in range(5, 0, -1):
        row = pl.multiple_of(64 * (height - 1) + 32 * bits_ref[height - 1], 32)
        matrix = em_ref[pl.ds(row, 32), 0:RANK]
        yield
        field = terms[height - 1] + joined(dot_nt(halves(field), matrix))
    stretch = where_eq(iota((RANK, 256), 0) * 8, iota((RANK, 256), 1))
    fields = [joined(dot(halves(field), stretch))]
    tile = UPPER
    for level_tiles in (1, 1, 1, 2, 4, 8):
        yield
        tile -= level_tiles
        fields = [
            joined(dot_nt(halves(fields[q // 2 if level_tiles > 1 else 0]), bdup_ref[tile + q]))
            for q in range(level_tiles)
        ]
    for q in range(8):
        field_ref[32 * q : 32 * q + 32, :] = halves(fields[q])


def down_kernel(bits_ref, index_ref, payload_ref, *refs):
    received = refs[:7]
    em_ref, sm_ref, coords_ref, rel_ref, bdup_in, d0_ref, d1_ref, bd_in, ub_in, near0_ref, near1_ref, near2_ref, near3_ref, out_ref, table_ref, field_ref, far_ref, gather_ref, edge_ref, d_ref, bdup_ref, bd_ref, ub_ref, sem = refs[7:]
    half = GROUPS // 2
    copies = [
        pltpu.make_async_copy(source, target, sem.at[k])
        for k, (source, target) in enumerate(
            (
                (bdup_in, bdup_ref),
                (d0_ref, d_ref.at[pl.ds(0, half)]),
                (bd_in, bd_ref),
                (ub_in, ub_ref),
                (d1_ref, d_ref.at[pl.ds(half, half)]),
            )
        )
    ]
    for copy in copies:
        copy.start()

    column = iota((256, 1024), 1)
    repeat = where_eq(iota((256, 1024), 0), (column % RANK) * 8 + column // 128)
    for k, ref in enumerate((payload_ref,) + received):
        stacked = jnp.concatenate([ref[:, 256 * g : 256 * g + 256] for g in range(GROUPS)], axis=0)
        wide = dot(stacked, repeat).astype(bf16)
        for m in range(8):
            table_ref[2048 * k + 256 * m : 2048 * k + 256 * m + 256, :] = wide[:, 128 * m : 128 * m + 128]
    table_ref[16384:16400, :] = jnp.zeros((16, 128), bf16)
    near_side = received[0][:, EDGE:WIDTH]
    far_side = received[1][:, EDGE:WIDTH]
    for height in range(2, 7):
        far_side = jnp.where(bits_ref[7] == height, received[height][:, EDGE:WIDTH], far_side)
    even = bits_ref[0] == 0
    left_halo = jnp.where(even, far_side, near_side)
    right_halo = jnp.where(even, near_side, far_side)

    def add(own, acc):
        edge_ref[own % 4] = acc

    edge_products(left_halo, right_halo, coords_ref, rel_ref, add)
    for copy in copies:
        copy.wait()
    block = iota((16, 128), 1) // RANK
    which = iota((16, 256), 1) % 8
    chain = field_chain(bits_ref, received, em_ref, sm_ref, bdup_ref, field_ref)
    fars = []
    for step in range(GROUPS):
        for leaf in range(8):
            for s_high in range(4):
                merged = None
                for low in range(4):
                    entry = index_ref[(8 * step + leaf) * NF + 4 * s_high + low]
                    value = table_ref[pl.ds(pl.multiple_of(entry, 16), 16), :]
                    merged = value if low == 0 else jnp.where(block == low, value, merged)
                gather_ref[step, 16 * leaf : 16 * leaf + 16, 128 * s_high : 128 * s_high + 128] = merged
        result = dot_nt(gather_ref[step], d_ref[step])
        next(chain, None)
        far = result[0:16]
        for leaf in range(1, 8):
            far = jnp.where(which == leaf, result[16 * leaf : 16 * leaf + 16], far)
        fars.append(far)
    for _ in chain:
        pass
    leaf_fields = []
    for step in range(GROUPS):
        parent = field_ref[32 * (step // 2) : 32 * (step // 2) + 32, :]
        leaf_fields.append((fars[step] + joined(dot_nt(parent, bd_ref[step]))).astype(bf16))
    for step in range(GROUPS):
        part = dot_nt(leaf_fields[step], ub_ref[step])
        high = part.astype(bf16)
        far_ref[16 * step : 16 * step + 16, :] = high
        far_ref[256 + 16 * step : 272 + 16 * step, :] = (part - high.astype(f32)).astype(bf16)
    column = iota((512, 512), 1)
    perm = where_eq(iota((512, 512), 0), (column % LEAF) * 8 + column // LEAF)
    whole = joined(dot(far_ref[...], perm))
    nears = (near0_ref, near1_ref, near2_ref, near3_ref)
    for g in range(GROUPS):
        per = GROUPS // CHUNKS
        chunk, place = g // per, 512 * (g % per)
        value = nears[chunk][:, place : place + 512] + whole[16 * g : 16 * g + 16, :]
        if chunk and g % per == 0:
            value = value + nears[chunk - 1][:, 512 * per : 512 * per + 512]
        if g == 0:
            value = value + jnp.concatenate([edge_ref[0], edge_ref[1]], axis=1)
        if g == GROUPS - 1:
            value = value + jnp.concatenate([edge_ref[2], edge_ref[3]], axis=1)
        out_ref[:, 512 * g : 512 * g + 512] = value


def downward(bits, index, payload, received, em, sm, bdup, coords, near_rel, d, ub, bd, nears):
    smem = pl.BlockSpec(memory_space=pltpu.SMEM)
    vmem = pl.BlockSpec(memory_space=pltpu.VMEM)
    hbm = pl.BlockSpec(memory_space=pltpu.HBM)
    return pl.pallas_call(
        down_kernel,
        out_shape=jax.ShapeDtypeStruct((16, LEAF_DEV * LEAF), f32),
        in_specs=[smem, smem] + [vmem] * 12 + [hbm] * 5 + [vmem] * CHUNKS,
        out_specs=vmem,
        scratch_shapes=[
            pltpu.VMEM((16400, 128), bf16),
            pltpu.VMEM((256, 256), bf16),
            pltpu.VMEM((512, 512), bf16),
            pltpu.VMEM((GROUPS, 128, 512), bf16),
            pltpu.VMEM((4, 16, BLK), f32),
            pltpu.VMEM((GROUPS, 256, 512), bf16),
            pltpu.VMEM((UPPER, 256, 256), bf16),
            pltpu.VMEM((GROUPS, 256, 256), bf16),
            pltpu.VMEM((GROUPS, 512, 256), bf16),
            pltpu.SemaphoreType.DMA((5,)),
        ],
        compiler_params=pltpu.CompilerParams(vmem_limit_bytes=40 * 1024 * 1024),
        cost_estimate=pl.CostEstimate(flops=3_000_000_000, bytes_accessed=16_000_000, transcendentals=0),
    )(bits, index, payload, *received, em, sm, coords, near_rel, bdup, *d, bd, ub, *nears)


def top_start(height, number):
    if height == 0:
        return 0
    return 2 * number - number // 2 ** (height - 1)


def per_device(
    points,
    coords,
    basis,
    far_list,
    far_coupling,
    near_list,
    local_transfer,
    top_transfer,
    top_coupling,
):
    device = lax.axis_index("leaf")
    outer = jnp.bitwise_xor(device, device + 2 * (device & 1) - 1)
    level = sum((outer >> k > 0).astype(jnp.int32) for k in range(7)) - 1
    number = jnp.arange(8, dtype=jnp.int32)
    bits = jnp.where(number == 7, jnp.maximum(level, 1), jnp.right_shift(device, number) & 1)
    starts = jnp.array([top_start(h, N_DEV) for h in range(6)], jnp.int32)
    heights = jnp.arange(6, dtype=jnp.int32)
    parity = jnp.right_shift(device, heights) & 1
    blank = jnp.zeros((2,), jnp.int32)
    nodes = jnp.concatenate([starts + jnp.right_shift(device, heights), blank, parity, blank])
    owner = jnp.bitwise_xor(jnp.right_shift(far_list, 7), device)
    slot = sum((owner >> k > 0).astype(jnp.int32) for k in range(7))
    within = far_list & (LEAF_DEV - 1)
    entry = slot * LEAF_DEV + (within & 7) * GROUPS + (within >> 3)
    index = 16 * jnp.where(far_list >= 0, entry, 8 * LEAF_DEV).reshape(LEAF_DEV * NF)
    payload, ub, bd, bdup = upward(bits, points, coords, basis, local_transfer)
    near_rel = jnp.transpose(jnp.where(near_list >= 0, near_list - device * LEAF_DEV, -1000))
    first = payload
    received = []
    nears = []
    halves_of = []
    for height, mask in enumerate(PARTNERS):
        route = [(i, i ^ mask) for i in range(N_DEV)]
        received.append(lax.ppermute(payload, "leaf", route))
        if height == 0:
            em, sm, token = opened_top(nodes, top_transfer, top_coupling, payload)
        elif height in (4, 5):
            part, token = regroup(height - 4, far_coupling, payload)
            halves_of.append(part)
        else:
            part, token = near_chunk(len(nears), coords, points, near_rel, payload)
            nears.append(part)
        if height < 6:
            extra = (token, index) if height == 1 else (token,)
            payload = tree_step(height, bits, first, payload, received[height], em, *extra)
    return downward(bits, index, first, received, em, sm, bdup, coords, near_rel, halves_of, ub, bd, nears)


def solution(mesh):
    return jax.shard_map(
        per_device,
        mesh=mesh,
        in_specs=(
            P(None, "leaf"),
            P(None, "leaf"),
            P("leaf", None),
            P("leaf", None),
            P("leaf", None, None),
            P("leaf", None),
            P("leaf", None),
            P(),
            P(),
        ),
        out_specs=P(None, "leaf"),
        check_vma=False,
    )
```

```python
import functools
import math

import jax
import jax.numpy as jnp
from jax import lax
from jax.experimental import pallas as pl
from jax.experimental.pallas import tpu as pltpu
from jax.sharding import PartitionSpec as P

LEAF = 64
RANK = 32
NF = 16
NN = 12
SPAN = 8
LEAF_DEV = 128
N_DEV = 128


variance = 1.0
nugget = 0.5
decay_rate = math.sqrt(3.0) / 0.3
highest = lax.Precision.HIGHEST


LOG2E = 1.4426950408889634
LN2 = 0.6931471805599453
SCALE = decay_rate * LOG2E
BLK = 256
BL = BLK // LEAF
FEAT = 64
f32 = jnp.float32
bf16 = jnp.bfloat16


def split3(v):
    a = v.astype(bf16).astype(f32)
    rest = v - a
    b = rest.astype(bf16).astype(f32)
    c = (rest - b).astype(bf16).astype(f32)
    return a, b, c


def scaled(coords):
    return (coords - 0.5) * SCALE


def widened(v):
    return jnp.concatenate([v, jnp.zeros((5, v.shape[1]), f32)], axis=0)


def features(parts):
    a, b, c = parts
    n = a.shape[1]
    v = a + b + c
    norm = split3(jnp.sum(v * v, axis=0, keepdims=True))
    row = lax.broadcasted_iota(jnp.int32, (8, n), 0)

    def place(first, second):
        out = jnp.zeros((8, n), f32)
        for k in range(3):
            out = jnp.where(row == k, first[k], out)
            out = jnp.where(row == k + 3, second[k], out)
        return out

    ones = [jnp.ones((1, n), f32)] * 3
    zero = jnp.zeros((8, n), f32)
    left = jnp.concatenate([a, a, a, b, b, c, place(norm, ones), zero], axis=0)
    a2, b2, c2 = -2.0 * a, -2.0 * b, -2.0 * c
    right = jnp.concatenate([a2, b2, c2, a2, b2, a2, place(ones, norm), zero], axis=0)
    return left, right


def matern(squared):
    m = jnp.maximum(squared, 1e-20)
    t = m * lax.rsqrt(m)
    return (variance + (variance * LN2) * t) * jnp.exp2(-t)


def expanded(x):
    leaf_of_lane = lax.broadcasted_iota(jnp.int32, (16, BLK), 1) // LEAF
    zero = jnp.zeros_like(x)
    return jnp.concatenate([jnp.where(leaf_of_lane == j, x, zero) for j in range(BL)], axis=0)


def slot_counts(rel_ref):
    leaf = lax.broadcasted_iota(jnp.int32, (32, LEAF_DEV), 1)
    row = lax.broadcasted_iota(jnp.int32, (32, LEAF_DEV), 0)
    base = (leaf // BL) * BL - SPAN
    count = jnp.zeros((32, LEAF_DEV), f32)
    for s in range(NN):
        count = count + jnp.where(rel_ref[s : s + 1, :] - base == row, 1.0, 0.0)
    return count


def spread_counts(count, b):
    spread = (
        lax.broadcasted_iota(jnp.int32, (LEAF_DEV, BLK), 0)
        == lax.broadcasted_iota(jnp.int32, (LEAF_DEV, BLK), 1) // LEAF
    ).astype(f32).astype(bf16)
    shifted = pltpu.roll(count, (LEAF_DEV - BL * b) % LEAF_DEV, 1) if b else count
    return jnp.dot(shifted.astype(bf16), spread, preferred_element_type=f32)


def weighed(acc, part, weight, offset):
    for k in range(BL):
        acc = acc + part[16 * k : 16 * k + 16] * weight[SPAN + offset + k : SPAN + offset + k + 1]
    return acc


def near_kernel(chunk, blocks, coords_ref, points_ref, rel_ref, after_ref, out_ref, token_ref, left_ref, right_ref, weight_ref, acc_ref, x_ref, *kerns):
    del after_ref
    total = blocks + 2
    begin = chunk * blocks
    valid = min(total, LEAF_DEV // BL - begin)
    token_ref[...] = jnp.zeros_like(token_ref)
    count = slot_counts(rel_ref)
    x_ref[:, : valid * BLK] = points_ref[:, begin * BLK : (begin + valid) * BLK]
    if valid < total:
        x_ref[:, valid * BLK :] = jnp.zeros((16, (total - valid) * BLK), bf16)
        left_ref[valid * BLK :, :] = jnp.zeros(((total - valid) * BLK, FEAT), bf16)
    for b in range(total):
        acc_ref[b] = jnp.zeros((16, BLK), f32)
        weight_ref[b] = spread_counts(count, begin + b) if b < valid else jnp.zeros((32, BLK), f32)
    for b in range(0, valid, 2):
        at = b * BLK
        left, right = features(split3(widened(scaled(coords_ref[:, begin * BLK + at : begin * BLK + at + 2 * BLK]))))
        left_ref[at : at + 2 * BLK, :] = jnp.transpose(left).astype(bf16)
        right_ref[:, at : at + 2 * BLK] = right.astype(bf16)

    rows = 128
    diagonal = [
        lax.broadcasted_iota(jnp.int32, (rows, BLK), 0) + rows * c
        == lax.broadcasted_iota(jnp.int32, (rows, BLK), 1)
        for c in range(BLK // rows)
    ]

    def block_x(b):
        return expanded(x_ref[:, pl.ds(pl.multiple_of(b * BLK, BLK), BLK)])

    def evaluate(n, step, next_ref):
        right = right_ref[:, pl.ds(pl.multiple_of(n * BLK, BLK), BLK)]
        for c in range(BLK // rows):
            left = left_ref[pl.ds(pl.multiple_of((n + step) * BLK, BLK) + rows * c, rows), :]
            block = matern(jnp.dot(left, right, preferred_element_type=f32))
            if step == 0:
                block = block + jnp.where(diagonal[c], nugget, 0.0)
            next_ref[step, rows * c : rows * c + rows, :] = block.astype(bf16)

    def both(i, kern_ref, n, next_ref):
        acc_i = acc_ref[i]
        x_i = block_x(i)
        weight_i = weight_ref[i]
        for step in range(3):
            j = i + step
            kern = kern_ref[step]
            part = jnp.dot(x_i if step == 0 else block_x(j), kern, preferred_element_type=f32)
            if step:
                mirror = lax.dot_general(x_i, kern, (((1,), (1,)), ((), ())), preferred_element_type=f32)
            if n is not None:
                evaluate(n, step, next_ref)
            acc_i = weighed(acc_i, part, weight_i, BL * step)
            if step:
                acc_ref[j] = weighed(acc_ref[j], mirror, weight_ref[j], -BL * step)
        acc_ref[i] = acc_i

    for step in range(3):
        evaluate(0, step, kerns[0])

    @pl.loop(0, blocks // 2 - 1)
    def _(m):
        both(2 * m, kerns[0], 2 * m + 1, kerns[1])
        both(2 * m + 1, kerns[1], 2 * m + 2, kerns[0])

    both(blocks - 2, kerns[0], blocks - 1, kerns[1])
    both(blocks - 1, kerns[1], None, None)
    for b in range(total):
        out_ref[:, b * BLK : b * BLK + BLK] = acc_ref[b]


CHUNKS = 4


def near_chunk(chunk, coords, points, near_rel, after):
    blocks = LEAF_DEV // BL // CHUNKS
    total = blocks + 2
    vmem = pl.BlockSpec(memory_space=pltpu.VMEM)
    return pl.pallas_call(
        functools.partial(near_kernel, chunk, blocks),
        out_shape=(
            jax.ShapeDtypeStruct((16, total * BLK), f32),
            jax.ShapeDtypeStruct((8, 128), f32),
        ),
        in_specs=[vmem] * 3 + [pl.BlockSpec(memory_space=pl.ANY)],
        out_specs=(vmem, vmem),
        scratch_shapes=[
            pltpu.VMEM((total * BLK, FEAT), bf16),
            pltpu.VMEM((FEAT, total * BLK), bf16),
            pltpu.VMEM((total, 32, BLK), f32),
            pltpu.VMEM((total, 16, BLK), f32),
            pltpu.VMEM((16, total * BLK), bf16),
            pltpu.VMEM((3, BLK, BLK), bf16),
            pltpu.VMEM((3, BLK, BLK), bf16),
        ],
        compiler_params=pltpu.CompilerParams(vmem_limit_bytes=16 * 1024 * 1024),
        cost_estimate=pl.CostEstimate(flops=1_000_000_000, bytes_accessed=1_000_000, transcendentals=4_000_000),
    )(coords, points, near_rel, after)


EDGES = ((0, -2, 0), (0, -1, 1), (1, -2, 1), (30, 2, 0), (31, 1, 0), (31, 2, 1))


def edge_products(left_halo, right_halo, coords_ref, rel_ref, add):
    count = slot_counts(rel_ref)
    halo_rows = []
    for halo in (left_halo, right_halo):
        splits = halo[:, SPAN * LEAF :].astype(f32)
        parts = [widened(splits[3 * k : 3 * k + 3]) for k in range(3)]
        halo_rows.append(jnp.transpose(features(parts)[0]).astype(bf16))
    for own in (0, 1, 30, 31):
        right = features(split3(widened(scaled(coords_ref[:, BLK * own : BLK * own + BLK]))))[1].astype(bf16)
        weight = spread_counts(count, own)
        acc = jnp.zeros((16, BLK), f32)
        for edge_own, offset, at in EDGES:
            if edge_own == own:
                side = 0 if offset < 0 else 1
                halo = (left_halo, right_halo)[side]
                left = halo_rows[side][BLK * at : BLK * at + BLK]
                kern = matern(jnp.dot(left, right, preferred_element_type=f32)).astype(bf16)
                part = jnp.dot(expanded(halo[:, BLK * at : BLK * at + BLK]), kern, preferred_element_type=f32)
                acc = weighed(acc, part, weight, BL * offset)
        add(own, acc)


TABLE = LEAF_DEV * RANK
STATE = 256
HALO = 2 * SPAN * LEAF
EDGE = TABLE + STATE
WIDTH = EDGE + HALO
FIRST = WIDTH + HALO
GROUPS = LEAF_DEV // 8
UPPER = 17
PARTNERS = (1, 2, 6, 8, 24, 32, 96)


def iota(shape, dim):
    return lax.broadcasted_iota(jnp.int32, shape, dim)


def where_eq(a, b):
    return jnp.where(a == b, 1.0, 0.0).astype(bf16)


def dot(a, b):
    return jnp.dot(a, b, preferred_element_type=f32)


def dot_nt(a, b):
    return lax.dot_general(a, b, (((1,), (1,)), ((), ())), preferred_element_type=f32)


def halves(v):
    high = v.astype(bf16)
    low = (v - high.astype(f32)).astype(bf16)
    return jnp.concatenate([high, low], axis=0)


def joined(v):
    rows = v.shape[0] // 2
    return v[:rows] + v[rows:]


def pack_state(first, second, third):
    parts = []
    for v in (first, second, third):
        high = v.astype(bf16).astype(f32)
        parts += [high, v - high]
    left = parts[0] + pltpu.roll(parts[1], 32, 1) + pltpu.roll(parts[2], 64, 1) + pltpu.roll(parts[3], 96, 1)
    right = parts[4] + pltpu.roll(parts[5], 32, 1)
    return jnp.concatenate([left, right], axis=1).astype(bf16)


def unpack_state(state):
    lanes = iota((16, 128), 1)
    left = state[:, :128].astype(f32)
    right = state[:, 128:].astype(f32)
    pair_left = left + pltpu.roll(left, 96, 1)
    pair_right = right + pltpu.roll(right, 96, 1)
    keep = lanes < RANK
    return (
        jnp.where(keep, pair_left, 0.0),
        jnp.where(keep, pltpu.roll(pair_left, 64, 1), 0.0),
        jnp.where(keep, pair_right, 0.0),
    )


def up_step(step, lanes, rows, basis_ref, local_ref, ub_ref, bd_ref, rep_ref):
    basis = basis_ref[16 * step : 16 * step + 16, :]
    wide = dot(jnp.concatenate([basis[:, 128 * k : 128 * k + 128] for k in range(16)], axis=0), rep_ref[...])
    keep = lanes == rows
    for e in range(2):
        for p in range(0, LEAF, 2):
            both = []
            for q in (p, p + 1):
                k, low = q // 4, q % 4
                both.append(jnp.where(keep, wide[16 * k + 8 * e : 16 * k + 8 * e + 8, 256 * low : 256 * low + 256], 0.0))
            ub_ref[2 * step + e, 8 * p : 8 * p + 16, :] = jnp.concatenate(both, axis=0).astype(bf16)
    local = local_ref[16 * step : 16 * step + 16, :]
    wide = dot(jnp.concatenate([local[:, 128 * k : 128 * k + 128] for k in range(8)], axis=0), rep_ref[...])
    for e in range(2):
        keep = lanes == rows // 2 + 4 * e
        for a in range(0, RANK, 2):
            both = []
            for q in (a, a + 1):
                k, low = q // 4, q % 4
                both.append(jnp.where(keep, wide[16 * k + 8 * e : 16 * k + 8 * e + 8, 256 * low : 256 * low + 256], 0.0))
            bd_ref[2 * step + e, 8 * a : 8 * a + 16, :] = jnp.concatenate(both, axis=0).astype(bf16)


def up_kernel(bits_ref, points_in, coords_in, basis_in, local_in, payload_ref, ub_out, bd_out, bdup_out, rep_ref, x_ref, y_ref, points_ref, coords_ref, basis_ref, local_ref, ub_ref, bd_ref, bdup_ref, in_sem, out_sem):
    arrivals = [
        pltpu.make_async_copy(source, target, in_sem.at[k])
        for k, (source, target) in enumerate(
            ((points_in, points_ref), (basis_in, basis_ref), (local_in, local_ref), (coords_in, coords_ref))
        )
    ]
    for copy in arrivals:
        copy.start()
    lanes = iota((8, 256), 1) % 8
    rows = iota((8, 256), 0)
    rep_ref[...] = where_eq(iota((128, 1024), 0), iota((128, 1024), 1) // 8)
    column = iota((512, 512), 1)
    perm = where_eq(iota((512, 512), 0), (column % 8) * LEAF + column // 8)
    for copy in arrivals:
        copy.wait()
    stacked = jnp.concatenate([points_ref[:, 512 * g : 512 * g + 512] for g in range(GROUPS)], axis=0)
    x_ref[...] = dot(stacked, perm).astype(bf16)
    departures = []
    for step in range(GROUPS // 2):
        up_step(step, lanes, rows, basis_ref, local_ref, ub_ref, bd_ref, rep_ref)
        part = pl.ds(2 * step, 2)
        departures.append(pltpu.make_async_copy(ub_ref.at[part], ub_out.at[part], out_sem.at[step]))
        departures[-1].start()
    coeffs = []
    for g in range(GROUPS):
        coeffs.append(dot(x_ref[16 * g : 16 * g + 16, :], ub_ref[g]).astype(bf16))
        payload_ref[:, 256 * g : 256 * g + 256] = coeffs[g]
    departures.append(pltpu.make_async_copy(bd_ref, bd_out, out_sem.at[8]))
    departures[-1].start()
    for k in range(8):
        y_ref[k, 0:126, :] = dot(local_ref[128:254, 128 * k : 128 * k + 128], rep_ref[...])
    tile = 0
    for level_tiles in (8, 4, 2, 1):
        for q in range(level_tiles):
            fill_upper(y_ref, bdup_ref, tile, tile, lanes == rows // 2 + 4 * (q % 2))
            tile += 1
    fill_upper(y_ref, bdup_ref, 15, 15, (lanes == rows // 2 + 4) & (rows < 4))
    fill_upper(y_ref, bdup_ref, 16, 15, (lanes == 0) & (rows >= 4) & (rows < 6))
    departures.append(pltpu.make_async_copy(bdup_ref, bdup_out, out_sem.at[9]))
    departures[-1].start()
    current = [dot(coeffs[2 * q], bd_ref[2 * q]) + dot(coeffs[2 * q + 1], bd_ref[2 * q + 1]) for q in range(8)]
    tile = 0
    for level_tiles in (8, 4, 2, 1, 1, 1):
        parts = [joined(dot(halves(current[q]), bdup_ref[tile + q])) for q in range(level_tiles)]
        tile += level_tiles
        if level_tiles > 1:
            current = [parts[2 * q] + parts[2 * q + 1] for q in range(level_tiles // 2)]
        else:
            current = parts
    squeeze = where_eq(iota((256, 128), 0), iota((256, 128), 1) * 8)
    mine = joined(dot(halves(current[0]), squeeze))
    zero = jnp.zeros_like(mine)
    payload_ref[:, TABLE:EDGE] = pack_state(mine, zero, zero)
    head = side(points_ref, coords_ref, 0)
    tail = side(points_ref, coords_ref, (LEAF_DEV - SPAN) * LEAF)
    even = bits_ref[0] == 0
    payload_ref[:, EDGE:WIDTH] = jnp.where(even, tail, head)
    payload_ref[:, WIDTH:] = jnp.where(even, head, tail)
    for copy in departures:
        copy.wait()


def side(points_ref, coords_ref, start):
    end = start + SPAN * LEAF
    parts = split3(scaled(coords_ref[:, start:end]))
    rows = jnp.concatenate(list(parts) + [jnp.zeros((7, SPAN * LEAF), f32)], axis=0)
    return jnp.concatenate([points_ref[:, start:end], rows.astype(bf16)], axis=1)


def open_kernel(nodes_ref, transfer_ref, couple_ref, after_ref, em_ref, sm_ref, token_ref, rows_ref, sem):
    del after_ref
    token_ref[...] = jnp.zeros_like(token_ref)
    copies = [
        pltpu.make_async_copy(couple_ref.at[pl.ds(nodes_ref[k], 1)], rows_ref.at[pl.ds(k, 1)], sem.at[k])
        for k in range(6)
    ]
    for copy in copies:
        copy.start()
    which = iota((16, 254), 0)
    wanted = jnp.full((16, 254), -1, jnp.int32)
    for k in range(5):
        first = nodes_ref[k] - nodes_ref[8 + k]
        wanted = jnp.where(which == 2 * k, first, wanted)
        wanted = jnp.where(which == 2 * k + 1, first + 1, wanted)
    pairs = dot(where_eq(wanted, iota((16, 254), 1)), transfer_ref[...])
    fold_row = iota((1024, 128), 0) % RANK
    fold_col = iota((1024, 128), 1)
    fold_first = where_eq(fold_row, fold_col)
    fold_second = where_eq(fold_row + RANK, fold_col)
    own = iota((RANK, 1024), 1) // RANK == iota((RANK, 1024), 0)

    def opened(values, k):
        return jnp.where(own, values[k : k + 1, :], 0.0).astype(bf16)

    for copy in copies:
        copy.wait()
    couples = [rows_ref[k].astype(f32) for k in range(6)]
    em_ref[...] = dot(jnp.concatenate([opened(pairs, k) for k in range(10)], axis=0), fold_first).astype(bf16)
    sm_ref[...] = (
        dot(jnp.concatenate([opened(couples[k], 0) for k in range(6)], axis=0), fold_first)
        + dot(jnp.concatenate([opened(couples[k], 1) for k in range(6)], axis=0), fold_second)
    ).astype(bf16)


def opened_top(nodes, top_transfer, top_coupling, after):
    vmem = pl.BlockSpec(memory_space=pltpu.VMEM)
    anywhere = pl.BlockSpec(memory_space=pl.ANY)
    return pl.pallas_call(
        open_kernel,
        out_shape=(
            jax.ShapeDtypeStruct((320, 128), bf16),
            jax.ShapeDtypeStruct((192, 128), bf16),
            jax.ShapeDtypeStruct((8, 128), f32),
        ),
        in_specs=[pl.BlockSpec(memory_space=pltpu.SMEM), vmem, anywhere, anywhere],
        out_specs=(vmem, vmem, vmem),
        scratch_shapes=[pltpu.VMEM((6, 2, 1024), bf16), pltpu.SemaphoreType.DMA((6,))],
        compiler_params=pltpu.CompilerParams(vmem_limit_bytes=8 * 1024 * 1024),
        cost_estimate=pl.CostEstimate(flops=100_000_000, bytes_accessed=800_000, transcendentals=0),
    )(nodes, top_transfer, top_coupling, after)


def fill_upper(y_ref, bdup_ref, target, tile, keep):
    for a in range(0, RANK, 2):
        both = []
        for q in (a, a + 1):
            k, low = q // 4, q % 4
            both.append(jnp.where(keep, y_ref[k, 8 * tile : 8 * tile + 8, 256 * low : 256 * low + 256], 0.0))
        bdup_ref[target, 8 * a : 8 * a + 16, :] = jnp.concatenate(both, axis=0).astype(bf16)


def upward(bits, points, coords, basis, local_transfer):
    vmem = pl.BlockSpec(memory_space=pltpu.VMEM)
    hbm = pl.BlockSpec(memory_space=pltpu.HBM)
    return pl.pallas_call(
        up_kernel,
        out_shape=(
            jax.ShapeDtypeStruct((16, FIRST), bf16),
            jax.ShapeDtypeStruct((GROUPS, 512, 256), bf16),
            jax.ShapeDtypeStruct((GROUPS, 256, 256), bf16),
            jax.ShapeDtypeStruct((UPPER, 256, 256), bf16),
        ),
        in_specs=[pl.BlockSpec(memory_space=pltpu.SMEM)] + [hbm] * 4,
        out_specs=(vmem,) + (hbm,) * 3,
        scratch_shapes=[
            pltpu.VMEM((128, 1024), bf16),
            pltpu.VMEM((256, 512), bf16),
            pltpu.VMEM((8, 128, 1024), f32),
            pltpu.VMEM((16, LEAF_DEV * LEAF), bf16),
            pltpu.VMEM((3, LEAF_DEV * LEAF), f32),
            pltpu.VMEM((LEAF_DEV, LEAF * RANK), bf16),
            pltpu.VMEM((254, 1024), bf16),
            pltpu.VMEM((GROUPS, 512, 256), bf16),
            pltpu.VMEM((GROUPS, 256, 256), bf16),
            pltpu.VMEM((UPPER, 256, 256), bf16),
            pltpu.SemaphoreType.DMA((4,)),
            pltpu.SemaphoreType.DMA((10,)),
        ],
        compiler_params=pltpu.CompilerParams(vmem_limit_bytes=60 * 1024 * 1024),
        cost_estimate=pl.CostEstimate(flops=1_000_000_000, bytes_accessed=10_000_000, transcendentals=0),
    )(bits, points, coords, basis, local_transfer)


def step_kernel(height, bits_ref, first_ref, payload_ref, received_ref, em_ref, *rest):
    next_ref = rest[-1]
    forward = height % 2 == 1
    next_ref[:, :TABLE] = received_ref[:, :TABLE] if forward else first_ref[:, :TABLE]
    start = WIDTH if height == 0 else EDGE
    next_ref[:, EDGE:] = payload_ref[:, EDGE:WIDTH] if forward else received_ref[:, start : start + HALO]
    mine, _, _ = unpack_state(payload_ref[:, TABLE:EDGE])
    sibling, _, _ = unpack_state(received_ref[:, TABLE:EDGE])
    if height <= 4:
        first = bits_ref[height] == 0
        left = jnp.where(first, mine, sibling)
        right = jnp.where(first, sibling, mine)
        both = (left + pltpu.roll(right, 32, 1))[:, : 2 * RANK]
        parent = joined(dot(halves(both), em_ref[64 * height : 64 * height + 64, :]))
    else:
        parent = jnp.zeros_like(mine)
    next_ref[:, TABLE:EDGE] = pack_state(parent, mine, sibling)


def tree_step(height, bits, first, payload, received, em, *after):
    vmem = pl.BlockSpec(memory_space=pltpu.VMEM)
    return pl.pallas_call(
        functools.partial(step_kernel, height),
        out_shape=jax.ShapeDtypeStruct((16, WIDTH), bf16),
        in_specs=[pl.BlockSpec(memory_space=pltpu.SMEM)] + [vmem] * 4 + [pl.BlockSpec(memory_space=pl.ANY)] * len(after),
        out_specs=vmem,
        compiler_params=pltpu.CompilerParams(vmem_limit_bytes=4 * 1024 * 1024),
        cost_estimate=pl.CostEstimate(flops=1_000_000, bytes_accessed=400_000, transcendentals=0),
    )(bits, first, payload, received, em, *after)


def regroup_kernel(c_ref, after_ref, out_ref, token_ref):
    del after_ref
    token_ref[...] = jnp.zeros_like(token_ref)
    row = iota((128, 128), 0)
    perm = where_eq((row % 8) * NF + row // 8, iota((128, 128), 1))
    x = dot(perm, c_ref[...].reshape(128, 1024))
    lanes = iota((8, 128), 1)
    low_half = lanes < 64
    even = (lanes // RANK) % 2 == 0
    for s_high in range(4):
        for a_high in range(8):
            v = [
                x[32 * s_high + 8 * k : 32 * s_high + 8 * k + 8, 128 * a_high : 128 * a_high + 128]
                for k in range(4)
            ]
            u0 = jnp.where(low_half, v[0], pltpu.roll(v[2], 64, 1))
            u2 = jnp.where(low_half, pltpu.roll(v[0], 64, 1), v[2])
            u1 = jnp.where(low_half, v[1], pltpu.roll(v[3], 64, 1))
            u3 = jnp.where(low_half, pltpu.roll(v[1], 64, 1), v[3])
            w = []
            for p, q in ((u0, u1), (u2, u3)):
                w.append(jnp.where(even, p, pltpu.roll(q, 32, 1)))
                w.append(jnp.where(even, pltpu.roll(p, 96, 1), q))
            lane = 128 * s_high
            row = 32 * a_high
            out_ref[0, row : row + 16, lane : lane + 128] = jnp.concatenate(w[:2], axis=0).astype(bf16)
            out_ref[0, row + 16 : row + 32, lane : lane + 128] = jnp.concatenate(w[2:], axis=0).astype(bf16)


def regroup(half, far_coupling, after):
    groups = GROUPS // 2
    return pl.pallas_call(
        regroup_kernel,
        grid=(groups,),
        out_shape=(
            jax.ShapeDtypeStruct((groups, 256, 512), bf16),
            jax.ShapeDtypeStruct((8, 128), f32),
        ),
        in_specs=[
            pl.BlockSpec((8, NF, 1024), lambda i: (i + half * groups, 0, 0)),
            pl.BlockSpec(memory_space=pl.ANY),
        ],
        out_specs=(
            pl.BlockSpec((1, 256, 512), lambda i: (i, 0, 0)),
            pl.BlockSpec((8, 128), lambda i: (0, 0)),
        ),
        compiler_params=pltpu.CompilerParams(vmem_limit_bytes=12 * 1024 * 1024),
        cost_estimate=pl.CostEstimate(flops=600_000_000, bytes_accessed=4_200_000, transcendentals=0),
    )(far_coupling, after)


def field_chain(bits_ref, received, em_ref, sm_ref, bdup_ref, field_ref):
    terms = []
    for height in range(1, 7):
        _, before_mine, before_sibling = unpack_state(received[height][:, TABLE:EDGE])
        plain = (bits_ref[height - 1] == 0) == (height % 2 == 1)
        left = jnp.where(plain, before_mine, before_sibling)
        right = jnp.where(plain, before_sibling, before_mine)
        both = left + pltpu.roll(right, 32, 1)
        yield
        terms.append(joined(dot_nt(halves(both), sm_ref[32 * height - 32 : 32 * height, :])))
    field = terms[5]
    for height in range(5, 0, -1):
        row = pl.multiple_of(64 * (height - 1) + 32 * bits_ref[height - 1], 32)
        matrix = em_ref[pl.ds(row, 32), 0:RANK]
        yield
        field = terms[height - 1] + joined(dot_nt(halves(field), matrix))
    stretch = where_eq(iota((RANK, 256), 0) * 8, iota((RANK, 256), 1))
    fields = [joined(dot(halves(field), stretch))]
    tile = UPPER
    for level_tiles in (1, 1, 1, 2, 4, 8):
        yield
        tile -= level_tiles
        fields = [
            joined(dot_nt(halves(fields[q // 2 if level_tiles > 1 else 0]), bdup_ref[tile + q]))
            for q in range(level_tiles)
        ]
    for q in range(8):
        field_ref[32 * q : 32 * q + 32, :] = halves(fields[q])


def down_kernel(bits_ref, index_ref, payload_ref, *refs):
    received = refs[:7]
    em_ref, sm_ref, coords_ref, rel_ref, bdup_in, d0_ref, d1_ref, bd_in, ub_in, near0_ref, near1_ref, near2_ref, near3_ref, out_ref, table_ref, field_ref, far_ref, gather_ref, edge_ref, d_ref, bdup_ref, bd_ref, ub_ref, sem = refs[7:]
    half = GROUPS // 2
    copies = [
        pltpu.make_async_copy(source, target, sem.at[k])
        for k, (source, target) in enumerate(
            (
                (d0_ref, d_ref.at[pl.ds(0, half)]),
                (d1_ref, d_ref.at[pl.ds(half, half)]),
                (bdup_in, bdup_ref),
                (bd_in, bd_ref),
                (ub_in, ub_ref),
            )
        )
    ]
    for copy in copies:
        copy.start()

    column = iota((256, 1024), 1)
    repeat = where_eq(iota((256, 1024), 0), (column % RANK) * 8 + column // 128)
    for k, ref in enumerate((payload_ref,) + received):
        stacked = jnp.concatenate([ref[:, 256 * g : 256 * g + 256] for g in range(GROUPS)], axis=0)
        wide = dot(stacked, repeat).astype(bf16)
        for m in range(8):
            table_ref[2048 * k + 256 * m : 2048 * k + 256 * m + 256, :] = wide[:, 128 * m : 128 * m + 128]
    table_ref[16384:16400, :] = jnp.zeros((16, 128), bf16)
    near_side = received[0][:, EDGE:WIDTH]
    far_side = received[1][:, EDGE:WIDTH]
    for height in range(2, 7):
        far_side = jnp.where(bits_ref[7] == height, received[height][:, EDGE:WIDTH], far_side)
    even = bits_ref[0] == 0
    left_halo = jnp.where(even, far_side, near_side)
    right_halo = jnp.where(even, near_side, far_side)

    def add(own, acc):
        edge_ref[own % 4] = acc

    edge_products(left_halo, right_halo, coords_ref, rel_ref, add)
    for copy in copies[:2]:
        copy.wait()
    block = iota((16, 128), 1) // RANK
    which = iota((16, 256), 1) % 8
    chain = field_chain(bits_ref, received, em_ref, sm_ref, bdup_ref, field_ref)
    fars = []
    for step in range(GROUPS):
        for leaf in range(8):
            for s_high in range(4):
                merged = None
                for low in range(4):
                    entry = index_ref[(8 * step + leaf) * NF + 4 * s_high + low]
                    value = table_ref[pl.ds(pl.multiple_of(entry, 16), 16), :]
                    merged = value if low == 0 else jnp.where(block == low, value, merged)
                gather_ref[step, 16 * leaf : 16 * leaf + 16, 128 * s_high : 128 * s_high + 128] = merged
        result = dot_nt(gather_ref[step], d_ref[step])
        if step == 8:
            copies[2].wait()
        next(chain, None)
        far = result[0:16]
        for leaf in range(1, 8):
            far = jnp.where(which == leaf, result[16 * leaf : 16 * leaf + 16], far)
        fars.append(far)
    for _ in chain:
        pass
    for copy in copies[3:]:
        copy.wait()
    leaf_fields = []
    for step in range(GROUPS):
        parent = field_ref[32 * (step // 2) : 32 * (step // 2) + 32, :]
        leaf_fields.append((fars[step] + joined(dot_nt(parent, bd_ref[step]))).astype(bf16))
    for step in range(GROUPS):
        part = dot_nt(leaf_fields[step], ub_ref[step])
        high = part.astype(bf16)
        far_ref[16 * step : 16 * step + 16, :] = high
        far_ref[256 + 16 * step : 272 + 16 * step, :] = (part - high.astype(f32)).astype(bf16)
    column = iota((512, 512), 1)
    perm = where_eq(iota((512, 512), 0), (column % LEAF) * 8 + column // LEAF)
    whole = joined(dot(far_ref[...], perm))
    nears = (near0_ref, near1_ref, near2_ref, near3_ref)
    for g in range(GROUPS):
        per = GROUPS // CHUNKS
        chunk, place = g // per, 512 * (g % per)
        value = nears[chunk][:, place : place + 512] + whole[16 * g : 16 * g + 16, :]
        if chunk and g % per == 0:
            value = value + nears[chunk - 1][:, 512 * per : 512 * per + 512]
        if g == 0:
            value = value + jnp.concatenate([edge_ref[0], edge_ref[1]], axis=1)
        if g == GROUPS - 1:
            value = value + jnp.concatenate([edge_ref[2], edge_ref[3]], axis=1)
        out_ref[:, 512 * g : 512 * g + 512] = value


def downward(bits, index, payload, received, em, sm, bdup, coords, near_rel, d, ub, bd, nears):
    smem = pl.BlockSpec(memory_space=pltpu.SMEM)
    vmem = pl.BlockSpec(memory_space=pltpu.VMEM)
    hbm = pl.BlockSpec(memory_space=pltpu.HBM)
    return pl.pallas_call(
        down_kernel,
        out_shape=jax.ShapeDtypeStruct((16, LEAF_DEV * LEAF), f32),
        in_specs=[smem, smem] + [vmem] * 12 + [hbm] * 5 + [vmem] * CHUNKS,
        out_specs=vmem,
        scratch_shapes=[
            pltpu.VMEM((16400, 128), bf16),
            pltpu.VMEM((256, 256), bf16),
            pltpu.VMEM((512, 512), bf16),
            pltpu.VMEM((GROUPS, 128, 512), bf16),
            pltpu.VMEM((4, 16, BLK), f32),
            pltpu.VMEM((GROUPS, 256, 512), bf16),
            pltpu.VMEM((UPPER, 256, 256), bf16),
            pltpu.VMEM((GROUPS, 256, 256), bf16),
            pltpu.VMEM((GROUPS, 512, 256), bf16),
            pltpu.SemaphoreType.DMA((5,)),
        ],
        compiler_params=pltpu.CompilerParams(vmem_limit_bytes=40 * 1024 * 1024),
        cost_estimate=pl.CostEstimate(flops=3_000_000_000, bytes_accessed=16_000_000, transcendentals=0),
    )(bits, index, payload, *received, em, sm, coords, near_rel, bdup, *d, bd, ub, *nears)


def top_start(height, number):
    if height == 0:
        return 0
    return 2 * number - number // 2 ** (height - 1)


def per_device(
    points,
    coords,
    basis,
    far_list,
    far_coupling,
    near_list,
    local_transfer,
    top_transfer,
    top_coupling,
):
    device = lax.axis_index("leaf")
    outer = jnp.bitwise_xor(device, device + 2 * (device & 1) - 1)
    level = sum((outer >> k > 0).astype(jnp.int32) for k in range(7)) - 1
    number = jnp.arange(8, dtype=jnp.int32)
    bits = jnp.where(number == 7, jnp.maximum(level, 1), jnp.right_shift(device, number) & 1)
    starts = jnp.array([top_start(h, N_DEV) for h in range(6)], jnp.int32)
    heights = jnp.arange(6, dtype=jnp.int32)
    parity = jnp.right_shift(device, heights) & 1
    blank = jnp.zeros((2,), jnp.int32)
    nodes = jnp.concatenate([starts + jnp.right_shift(device, heights), blank, parity, blank])
    owner = jnp.bitwise_xor(jnp.right_shift(far_list, 7), device)
    slot = sum((owner >> k > 0).astype(jnp.int32) for k in range(7))
    within = far_list & (LEAF_DEV - 1)
    entry = slot * LEAF_DEV + (within & 7) * GROUPS + (within >> 3)
    index = 16 * jnp.where(far_list >= 0, entry, 8 * LEAF_DEV).reshape(LEAF_DEV * NF)
    payload, ub, bd, bdup = upward(bits, points, coords, basis, local_transfer)
    near_rel = jnp.transpose(jnp.where(near_list >= 0, near_list - device * LEAF_DEV, -1000))
    first = payload
    received = []
    nears = []
    halves_of = []
    for height, mask in enumerate(PARTNERS):
        route = [(i, i ^ mask) for i in range(N_DEV)]
        received.append(lax.ppermute(payload, "leaf", route))
        if height == 0:
            em, sm, token = opened_top(nodes, top_transfer, top_coupling, payload)
        elif height in (4, 5):
            part, token = regroup(height - 4, far_coupling, payload)
            halves_of.append(part)
        else:
            part, token = near_chunk(len(nears), coords, points, near_rel, payload)
            nears.append(part)
        if height < 6:
            extra = (token, index) if height == 1 else (token,)
            payload = tree_step(height, bits, first, payload, received[height], em, *extra)
    return downward(bits, index, first, received, em, sm, bdup, coords, near_rel, halves_of, ub, bd, nears)


def solution(mesh):
    return jax.shard_map(
        per_device,
        mesh=mesh,
        in_specs=(
            P(None, "leaf"),
            P(None, "leaf"),
            P("leaf", None),
            P("leaf", None),
            P("leaf", None, None),
            P("leaf", None),
            P("leaf", None),
            P(),
            P(),
        ),
        out_specs=P(None, "leaf"),
        check_vma=False,
    )
```
